256 devices in a mesh: gx: 16 (over y, x), gy: 16 (over z, core).
Axes of the slice: x: 4, y: 4, z: 8, core: 2. Of those that a mesh axis runs over, the one named last changes fastest.
Arguments:
- vectors: float32 [8, 128, 256, 256], P(None, 'gx', 'gy'), may hold values from -10 to 10
- weight_x: float32 [128, 256, 256], P('gx', 'gy'), may hold values from 0.05 to 1
- weight_y: float32 [128, 256, 256], P('gx', 'gy'), may hold values from 0.05 to 1
- weight_z: float32 [128, 256, 256], P('gx', 'gy'), may hold values from 0.05 to 1
Outputs:
- refined: float32 [8, 128, 256, 256], P(None, 'gx', 'gy')
- eigenvalues: float32 [8], replicated
The draws below stay inside these ranges and needn't reach their ends.
All inputs are finite; a program needn't handle non-finite values.
Results may differ from the reference program's by a relative error of at most 0.000075.
Values sent between devices are 32-bit elements; how exact they have to be, the bound alone decides.
No kernel may reach another device: no remote copies, remote signals or barrier semaphores. Data moves between devices by JAX's collectives and lax.ppermute only.
A program may use at most 128 MiB of HBM per device.

```python
import math
import jax
import jax.numpy as jnp
from jax import lax

K = 8
NZ = 256
COARSE_SWEEPS = 4
NX = 128
NY = 256


def draw_vectors(key, part):
    keys = jax.random.split(jax.random.fold_in(key, 7), 5)
    shape = (K, NX, NY, NZ)
    base = jax.random.truncated_normal(keys[0], -4.0, 4.0, shape, jnp.float32)
    common = jax.random.truncated_normal(keys[1], -4.0, 4.0, (NX, NY, NZ), jnp.float32)
    offdiag = 1.0 - jnp.eye(K, dtype=jnp.float32)
    mixing = jax.random.uniform(keys[2], (K, K), jnp.float32, -0.12, 0.12) * offdiag
    signs = jnp.where(jax.random.bernoulli(keys[3], 0.5, (K,)), 1.0, -1.0).astype(jnp.float32)
    loads = jax.random.uniform(keys[4], (K,), jnp.float32, 0.25, 0.5) * signs
    mixed = base
    for source in range(K):
        mixed = mixed + mixing[:, source][:, None, None, None] * base[source][None]
    mixed = mixed + loads[:, None, None, None] * common[None]
    return mixed


def levels(own_key, shape, pieces, smallest, largest):
    loudness, own = 1.0, jax.random.fold_in(own_key, 6)
    for axis_at, blocks in pieces:
        heights = jnp.exp(jax.random.uniform(jax.random.fold_in(own, axis_at), (blocks,), jnp.float32, smallest / len(pieces), largest / len(pieces)))
        loudness = loudness * jnp.repeat(heights, shape[axis_at] // blocks).reshape([-1 if axis == axis_at else 1 for axis in range(len(shape))])
    return loudness


def setup_inputs(seed: int = 0) -> dict:
    key_of = jax.random.split(jax.random.key(seed), 5)
    return {
        "vectors": draw_vectors(jax.random.fold_in(key_of[4], 71), 0),
        "weight_x": jnp.clip(jnp.exp(math.log(1.0) - 2.9957323 * jax.random.uniform(key_of[1], (NX, NY, NZ), jnp.float32) ** levels(key_of[1], (NX, NY, NZ), ((0, 16), (1, 16)), -0.2, 0.2)), 0.05, 1.0),
        "weight_y": jnp.clip(jnp.exp(math.log(1.0) - 2.9957323 * jax.random.uniform(key_of[2], (NX, NY, NZ), jnp.float32) ** levels(key_of[2], (NX, NY, NZ), ((0, 16), (1, 16)), -0.2, 0.2)), 0.05, 1.0),
        "weight_z": jnp.clip(jnp.exp(math.log(1.0) - 2.9957323 * jax.random.uniform(key_of[3], (NX, NY, NZ), jnp.float32) ** levels(key_of[3], (NX, NY, NZ), ((0, 16), (1, 16)), -0.2, 0.2)), 0.05, 1.0),
    }


OMEGA = 0.8
SHIFT = 0.1

def lower(weights, axis):
    zeros = jnp.zeros_like(lax.slice_in_dim(weights, 0, 1, axis=axis))
    return jnp.concatenate([zeros, lax.slice_in_dim(weights, 0, weights.shape[axis] - 1, axis=axis)], axis)

def neighbours(field, parts):
    wx, lx, wy, ly, wz, lz = parts
    padded = jnp.pad(field, ((0, 0), (1, 1), (1, 1), (1, 1)))
    total = wx[None] * padded[:, 2:, 1:-1, 1:-1] + lx[None] * padded[:, :-2, 1:-1, 1:-1]
    total = total + wy[None] * padded[:, 1:-1, 2:, 1:-1] + ly[None] * padded[:, 1:-1, :-2, 1:-1]
    total = total + wz[None] * padded[:, 1:-1, 1:-1, 2:] + lz[None] * padded[:, 1:-1, 1:-1, :-2]
    return total

def jacobi(guess, source, diag, parts):
    return guess + OMEGA * (source - (diag[None] * guess - neighbours(guess, parts))) / diag[None]

def coarse_weights(wx, wy, wz, degree):
    sx, sy, sz = wx.shape
    shape = (sx // 2, 2, sy // 2, 2, sz // 2, 2)
    cx = wx.reshape(shape)[:, 1].sum(axis=(2, 4))
    cy = wy.reshape(shape)[:, :, :, 1].sum(axis=(1, 4))
    cz = wz.reshape(shape)[..., 1].sum(axis=(1, 3))
    dsum = degree.reshape(shape).sum(axis=(1, 3, 5))
    return (cx, cy, cz, dsum)

def restrict(field):
    kk, sx, sy, sz = field.shape
    return field.reshape(kk, sx // 2, 2, sy // 2, 2, sz // 2, 2).sum(axis=(2, 4, 6))

def prolong(field):
    kk, sx, sy, sz = field.shape
    return jnp.broadcast_to(field[:, :, None, :, None, :, None], (kk, sx, 2, sy, 2, sz, 2)).reshape(kk, 2 * sx, 2 * sy, 2 * sz)

def reference(vectors, weight_x, weight_y, weight_z):
    nx, ny, nz = weight_x.shape
    wx = jnp.where(jnp.arange(nx)[:, None, None] < nx - 1, weight_x, jnp.zeros_like(weight_x))
    wy = jnp.where(jnp.arange(ny)[None, :, None] < ny - 1, weight_y, jnp.zeros_like(weight_y))
    wz = jnp.where(jnp.arange(nz)[None, None, :] < nz - 1, weight_z, jnp.zeros_like(weight_z))
    parts = (wx, lower(wx, 0), wy, lower(wy, 1), wz, lower(wz, 2))
    degree = parts[0] + parts[1] + parts[2] + parts[3] + parts[4] + parts[5]
    applied = degree[None] * vectors - neighbours(vectors, parts)
    numer = jnp.sum(vectors * applied, axis=(1, 2, 3))
    denom = jnp.sum(vectors * (degree[None] * vectors), axis=(1, 2, 3))
    eigenvalues = numer / denom
    resid = applied - eigenvalues[:, None, None, None] * (degree[None] * vectors)
    cx, cy, cz, dsum = coarse_weights(wx, wy, wz, degree)
    cparts = (cx, lower(cx, 0), cy, lower(cy, 1), cz, lower(cz, 2))
    dcoarse = cparts[0] + cparts[1] + cparts[2] + cparts[3] + cparts[4] + cparts[5] + SHIFT * dsum
    dfine = (1.0 + SHIFT) * degree
    guess = OMEGA * resid / dfine[None]
    guess = jacobi(guess, resid, dfine, parts)
    fine_rest = resid - (dfine[None] * guess - neighbours(guess, parts))
    rcoarse = restrict(fine_rest)
    correction = OMEGA * rcoarse / dcoarse[None]
    for sweep in range(COARSE_SWEEPS - 1):
        correction = jacobi(correction, rcoarse, dcoarse, cparts)
    guess = guess + prolong(correction)
    guess = jacobi(guess, resid, dfine, parts)
    updated = vectors - guess
    gram = jnp.einsum('aijk,bijk->ab', updated, degree[None] * updated, precision=lax.Precision.HIGHEST)
    gram = gram / (nx * ny * nz)
    chol = jnp.linalg.cholesky(gram)
    flat = updated.reshape(updated.shape[0], -1)
    refined = jax.scipy.linalg.solve_triangular(chol, flat, lower=True).reshape(updated.shape)
    return (refined, eigenvalues)
```

```python
import jax
import jax.numpy as jnp
from jax import lax
from jax.experimental import pallas as pl
from jax.experimental.pallas import tpu as pltpu
from jax.sharding import PartitionSpec as P

OMEGA = 0.8
SHIFT = 0.1
DIAG = 1.0 + SHIFT
C = OMEGA / DIAG
Z0 = 2.0 * C - DIAG * C * C
Z1 = C * C
G0, G1, G2 = 1.0 - DIAG * Z0, Z0 - DIAG * Z1, Z1
KEEP = 1.0 - DIAG * C
B0, B1, B2 = KEEP * Z0 + C, KEEP * Z1 + C * Z0, C * Z1

K = 8
LX, LY, NZ = 8, 16, 256
CX, CY, CZ = LX // 2, LY // 2, NZ // 2
H = 3
CH = 4
JW = 8
MIB = 1024 * 1024
VMEM = pl.BlockSpec(memory_space=pltpu.VMEM)


def call(body, outs, ins, scratch=(), flops=1_000_000):
    nbytes = sum(4 * a.size for a in ins)
    return pl.pallas_call(
        body,
        out_shape=[jax.ShapeDtypeStruct(s, jnp.float32) for s in outs],
        in_specs=[VMEM] * len(ins),
        out_specs=[VMEM] * len(outs),
        scratch_shapes=[pltpu.VMEM(s, jnp.float32) for s in scratch],
        compiler_params=pltpu.CompilerParams(vmem_limit_bytes=56 * MIB),
        cost_estimate=pl.CostEstimate(flops=flops, bytes_accessed=nbytes, transcendentals=0),
    )(*ins)


def row(ref, *at):
    *lead, r = at
    r_ = ref[(*lead, pl.ds(r, 1), slice(None))]
    return jnp.broadcast_to(r_, (8, r_.shape[-1]))


def up_z(a):
    return pltpu.roll(a, a.shape[-1] - 1, a.ndim - 1)


def down_z(a):
    return pltpu.roll(a, 1, a.ndim - 1)


def prepare(v, wx, wy, wz, vt, wm, xu, xd, ylo, yhi):
    last_x = lax.axis_index("gx") == lax.axis_size("gx") - 1
    last_y = lax.axis_index("gy") == lax.axis_size("gy") - 1
    keep_x = jnp.where(last_x, 0.0, 1.0)
    keep_y = jnp.where(last_y, 0.0, 1.0)
    for x in range(LX):
        for t in range(0, LY, 8):
            vt[x, t : t + 8] = jnp.swapaxes(v[:, x, t : t + 8, :], 0, 1)
    wm[0] = wx[...]
    wm[0, LX - 1] = wx[LX - 1] * keep_x
    sub = lax.broadcasted_iota(jnp.int32, (LX, LY, NZ), 1)
    wm[1] = jnp.where(sub == LY - 1, wy[...] * keep_y, wy[...])
    lane = lax.broadcasted_iota(jnp.int32, (LX, LY, NZ), 2)
    wm[2] = jnp.where(lane == NZ - 1, 0.0, wz[...])
    for d in range(H):
        xu[d * LY : (d + 1) * LY] = vt[LX - H + d]
        xd[d * LY : (d + 1) * LY] = vt[d]
    at = H * LY
    for w, x in UP_W:
        xu[at] = wm[w, x, 0:8]
        xu[at + 1] = wm[w, x, 8:16]
        at += 2
    at = H * LY
    for w, x in DN_W:
        xd[at] = wm[w, x, 0:8]
        xd[at + 1] = wm[w, x, 8:16]
        at += 2
    ylo[...] = vt[:, 0:H]
    yhi[...] = vt[:, LY - H : LY]


UP_W = [(0, 5), (0, 6), (0, 7), (1, 6), (1, 7), (2, 6), (2, 7)]
DN_W = [(0, 0), (0, 1), (1, 0), (1, 1), (2, 0), (2, 1)]
NXB = H * LY + 2 * len(UP_W)
YV = [(d, p) for d in (1, 2, 3) for p in range(d - H, LX + H - d)]
YP = list(range(-2, LX + 2))
NYB = len(YV) + len(YP)


def weight_plane(wm, xl, xr, w, p):
    if 0 <= p < LX:
        return wm[w, p, 0:8], wm[w, p, 8:16]
    if p < 0:
        at = H * LY + 2 * UP_W.index((w, p + LX))
        return xl[at], xl[at + 1]
    at = H * LY + 2 * DN_W.index((w, p - LX))
    return xr[at], xr[at + 1]


def fine_y_send(wm, ylo, yhi, xl, xr, yu, yd):
    def cell(p, y):
        if p < 0:
            return xl[(p + H) * LY + y]
        if p >= LX:
            return xr[(p - LX) * LY + y]
        return ylo[p, y] if y < H else yhi[p, y - (LY - H)]

    for n, (d, p) in enumerate(YV):
        yu[n] = cell(p, LY - d)
        yd[n] = cell(p, d - 1)
    for n, p in enumerate(YP, len(YV)):
        wxl, wxh = weight_plane(wm, xl, xr, 0, p)
        wyl, wyh = weight_plane(wm, xl, xr, 1, p)
        wzl, wzh = weight_plane(wm, xl, xr, 2, p)
        yu[n, 0:2] = wxh[6:8]
        yu[n, 2:5] = wyh[5:8]
        yu[n, 5:7] = wzh[6:8]
        yu[n, 7:8] = wzh[7:8]
        yd[n, 0:2] = wxl[0:2]
        yd[n, 2:4] = wyl[0:2]
        yd[n, 4:6] = wzl[0:2]
        yd[n, 6:8] = wzl[0:2]


def planes(radius, body, own, halo):
    def step(n, _):
        body(n + halo, radius)
        return 0

    lax.fori_loop(0, own, step, 0)
    for d in range(1, radius + 1):
        body(halo - d, radius - d)
        body(halo + own - 1 + d, radius - d)


def compress(a, odd=False):
    lane = lax.broadcasted_iota(jnp.int32, (8, 128), 1)
    t = a if odd else a + up_z(a)
    at = (2 * lane + (1 if odd else 0)) & 127
    lo = jnp.take_along_axis(t[:, :128], at, 1)
    hi = jnp.take_along_axis(t[:, 128:], at, 1)
    return jnp.where(lane < 64, lo, hi)


def expand(a):
    lane = lax.broadcasted_iota(jnp.int32, (8, 128), 1)
    half = lane >> 1
    return jnp.concatenate(
        [jnp.take_along_axis(a, half, 1), jnp.take_along_axis(a, half + 64, 1)], 1
    )


def fine_level(vt, wm, xl, xr, yl, yr, pb, nwo, xs, nd, V, W, NW, Y1, Y2, Y3, CW, Q):
    V[H : H + LX, H : H + LY] = vt[...]
    for d in range(H):
        V[d, H : H + LY] = xl[d * LY : (d + 1) * LY]
        V[H + LX + d, H : H + LY] = xr[d * LY : (d + 1) * LY]
    for n, (d, p) in enumerate(YV):
        V[p + H, H - d] = yl[n]
        V[p + H, H + LY - 1 + d] = yr[n]
    for p in range(-H, LX + 2):
        for w in range(3):
            if p == -H and w:
                continue
            lo, hi = weight_plane(wm, xl, xr, w, p)
            W[w, p + H, JW : JW + 8] = lo
            W[w, p + H, JW + 8 : JW + 16] = hi
    for n, p in enumerate(YP, len(YV)):
        i = p + H
        W[0, i, JW - 2 : JW] = yl[n, 0:2]
        W[1, i, JW - 3 : JW] = yl[n, 2:5]
        W[2, i, JW - 2 : JW] = yl[n, 5:7]
        W[0, i, JW + LY : JW + LY + 2] = yr[n, 0:2]
        W[1, i, JW + LY : JW + LY + 2] = yr[n, 2:4]
        W[2, i, JW + LY : JW + LY + 2] = yr[n, 4:6]

    def norm(i, _):
        wx, lx = W[0, i], W[0, i - 1]
        wy = W[1, i]
        ly = pltpu.roll(wy, 1, 0)
        wz = W[2, i]
        lz = down_z(wz)
        deg = wx + lx + wy + ly + wz + lz
        inv = 1.0 / deg
        for a, w in enumerate((wx, lx, wy, ly, wz, lz)):
            NW[a, i] = w * inv
        NW[6, i] = deg
        return 0

    lax.fori_loop(1, LX + 5, norm, 0)

    def apply(src, dst):
        def body(i, reach):
            for j in range(H - reach, H + LY + reach):
                r = j - H + JW
                c = src[i, j]
                dst[i, j] = (
                    row(NW, 0, i, r) * src[i + 1, j]
                    + row(NW, 1, i, r) * src[i - 1, j]
                    + row(NW, 2, i, r) * src[i, j + 1]
                    + row(NW, 3, i, r) * src[i, j - 1]
                    + row(NW, 4, i, r) * up_z(c)
                    + row(NW, 5, i, r) * down_z(c)
                )

        return body

    planes(2, apply(V, Y1), LX, H)
    planes(1, apply(Y1, Y2), LX, H)
    planes(0, apply(Y2, Y3), LX, H)

    for x in range(CX):
        i = 2 * x + H
        own = slice(JW, JW + LY)
        wx, lx = W[0, i + 1, own], W[0, i - 1, own]
        wy = W[1, i] + W[1, i + 1]
        ly = pltpu.roll(wy, 1, 0)
        wz = W[2, i, own] + W[2, i + 1, own]
        dg = NW[6, i, own] + NW[6, i + 1, own]
        for q, (a, odd) in enumerate(
            ((wx, False), (lx, False), (wy[own], False), (ly[own], False), (wz, True), (dg, False))
        ):
            Q[q, x * LY : x * LY + 8] = compress(a[0:8], odd)
            Q[q, x * LY + 8 : x * LY + 16] = compress(a[8:16], odd)
    ri = lax.broadcasted_iota(jnp.int32, (CX * CY, CX * LY), 0)
    ci = lax.broadcasted_iota(jnp.int32, (CX * CY, CX * LY), 1)
    both = jnp.where((ci >> 1) == ri, 1.0, 0.0)
    first = jnp.where(ci == 2 * ri, 1.0, 0.0)
    second = jnp.where(ci == 2 * ri + 1, 1.0, 0.0)

    def rows(m, q):
        return jnp.dot(m, Q[q], precision=lax.Precision.HIGHEST, preferred_element_type=jnp.float32)

    cx, lcx = rows(both, 0), rows(both, 1)
    cy, lcy = rows(second, 2), rows(first, 3)
    cz, dsum = rows(both, 4), rows(both, 5)
    lcz = down_z(cz)
    dc = cx + lcx + cy + lcy + cz + lcz + SHIFT * dsum
    inv = 1.0 / dc
    for a, w in enumerate((cx, lcx, cy, lcy, cz, lcz)):
        w = w * inv
        for x in range(CX):
            xs[2 * CX * CY + 6 * x + a] = w[x * CY : (x + 1) * CY]
    for x in range(CX):
        CW[x] = inv[x * CY : (x + 1) * CY]
    for a in range(7):
        nwo[a] = NW[a, H : H + LX, JW : JW + LY]

    def block(x, sums):
        num, den = sums
        for y in range(CY):
            ra = rb = None
            for dx in range(2):
                for dy in range(2):
                    i = H + 2 * x + dx
                    j = H + 2 * y + dy
                    v, y1, y2, y3 = V[i, j], Y1[i, j], Y2[i, j], Y3[i, j]
                    deg = row(NW, 6, i, j - H + JW)
                    gb = G0 * v + G1 * y1 + G2 * y2
                    ga = gb - (G0 * y1 + G1 * y2 + G2 * y3)
                    b = B0 * v + B1 * y1 + B2 * y2
                    pb[i - H, j - H, 0:8] = v - (b - (B0 * y1 + B1 * y2 + B2 * y3))
                    pb[i - H, j - H, 8:16] = b
                    dv = deg * v
                    num = num + dv * (v - y1)
                    den = den + dv * v
                    ra = deg * ga if ra is None else ra + deg * ga
                    rb = deg * gb if rb is None else rb + deg * gb
            over = row(CW, x, y)
            at = 2 * (x * CY + y)
            xs[at] = compress(ra) * over
            xs[at + 1] = compress(rb) * over
        return num, den

    zero = jnp.zeros((8, NZ), jnp.float32)
    num, den = lax.fori_loop(0, CX, block, (zero, zero))
    nd[0] = num
    nd[1] = den


NCS = 2 * CX * CY + 6 * CX
CF = [(d, i) for d in (1, 2, 3, 4) for i in range(d, CX + 2 * CH - d)]
CP = list(range(2, CX + 2 * CH - 2))
NCY = 2 * len(CF) + 3 * len(CP)


def coarse_plane(own, left, right, i):
    if i < CH:
        return left, i
    if i < CH + CX:
        return own, i - CH
    return right, i - CH - CX


def coarse_y_send(own, left, right, yu, yd):
    for n, (d, i) in enumerate(CF):
        src, x = coarse_plane(own, left, right, i)
        for half in range(2):
            yu[2 * n + half] = src[2 * (x * CY + CY - d) + half]
            yd[2 * n + half] = src[2 * (x * CY + d - 1) + half]
    at = 2 * len(CF)
    for i in CP:
        src, x = coarse_plane(own, left, right, i)
        for t in range(3):
            for u in range(2):
                w = 2 * CX * CY + 6 * x + 2 * t + u
                yu[at, 4 * u : 4 * u + 4] = src[w, 4:8]
                yd[at, 4 * u : 4 * u + 4] = src[w, 0:4]
            at += 1


def coarse_level(own, left, right, yl, yr, pb, nwo, nd, po, bo, sums, F, CW, EA, EB, EX):
    JC = 8
    for i in range(CX + 2 * CH):
        src, x = coarse_plane(own, left, right, i)
        for y in range(CY):
            at = 2 * (x * CY + y)
            for half in range(2):
                f = OMEGA * src[at + half]
                F[i, y + CH, half] = f
                EA[i, y + CH, half] = f
        for a in range(6):
            CW[a, i, JC : JC + CY] = OMEGA * src[2 * CX * CY + 6 * x + a]
    for n, (d, i) in enumerate(CF):
        for half in range(2):
            lo = OMEGA * yl[2 * n + half]
            hi = OMEGA * yr[2 * n + half]
            F[i, CH - d, half] = lo
            EA[i, CH - d, half] = lo
            F[i, CH + CY - 1 + d, half] = hi
            EA[i, CH + CY - 1 + d, half] = hi
    at = 2 * len(CF)
    for i in CP:
        for t in range(3):
            for u in range(2):
                CW[2 * t + u, i, JC - 4 : JC] = OMEGA * yl[at, 4 * u : 4 * u + 4]
                CW[2 * t + u, i, JC + CY : JC + CY + 4] = OMEGA * yr[at, 4 * u : 4 * u + 4]
            at += 1

    def sweep(src, dst):
        def body(i, reach):
            for j in range(CH - reach, CH + CY + reach):
                r = j - CH + JC
                ws = [row(CW, a, i, r) for a in range(6)]
                for half in range(2):
                    c = src[i, j, half]
                    dst[i, j, half] = (
                        (1.0 - OMEGA) * c
                        + F[i, j, half]
                        + ws[0] * src[i + 1, j, half]
                        + ws[1] * src[i - 1, j, half]
                        + ws[2] * src[i, j + 1, half]
                        + ws[3] * src[i, j - 1, half]
                        + ws[4] * up_z(c)
                        + ws[5] * down_z(c)
                    )

        return body

    planes(3, sweep(EA, EB), CX, CH)
    planes(2, sweep(EB, EA), CX, CH)
    planes(1, sweep(EA, EB), CX, CH)

    def spread(i, reach):
        for j in range(CH - reach, CH + CY + reach):
            for half in range(2):
                EX[i, j, half] = expand(EB[i, j, half])

    planes(1, spread, CX, CH)

    def block(x, _):
        for y in range(CY):
            for half in range(2):
                e = EX[x + CH, y + CH, half]
                ez = (up_z(e), down_z(e))
                ke = KEEP * e
                ce = C * e
                for dx in range(2):
                    ex = C * EX[x + CH + 2 * dx - 1, y + CH, half]
                    for dy in range(2):
                        ey = C * EX[x + CH, y + CH + 2 * dy - 1, half]
                        xx, yy = 2 * x + dx, 2 * y + dy
                        nw = [row(nwo, a, xx, yy) for a in range(6)]
                        s = (
                            ke
                            + (nw[dx] + nw[2 + dy]) * ce
                            + nw[1 - dx] * ex
                            + nw[3 - dy] * ey
                            + C * (nw[4] * ez[0] + nw[5] * ez[1])
                        )
                        if half == 0:
                            po[xx, yy] = pb[xx, yy, 0:8] - s
                        else:
                            bo[xx, yy] = pb[xx, yy, 8:16] + s
        return 0

    lax.fori_loop(0, CX, block, 0)

    def gram(n, acc):
        x = n >> 2
        acc = list(acc)
        for q in range(4):
            yy = (n & 3) * 4 + q
            deg = row(nwo, 6, x, yy)
            for h in range(0, NZ, 128):
                z = slice(h, h + 128)
                p = po[x, yy, :, z]
                b = bo[x, yy, :, z]
                dp = deg[:, z] * p
                db = deg[:, z] * b
                for s in range(8):
                    rb = pltpu.roll(db, s, 0) if s else db
                    if s < 5:
                        rp = pltpu.roll(dp, s, 0) if s else dp
                        acc[s] = acc[s] + p * rp
                        acc[5 + s] = acc[5 + s] + b * rb
                    acc[10 + s] = acc[10 + s] + p * rb
        return tuple(acc)

    zero = jnp.zeros((8, 128), jnp.float32)
    acc = list(lax.fori_loop(0, 4 * LX, gram, (zero,) * 18))
    for q in range(2):
        acc.append(nd[q, :, :128] + nd[q, :, 128:])
    ones = jnp.ones((8, 128), jnp.float32)

    def over_lanes(m):
        return lax.dot_general(
            ones,
            m,
            (((1,), (1,)), ((), ())),
            precision=lax.Precision.HIGHEST,
            preferred_element_type=jnp.float32,
        )

    t0 = over_lanes(jnp.concatenate(acc[:16], 0))
    t1 = over_lanes(jnp.concatenate(acc[16:] + [zero] * 12, 0))
    sums[0:1] = t0[0:1]
    sums[1:2] = t1[0:1]


def finish(parts, po, bo, out, eig, SP):
    t = parts[...]
    n = t.shape[0]
    while n > 1:
        n //= 2
        t = t[:n] + t[n:]
    t = t[0]
    eye = lax.broadcasted_iota(jnp.int32, (128, 128), 0) == lax.broadcasted_iota(
        jnp.int32, (128, 128), 1
    )
    ones = jnp.ones((128, 128), jnp.float32)
    for q in range(2):
        m = jnp.where(eye, jnp.broadcast_to(t[q : q + 1], (128, 128)), 0.0)
        SP[128 * q : 128 * (q + 1)] = jnp.dot(
            m, ones, precision=lax.Precision.HIGHEST, preferred_element_type=jnp.float32
        )
    eig[...] = jnp.broadcast_to(t[1:2] / pltpu.roll(t[1:2], 120, 1), (8, 128))

    def entry(block, k):
        return row(SP, 8 * block + k)

    def sym(base, a, b):
        s = (a - b) % 8
        return entry(base + s, a) if s < 5 else entry(base + 8 - s, b)

    def cross(a, b):
        return entry(10 + (a - b) % 8, a)

    lam = [entry(18, k) / entry(19, k) for k in range(K)]
    voxels = LX * LY * NZ * lax.axis_size("gx") * lax.axis_size("gy")
    g = {}
    for a in range(K):
        for b in range(a + 1):
            g[a, b] = (
                sym(0, a, b) + lam[b] * cross(a, b) + lam[a] * (cross(b, a) + lam[b] * sym(5, a, b))
            ) * (1.0 / voxels)
    low, inv = {}, []
    for j in range(K):
        d = g[j, j]
        r = lax.rsqrt(d)
        r = r * (1.5 - 0.5 * d * r * r)
        inv.append(r)
        for a in range(j + 1, K):
            low[a, j] = g[a, j] * r
        for a in range(j + 1, K):
            for b in range(j + 1, a + 1):
                g[a, b] = g[a, b] - low[a, j] * low[b, j]

    for k in range(K):
        SP[8 * k : 8 * k + 8] = lam[k]
        SP[64 + 8 * k : 72 + 8 * k] = inv[k]
    at = {}
    for n, (a, b) in enumerate(sorted(low)):
        at[a, b] = 128 + 8 * n
        SP[128 + 8 * n : 136 + 8 * n] = low[a, b]

    def body(x, _):
        for t in range(0, LY, 8):
            for h in range(0, NZ, 128):
                z = slice(h, h + 128)
                p = jnp.swapaxes(po[x, t : t + 8, :, z], 0, 1)
                b = jnp.swapaxes(bo[x, t : t + 8, :, z], 0, 1)
                done = []
                for k in range(K):
                    u = p[k] + SP[8 * k : 8 * k + 8] * b[k]
                    for j in range(k):
                        u = u - SP[at[k, j] : at[k, j] + 8] * done[j]
                    u = u * SP[64 + 8 * k : 72 + 8 * k]
                    done.append(u)
                    out[k, x, t : t + 8, z] = u
        return 0

    lax.fori_loop(0, LX, body, 0)


def both_ways(up, down, axis):
    n = lax.axis_size(axis)
    fwd = [(i, (i + 1) % n) for i in range(n)]
    back = [((i + 1) % n, i) for i in range(n)]
    return lax.ppermute(up, axis, fwd), lax.ppermute(down, axis, back)


def per_device(vectors, weight_x, weight_y, weight_z):
    vt, wm, xu, xd, ylo, yhi = call(
        prepare,
        [
            (LX, LY, K, NZ),
            (3, LX, LY, NZ),
            (NXB, 8, NZ),
            (NXB, 8, NZ),
            (LX, H, K, NZ),
            (LX, H, K, NZ),
        ],
        (vectors, weight_x, weight_y, weight_z),
    )
    xl, xr = both_ways(xu, xd, "gx")
    yu, yd = call(fine_y_send, [(NYB, 8, NZ)] * 2, (wm, ylo, yhi, xl, xr))
    yl, yr = both_ways(yu, yd, "gy")
    ext = (LX + 2 * H, LY + 2 * H, K, NZ)
    pb, nwo, xs, nd = call(
        fine_level,
        [(LX, LY, 16, NZ), (7, LX, LY, NZ), (NCS, 8, CZ), (2, 8, NZ)],
        (vt, wm, xl, xr, yl, yr),
        [
            ext,
            (3, LX + 2 * H, 32, NZ),
            (7, LX + 2 * H, 32, NZ),
            ext,
            ext,
            ext,
            (CX, CY, CZ),
            (6, CX * LY, CZ),
        ],
    )
    cl, cr = both_ways(xs, xs, "gx")
    yu, yd = call(coarse_y_send, [(NCY, 8, CZ)] * 2, (xs, cl, cr))
    yl, yr = both_ways(yu, yd, "gy")
    cext = (CX + 2 * CH, CY + 2 * CH, 2, 8, CZ)
    po, bo, sums = call(
        coarse_level,
        [(LX, LY, K, NZ), (LX, LY, K, NZ), (2, 128)],
        (xs, cl, cr, yl, yr, pb, nwo, nd),
        [
            cext,
            (6, CX + 2 * CH, 24, CZ),
            cext,
            cext,
            (CX + 2 * CH, CY + 2 * CH, 2, 8, NZ),
        ],
    )
    n = lax.axis_size("gx") * lax.axis_size("gy")
    parts = lax.all_to_all(jnp.broadcast_to(sums[None], (n, 2, 128)), ("gx", "gy"), 0, 0)
    refined, eig = call(
        finish,
        [(K, LX, LY, NZ), (8, 128)],
        (parts, po, bo),
        [(384, 128)],
    )
    return refined, eig[0, 16:24]


def solution(mesh):
    return jax.shard_map(
        per_device,
        mesh=mesh,
        in_specs=(
            P(None, "gx", "gy", None),
            P("gx", "gy", None),
            P("gx", "gy", None),
            P("gx", "gy", None),
        ),
        out_specs=(P(None, "gx", "gy", None), P()),
        check_vma=False,
    )
```

```python
import jax
import jax.numpy as jnp
from jax import lax
from jax.experimental import pallas as pl
from jax.experimental.pallas import tpu as pltpu
from jax.sharding import PartitionSpec as P

OMEGA = 0.8
SHIFT = 0.1
DIAG = 1.0 + SHIFT
C = OMEGA / DIAG
Z0 = 2.0 * C - DIAG * C * C
Z1 = C * C
G0, G1, G2 = 1.0 - DIAG * Z0, Z0 - DIAG * Z1, Z1
KEEP = 1.0 - DIAG * C
B0, B1, B2 = KEEP * Z0 + C, KEEP * Z1 + C * Z0, C * Z1

K = 8
LX, LY, NZ = 8, 16, 256
CX, CY, CZ = LX // 2, LY // 2, NZ // 2
H = 3
CH = 4
JW = 8
MIB = 1024 * 1024
VMEM = pl.BlockSpec(memory_space=pltpu.VMEM)


def call(body, outs, ins, scratch=(), limit=10):
    nbytes = sum(4 * a.size for a in ins)
    return pl.pallas_call(
        body,
        out_shape=[jax.ShapeDtypeStruct(s, jnp.float32) for s in outs],
        in_specs=[VMEM] * len(ins),
        out_specs=[VMEM] * len(outs),
        scratch_shapes=[pltpu.VMEM(s, jnp.float32) for s in scratch],
        compiler_params=pltpu.CompilerParams(vmem_limit_bytes=limit * MIB),
        cost_estimate=pl.CostEstimate(flops=1_000_000, bytes_accessed=nbytes, transcendentals=0),
    )(*ins)


def row(ref, *at):
    *lead, r = at
    r_ = ref[(*lead, pl.ds(r, 1), slice(None))]
    return jnp.broadcast_to(r_, (8, r_.shape[-1]))


def up_z(a):
    return pltpu.roll(a, a.shape[-1] - 1, a.ndim - 1)


def down_z(a):
    return pltpu.roll(a, 1, a.ndim - 1)


def prepare(v, wx, wy, wz, vt, wm, xu, xd, ylo, yhi):
    last_x = lax.axis_index("gx") == lax.axis_size("gx") - 1
    last_y = lax.axis_index("gy") == lax.axis_size("gy") - 1
    keep_x = jnp.where(last_x, 0.0, 1.0)
    keep_y = jnp.where(last_y, 0.0, 1.0)
    for x in range(LX):
        for t in range(0, LY, 8):
            vt[x, t : t + 8] = jnp.swapaxes(v[:, x, t : t + 8, :], 0, 1)
    wm[0] = wx[...]
    wm[0, LX - 1] = wx[LX - 1] * keep_x
    sub = lax.broadcasted_iota(jnp.int32, (LX, LY, NZ), 1)
    wm[1] = jnp.where(sub == LY - 1, wy[...] * keep_y, wy[...])
    lane = lax.broadcasted_iota(jnp.int32, (LX, LY, NZ), 2)
    wm[2] = jnp.where(lane == NZ - 1, 0.0, wz[...])
    for d in range(H):
        xu[d * LY : (d + 1) * LY] = vt[LX - H + d]
        xd[d * LY : (d + 1) * LY] = vt[d]
    at = H * LY
    for w, x in UP_W:
        xu[at] = wm[w, x, 0:8]
        xu[at + 1] = wm[w, x, 8:16]
        at += 2
    at = H * LY
    for w, x in DN_W:
        xd[at] = wm[w, x, 0:8]
        xd[at + 1] = wm[w, x, 8:16]
        at += 2
    ylo[...] = vt[:, 0:H]
    yhi[...] = vt[:, LY - H : LY]


UP_W = [(0, 5), (0, 6), (0, 7), (1, 6), (1, 7), (2, 6), (2, 7)]
DN_W = [(0, 0), (0, 1), (1, 0), (1, 1), (2, 0), (2, 1)]
NXB = H * LY + 2 * len(UP_W)
YV = [(d, p) for d in (1, 2, 3) for p in range(d - H, LX + H - d)]
YP = list(range(-2, LX + 2))
NYB = len(YV) + len(YP)


def weight_plane(wm, xl, xr, w, p):
    if 0 <= p < LX:
        return wm[w, p, 0:8], wm[w, p, 8:16]
    if p < 0:
        at = H * LY + 2 * UP_W.index((w, p + LX))
        return xl[at], xl[at + 1]
    at = H * LY + 2 * DN_W.index((w, p - LX))
    return xr[at], xr[at + 1]


def fine_y_send(wm, ylo, yhi, xl, xr, yu, yd):
    def cell(p, y):
        if p < 0:
            return xl[(p + H) * LY + y]
        if p >= LX:
            return xr[(p - LX) * LY + y]
        return ylo[p, y] if y < H else yhi[p, y - (LY - H)]

    for n, (d, p) in enumerate(YV):
        yu[n] = cell(p, LY - d)
        yd[n] = cell(p, d - 1)
    for n, p in enumerate(YP, len(YV)):
        wxl, wxh = weight_plane(wm, xl, xr, 0, p)
        wyl, wyh = weight_plane(wm, xl, xr, 1, p)
        wzl, wzh = weight_plane(wm, xl, xr, 2, p)
        yu[n, 0:2] = wxh[6:8]
        yu[n, 2:5] = wyh[5:8]
        yu[n, 5:7] = wzh[6:8]
        yu[n, 7:8] = wzh[7:8]
        yd[n, 0:2] = wxl[0:2]
        yd[n, 2:4] = wyl[0:2]
        yd[n, 4:6] = wzl[0:2]
        yd[n, 6:8] = wzl[0:2]


def planes(radius, body, own, halo):
    def step(n, _):
        body(n + halo, radius)
        return 0

    lax.fori_loop(0, own, step, 0)
    for d in range(1, radius + 1):
        body(halo - d, radius - d)
        body(halo + own - 1 + d, radius - d)


def compress(a, odd=False):
    lane = lax.broadcasted_iota(jnp.int32, (8, 128), 1)
    t = a if odd else a + up_z(a)
    at = (2 * lane + (1 if odd else 0)) & 127
    lo = jnp.take_along_axis(t[:, :128], at, 1)
    hi = jnp.take_along_axis(t[:, 128:], at, 1)
    return jnp.where(lane < 64, lo, hi)


def expand(a):
    lane = lax.broadcasted_iota(jnp.int32, (8, 128), 1)
    half = lane >> 1
    return jnp.concatenate(
        [jnp.take_along_axis(a, half, 1), jnp.take_along_axis(a, half + 64, 1)], 1
    )


def fine_level(vt, wm, xl, xr, yl, yr, pb, nwo, xs, nd, V, W, NW, Y1, Y2, Y3, CW, Q):
    V[H : H + LX, H : H + LY] = vt[...]
    for d in range(H):
        V[d, H : H + LY] = xl[d * LY : (d + 1) * LY]
        V[H + LX + d, H : H + LY] = xr[d * LY : (d + 1) * LY]
    for n, (d, p) in enumerate(YV):
        V[p + H, H - d] = yl[n]
        V[p + H, H + LY - 1 + d] = yr[n]
    for p in range(-H, LX + 2):
        for w in range(3):
            if p == -H and w:
                continue
            lo, hi = weight_plane(wm, xl, xr, w, p)
            W[w, p + H, JW : JW + 8] = lo
            W[w, p + H, JW + 8 : JW + 16] = hi
    for n, p in enumerate(YP, len(YV)):
        i = p + H
        W[0, i, JW - 2 : JW] = yl[n, 0:2]
        W[1, i, JW - 3 : JW] = yl[n, 2:5]
        W[2, i, JW - 2 : JW] = yl[n, 5:7]
        W[0, i, JW + LY : JW + LY + 2] = yr[n, 0:2]
        W[1, i, JW + LY : JW + LY + 2] = yr[n, 2:4]
        W[2, i, JW + LY : JW + LY + 2] = yr[n, 4:6]

    def norm(i, _):
        wx, lx = W[0, i], W[0, i - 1]
        wy = W[1, i]
        ly = pltpu.roll(wy, 1, 0)
        wz = W[2, i]
        lz = down_z(wz)
        deg = wx + lx + wy + ly + wz + lz
        inv = 1.0 / deg
        for a, w in enumerate((wx, lx, wy, ly, wz, lz)):
            NW[a, i] = w * inv
        NW[6, i] = deg
        return 0

    lax.fori_loop(1, LX + 5, norm, 0)

    def apply(src, dst):
        def body(i, reach):
            for j in range(H - reach, H + LY + reach):
                r = j - H + JW
                c = src[i, j]
                dst[i, j] = (
                    row(NW, 0, i, r) * src[i + 1, j]
                    + row(NW, 1, i, r) * src[i - 1, j]
                    + row(NW, 2, i, r) * src[i, j + 1]
                    + row(NW, 3, i, r) * src[i, j - 1]
                    + row(NW, 4, i, r) * up_z(c)
                    + row(NW, 5, i, r) * down_z(c)
                )

        return body

    planes(2, apply(V, Y1), LX, H)
    planes(1, apply(Y1, Y2), LX, H)
    planes(0, apply(Y2, Y3), LX, H)

    for x in range(CX):
        i = 2 * x + H
        own = slice(JW, JW + LY)
        wx, lx = W[0, i + 1, own], W[0, i - 1, own]
        wy = W[1, i] + W[1, i + 1]
        ly = pltpu.roll(wy, 1, 0)
        wz = W[2, i, own] + W[2, i + 1, own]
        dg = NW[6, i, own] + NW[6, i + 1, own]
        for q, (a, odd) in enumerate(
            ((wx, False), (lx, False), (wy[own], False), (ly[own], False), (wz, True), (dg, False))
        ):
            Q[q, x * LY : x * LY + 8] = compress(a[0:8], odd)
            Q[q, x * LY + 8 : x * LY + 16] = compress(a[8:16], odd)
    ri = lax.broadcasted_iota(jnp.int32, (CX * CY, CX * LY), 0)
    ci = lax.broadcasted_iota(jnp.int32, (CX * CY, CX * LY), 1)
    both = jnp.where((ci >> 1) == ri, 1.0, 0.0)
    first = jnp.where(ci == 2 * ri, 1.0, 0.0)
    second = jnp.where(ci == 2 * ri + 1, 1.0, 0.0)

    def rows(m, q):
        return jnp.dot(m, Q[q], precision=lax.Precision.HIGHEST, preferred_element_type=jnp.float32)

    cx, lcx = rows(both, 0), rows(both, 1)
    cy, lcy = rows(second, 2), rows(first, 3)
    cz, dsum = rows(both, 4), rows(both, 5)
    lcz = down_z(cz)
    dc = cx + lcx + cy + lcy + cz + lcz + SHIFT * dsum
    inv = 1.0 / dc
    for a, w in enumerate((cx, lcx, cy, lcy, cz, lcz)):
        w = w * inv
        for x in range(CX):
            xs[2 * CX * CY + 6 * x + a] = w[x * CY : (x + 1) * CY]
    for x in range(CX):
        CW[x] = inv[x * CY : (x + 1) * CY]
    for a in range(7):
        nwo[a] = NW[a, H : H + LX, JW : JW + LY]

    def block(x, sums):
        num, den = sums
        for y in range(CY):
            ra = rb = None
            for dx in range(2):
                for dy in range(2):
                    i = H + 2 * x + dx
                    j = H + 2 * y + dy
                    v, y1, y2, y3 = V[i, j], Y1[i, j], Y2[i, j], Y3[i, j]
                    deg = row(NW, 6, i, j - H + JW)
                    gb = G0 * v + G1 * y1 + G2 * y2
                    ga = gb - (G0 * y1 + G1 * y2 + G2 * y3)
                    b = B0 * v + B1 * y1 + B2 * y2
                    pb[i - H, j - H, 0:8] = v - (b - (B0 * y1 + B1 * y2 + B2 * y3))
                    pb[i - H, j - H, 8:16] = b
                    dv = deg * v
                    num = num + dv * (v - y1)
                    den = den + dv * v
                    ra = deg * ga if ra is None else ra + deg * ga
                    rb = deg * gb if rb is None else rb + deg * gb
            over = row(CW, x, y)
            at = 2 * (x * CY + y)
            xs[at] = compress(ra) * over
            xs[at + 1] = compress(rb) * over
        return num, den

    zero = jnp.zeros((8, NZ), jnp.float32)
    num, den = lax.fori_loop(0, CX, block, (zero, zero))
    nd[0] = num
    nd[1] = den


NCS = 2 * CX * CY + 6 * CX
CF = [(d, i) for d in (1, 2, 3, 4) for i in range(d, CX + 2 * CH - d)]
CP = list(range(2, CX + 2 * CH - 2))
NCY = 2 * len(CF) + 3 * len(CP)


def coarse_plane(own, left, right, i):
    if i < CH:
        return left, i
    if i < CH + CX:
        return own, i - CH
    return right, i - CH - CX


def coarse_y_send(own, left, right, yu, yd):
    for n, (d, i) in enumerate(CF):
        src, x = coarse_plane(own, left, right, i)
        for half in range(2):
            yu[2 * n + half] = src[2 * (x * CY + CY - d) + half]
            yd[2 * n + half] = src[2 * (x * CY + d - 1) + half]
    at = 2 * len(CF)
    for i in CP:
        src, x = coarse_plane(own, left, right, i)
        for t in range(3):
            for u in range(2):
                w = 2 * CX * CY + 6 * x + 2 * t + u
                yu[at, 4 * u : 4 * u + 4] = src[w, 4:8]
                yd[at, 4 * u : 4 * u + 4] = src[w, 0:4]
            at += 1


def coarse_level(own, left, right, yl, yr, pb, nwo, nd, po, bo, sums, F, CW, EA, EB, EX):
    JC = 8
    for i in range(CX + 2 * CH):
        src, x = coarse_plane(own, left, right, i)
        for y in range(CY):
            at = 2 * (x * CY + y)
            for half in range(2):
                f = OMEGA * src[at + half]
                F[i, y + CH, half] = f
                EA[i, y + CH, half] = f
        for a in range(6):
            CW[a, i, JC : JC + CY] = OMEGA * src[2 * CX * CY + 6 * x + a]
    for n, (d, i) in enumerate(CF):
        for half in range(2):
            lo = OMEGA * yl[2 * n + half]
            hi = OMEGA * yr[2 * n + half]
            F[i, CH - d, half] = lo
            EA[i, CH - d, half] = lo
            F[i, CH + CY - 1 + d, half] = hi
            EA[i, CH + CY - 1 + d, half] = hi
    at = 2 * len(CF)
    for i in CP:
        for t in range(3):
            for u in range(2):
                CW[2 * t + u, i, JC - 4 : JC] = OMEGA * yl[at, 4 * u : 4 * u + 4]
                CW[2 * t + u, i, JC + CY : JC + CY + 4] = OMEGA * yr[at, 4 * u : 4 * u + 4]
            at += 1

    def sweep(src, dst):
        def body(i, reach):
            for j in range(CH - reach, CH + CY + reach):
                r = j - CH + JC
                ws = [row(CW, a, i, r) for a in range(6)]
                for half in range(2):
                    c = src[i, j, half]
                    dst[i, j, half] = (
                        (1.0 - OMEGA) * c
                        + F[i, j, half]
                        + ws[0] * src[i + 1, j, half]
                        + ws[1] * src[i - 1, j, half]
                        + ws[2] * src[i, j + 1, half]
                        + ws[3] * src[i, j - 1, half]
                        + ws[4] * up_z(c)
                        + ws[5] * down_z(c)
                    )

        return body

    planes(3, sweep(EA, EB), CX, CH)
    planes(2, sweep(EB, EA), CX, CH)
    planes(1, sweep(EA, EB), CX, CH)

    def spread(i, reach):
        for j in range(CH - reach, CH + CY + reach):
            for half in range(2):
                EX[i, j, half] = expand(EB[i, j, half])

    planes(1, spread, CX, CH)

    def block(x, _):
        for y in range(CY):
            for half in range(2):
                e = EX[x + CH, y + CH, half]
                ez = (up_z(e), down_z(e))
                ke = KEEP * e
                ce = C * e
                for dx in range(2):
                    ex = C * EX[x + CH + 2 * dx - 1, y + CH, half]
                    for dy in range(2):
                        ey = C * EX[x + CH, y + CH + 2 * dy - 1, half]
                        xx, yy = 2 * x + dx, 2 * y + dy
                        nw = [row(nwo, a, xx, yy) for a in range(6)]
                        s = (
                            ke
                            + (nw[dx] + nw[2 + dy]) * ce
                            + nw[1 - dx] * ex
                            + nw[3 - dy] * ey
                            + C * (nw[4] * ez[0] + nw[5] * ez[1])
                        )
                        if half == 0:
                            po[xx, yy] = pb[xx, yy, 0:8] - s
                        else:
                            bo[xx, yy] = pb[xx, yy, 8:16] + s
        return 0

    lax.fori_loop(0, CX, block, 0)

    def gram(n, acc):
        x = n >> 2
        acc = list(acc)
        for q in range(4):
            yy = (n & 3) * 4 + q
            deg = row(nwo, 6, x, yy)
            for h in range(0, NZ, 128):
                z = slice(h, h + 128)
                p = po[x, yy, :, z]
                b = bo[x, yy, :, z]
                dp = deg[:, z] * p
                db = deg[:, z] * b
                for s in range(8):
                    rb = pltpu.roll(db, s, 0) if s else db
                    if s < 5:
                        rp = pltpu.roll(dp, s, 0) if s else dp
                        acc[s] = acc[s] + p * rp
                        acc[5 + s] = acc[5 + s] + b * rb
                    acc[10 + s] = acc[10 + s] + p * rb
        return tuple(acc)

    zero = jnp.zeros((8, 128), jnp.float32)
    acc = list(lax.fori_loop(0, 4 * LX, gram, (zero,) * 18))
    for q in range(2):
        acc.append(nd[q, :, :128] + nd[q, :, 128:])
    ones = jnp.ones((8, 128), jnp.float32)

    def over_lanes(m):
        return lax.dot_general(
            ones,
            m,
            (((1,), (1,)), ((), ())),
            precision=lax.Precision.HIGHEST,
            preferred_element_type=jnp.float32,
        )

    t0 = over_lanes(jnp.concatenate(acc[:16], 0))
    t1 = over_lanes(jnp.concatenate(acc[16:] + [zero] * 12, 0))
    both = jnp.concatenate([t0[0:1], t1[0:1]], 0)
    sums[...] = jnp.broadcast_to(both[None], sums.shape)


def finish(parts, po, bo, out, eig, SP):
    t = parts[...]
    n = t.shape[0]
    while n > 1:
        n //= 2
        t = t[:n] + t[n:]
    t = t[0]
    eye = lax.broadcasted_iota(jnp.int32, (128, 128), 0) == lax.broadcasted_iota(
        jnp.int32, (128, 128), 1
    )
    ones = jnp.ones((128, 128), jnp.float32)
    for q in range(2):
        m = jnp.where(eye, jnp.broadcast_to(t[q : q + 1], (128, 128)), 0.0)
        SP[128 * q : 128 * (q + 1)] = jnp.dot(
            m, ones, precision=lax.Precision.HIGHEST, preferred_element_type=jnp.float32
        )
    lams = t[1:2] / pltpu.roll(t[1:2], 120, 1)
    eig[...] = pltpu.roll(lams, 112, 1)[:, :K]

    def entry(block, k):
        return row(SP, 8 * block + k)

    def sym(base, a, b):
        s = (a - b) % 8
        return entry(base + s, a) if s < 5 else entry(base + 8 - s, b)

    def cross(a, b):
        return entry(10 + (a - b) % 8, a)

    lam = [entry(18, k) / entry(19, k) for k in range(K)]
    voxels = LX * LY * NZ * lax.axis_size("gx") * lax.axis_size("gy")
    g = {}
    for a in range(K):
        for b in range(a + 1):
            g[a, b] = (
                sym(0, a, b) + lam[b] * cross(a, b) + lam[a] * (cross(b, a) + lam[b] * sym(5, a, b))
            ) * (1.0 / voxels)
    low, inv = {}, []
    for j in range(K):
        d = g[j, j]
        r = lax.rsqrt(d)
        r = r * (1.5 - 0.5 * d * r * r)
        inv.append(r)
        for a in range(j + 1, K):
            low[a, j] = g[a, j] * r
        for a in range(j + 1, K):
            for b in range(j + 1, a + 1):
                g[a, b] = g[a, b] - low[a, j] * low[b, j]

    for k in range(K):
        SP[8 * k : 8 * k + 8] = lam[k]
        SP[64 + 8 * k : 72 + 8 * k] = inv[k]
    at = {}
    for n, (a, b) in enumerate(sorted(low)):
        at[a, b] = 128 + 8 * n
        SP[128 + 8 * n : 136 + 8 * n] = low[a, b]

    def body(x, _):
        for t in range(0, LY, 8):
            for h in range(0, NZ, 128):
                z = slice(h, h + 128)
                p = jnp.swapaxes(po[x, t : t + 8, :, z], 0, 1)
                b = jnp.swapaxes(bo[x, t : t + 8, :, z], 0, 1)
                done = []
                for k in range(K):
                    u = p[k] + SP[8 * k : 8 * k + 8] * b[k]
                    for j in range(k):
                        u = u - SP[at[k, j] : at[k, j] + 8] * done[j]
                    u = u * SP[64 + 8 * k : 72 + 8 * k]
                    done.append(u)
                    out[k, x, t : t + 8, z] = u
        return 0

    lax.fori_loop(0, LX, body, 0)


def both_ways(up, down, axis):
    n = lax.axis_size(axis)
    fwd = [(i, (i + 1) % n) for i in range(n)]
    back = [((i + 1) % n, i) for i in range(n)]
    return lax.ppermute(up, axis, fwd), lax.ppermute(down, axis, back)


def per_device(vectors, weight_x, weight_y, weight_z):
    vt, wm, xu, xd, ylo, yhi = call(
        prepare,
        [
            (LX, LY, K, NZ),
            (3, LX, LY, NZ),
            (NXB, 8, NZ),
            (NXB, 8, NZ),
            (LX, H, K, NZ),
            (LX, H, K, NZ),
        ],
        (vectors, weight_x, weight_y, weight_z),
    )
    xl, xr = both_ways(xu, xd, "gx")
    yu, yd = call(fine_y_send, [(NYB, 8, NZ)] * 2, (wm, ylo, yhi, xl, xr))
    yl, yr = both_ways(yu, yd, "gy")
    ext = (LX + 2 * H, LY + 2 * H, K, NZ)
    pb, nwo, xs, nd = call(
        fine_level,
        [(LX, LY, 16, NZ), (7, LX, LY, NZ), (NCS, 8, CZ), (2, 8, NZ)],
        (vt, wm, xl, xr, yl, yr),
        [
            ext,
            (3, LX + 2 * H, 32, NZ),
            (7, LX + 2 * H, 32, NZ),
            ext,
            ext,
            ext,
            (CX, CY, CZ),
            (6, CX * LY, CZ),
        ],
        limit=24,
    )
    cl, cr = both_ways(xs, xs, "gx")
    yu, yd = call(coarse_y_send, [(NCY, 8, CZ)] * 2, (xs, cl, cr))
    yl, yr = both_ways(yu, yd, "gy")
    n = lax.axis_size("gx") * lax.axis_size("gy")
    cext = (CX + 2 * CH, CY + 2 * CH, 2, 8, CZ)
    po, bo, sums = call(
        coarse_level,
        [(LX, LY, K, NZ), (LX, LY, K, NZ), (n, 2, 128)],
        (xs, cl, cr, yl, yr, pb, nwo, nd),
        [
            cext,
            (6, CX + 2 * CH, 24, CZ),
            cext,
            cext,
            (CX + 2 * CH, CY + 2 * CH, 2, 8, NZ),
        ],
        limit=16,
    )
    parts = lax.all_to_all(sums, ("gx", "gy"), 0, 0)
    refined, eig = call(
        finish,
        [(K, LX, LY, NZ), (1, K)],
        (parts, po, bo),
        [(384, 128)],
    )
    return refined, eig.reshape(K)


def solution(mesh):
    return jax.shard_map(
        per_device,
        mesh=mesh,
        in_specs=(
            P(None, "gx", "gy", None),
            P("gx", "gy", None),
            P("gx", "gy", None),
            P("gx", "gy", None),
        ),
        out_specs=(P(None, "gx", "gy", None), P()),
        check_vma=False,
    )
```

```python
import jax
import jax.numpy as jnp
from jax import lax
from jax.experimental import pallas as pl
from jax.experimental.pallas import tpu as pltpu
from jax.sharding import PartitionSpec as P

OMEGA = 0.8
SHIFT = 0.1
DIAG = 1.0 + SHIFT
C = OMEGA / DIAG
Z0 = 2.0 * C - DIAG * C * C
Z1 = C * C
G0, G1, G2 = 1.0 - DIAG * Z0, Z0 - DIAG * Z1, Z1
KEEP = 1.0 - DIAG * C
B0, B1, B2 = KEEP * Z0 + C, KEEP * Z1 + C * Z0, C * Z1

K = 8
LX, LY, NZ = 8, 16, 256
CX, CY, CZ = LX // 2, LY // 2, NZ // 2
H = 3
CH = 4
JW = 8
MIB = 1024 * 1024
VMEM = pl.BlockSpec(memory_space=pltpu.VMEM)


HBM = pl.BlockSpec(memory_space=pltpu.HBM)


def call(body, outs, ins, scratch=(), limit=8, where=VMEM, us=1):
    return pl.pallas_call(
        body,
        out_shape=[jax.ShapeDtypeStruct(s, jnp.float32) for s in outs],
        in_specs=[where] * len(ins),
        out_specs=[VMEM] * len(outs),
        scratch_shapes=[pltpu.VMEM(s, jnp.float32) if isinstance(s, tuple) else s for s in scratch],
        compiler_params=pltpu.CompilerParams(vmem_limit_bytes=limit * MIB),
        cost_estimate=pl.CostEstimate(
            flops=0, bytes_accessed=us * 3_000_000, transcendentals=0
        ),
    )(*ins)


def row(ref, *at):
    *lead, r = at
    r_ = ref[(*lead, pl.ds(r, 1), slice(None))]
    return jnp.broadcast_to(r_, (8, r_.shape[-1]))


def up_z(a):
    return pltpu.roll(a, a.shape[-1] - 1, a.ndim - 1)


def down_z(a):
    return pltpu.roll(a, 1, a.ndim - 1)


UP_W = [(0, 5), (0, 6), (0, 7), (1, 6), (1, 7), (2, 6), (2, 7)]
DN_W = [(0, 0), (0, 1), (1, 0), (1, 1), (2, 0), (2, 1)]
NV = H * LY
NXU = NV + 2 * len(UP_W) + 2 * CX
NXD = NV + 2 * len(DN_W) + 2 * CX
NYB = H * LX + LX + CX
CELLS = [(1, 1), (1, 2), (2, 1)]
WP = [-2, -1, LX, LX + 1]
CWP = [-3, -2, -1, CX, CX + 1, CX + 2]
NCB = 2 * len(CELLS) + len(WP) + len(CWP)


def put_rows(up, down, n, lows, highs):
    up[n, 0:2] = highs[0][6:8]
    up[n, 2:5] = highs[1][5:8]
    up[n, 5:8] = highs[2][5:8]
    down[n, 0:2] = lows[0][0:2]
    down[n, 2:4] = lows[1][0:2]
    down[n, 4:8] = lows[2][0:4]


def put_coarse_rows(up, down, n, arrays):
    for a, w in enumerate(arrays):
        r, z = 4 * (a & 1), 128 * (a >> 1)
        up[n, r : r + 4, z : z + 128] = w[4:8]
        down[n, r : r + 4, z : z + 128] = w[0:4]


def coarse_rows(msg, n, a):
    r, z = 4 * (a & 1), 128 * (a >> 1)
    return msg[n, r : r + 4, z : z + 128]


def prepare(v_, wx_, wy_, wz_, vt, wm, cw, xu, xd, yu, yd, v, wx, wy, wz, Q, sem):
    copies = [
        pltpu.make_async_copy(a, b, sem.at[n])
        for n, (a, b) in enumerate(((v_, v), (wx_, wx), (wy_, wy), (wz_, wz)))
    ]
    for c in copies:
        c.start()
    for c in copies[1:]:
        c.wait()
    last_x = lax.axis_index("gx") == lax.axis_size("gx") - 1
    last_y = lax.axis_index("gy") == lax.axis_size("gy") - 1
    keep_x = jnp.where(last_x, 0.0, 1.0)
    keep_y = jnp.where(last_y, 0.0, 1.0)
    wm[0] = wx[...]
    wm[0, LX - 1] = wx[LX - 1] * keep_x
    sub = lax.broadcasted_iota(jnp.int32, (LX, LY, NZ), 1)
    wm[1] = jnp.where(sub == LY - 1, wy[...] * keep_y, wy[...])
    lane = lax.broadcasted_iota(jnp.int32, (LX, LY, NZ), 2)
    wm[2] = jnp.where(lane == NZ - 1, 0.0, wz[...])

    for x in range(CX):
        i = 2 * x
        wyp = wm[1, i] + wm[1, i + 1]
        wzp = wm[2, i] + wm[2, i + 1]
        parts = (
            (wm[0, i + 1], SUM),
            (wm[0, i], SUM),
            (wyp, SUM),
            (wzp, ODD),
            (wzp, EVEN),
        )
        for q, (a, how) in enumerate(parts):
            Q[q, x * LY : x * LY + 8] = compress(a[0:8], how)
            Q[q, x * LY + 8 : x * LY + 16] = compress(a[8:16], how)
    ri = lax.broadcasted_iota(jnp.int32, (CX * CY, CX * LY), 0)
    ci = lax.broadcasted_iota(jnp.int32, (CX * CY, CX * LY), 1)
    both = jnp.where((ci >> 1) == ri, 1.0, 0.0)
    first = jnp.where(ci == 2 * ri, 1.0, 0.0)
    second = jnp.where(ci == 2 * ri + 1, 1.0, 0.0)

    def rows(m, q):
        return jnp.dot(m, Q[q], precision=lax.Precision.HIGHEST, preferred_element_type=jnp.float32)

    inside = 2.0 * (rows(both, 1) + rows(first, 2) + rows(both, 4))
    for a, w in enumerate((rows(both, 0), rows(second, 2), rows(both, 3), inside)):
        for x in range(CX):
            cw[a, x] = w[x * CY : (x + 1) * CY]

    for msg, planes_ in ((xu, UP_W), (xd, DN_W)):
        at = NV
        for w, x in planes_:
            msg[at] = wm[w, x, 0:8]
            msg[at + 1] = wm[w, x, 8:16]
            at += 2
        for x in range(CX):
            for a in range(4):
                z = 128 * (a & 1)
                msg[at + 2 * x + (a >> 1), :, z : z + 128] = cw[a, x]
    for x in range(LX):
        put_rows(
            yu,
            yd,
            H * LX + x,
            [wm[w, x, 0:8] for w in range(3)],
            [wm[w, x, 8:16] for w in range(3)],
        )
    for x in range(CX):
        put_coarse_rows(yu, yd, H * LX + LX + x, [cw[a, x] for a in range(4)])

    copies[0].wait()
    for x in range(LX):
        for t in range(0, LY, 8):
            vt[x, t : t + 8] = jnp.swapaxes(v[:, x, t : t + 8, :], 0, 1)
    for d in range(H):
        xu[d * LY : (d + 1) * LY] = vt[LX - H + d]
        xd[d * LY : (d + 1) * LY] = vt[d]
    for x in range(LX):
        for d in range(1, H + 1):
            yu[x * H + d - 1] = vt[x, LY - d]
            yd[x * H + d - 1] = vt[x, d - 1]


def x_cell(xl, xr, p, y):
    return xl[(p + H) * LY + y] if p < 0 else xr[(p - LX) * LY + y]


def x_weight(xl, xr, w, p):
    if p < 0:
        at = NV + 2 * UP_W.index((w, p + LX))
        return xl[at], xl[at + 1]
    at = NV + 2 * DN_W.index((w, p - LX))
    return xr[at], xr[at + 1]


def x_coarse(xl, xr, a, p):
    z = 128 * (a & 1)
    if p < 0:
        return xl[NXU - 2 * CX + 2 * (p + CX) + (a >> 1), :, z : z + 128]
    return xr[NXD - 2 * CX + 2 * (p - CX) + (a >> 1), :, z : z + 128]


def corner_send(xl, xr, cu, cd):
    n = 0
    for side in (-1, 1):
        for dx, dy in CELLS:
            p = -dx if side < 0 else LX - 1 + dx
            cu[n] = x_cell(xl, xr, p, LY - dy)
            cd[n] = x_cell(xl, xr, p, dy - 1)
            n += 1
    for p in WP:
        tiles = [x_weight(xl, xr, w, p) for w in range(3)]
        put_rows(cu, cd, n, [t[0] for t in tiles], [t[1] for t in tiles])
        n += 1
    for p in CWP:
        put_coarse_rows(cu, cd, n, [x_coarse(xl, xr, a, p) for a in range(4)])
        n += 1


def planes(radius, body, own, halo):
    def step(n, _):
        body(n + halo, radius)
        return 0

    lax.fori_loop(0, own, step, 0)
    for d in range(1, radius + 1):
        body(halo - d, radius - d)
        body(halo + own - 1 + d, radius - d)


SUM, EVEN, ODD = 0, 1, 2


def compress(a, how=SUM):
    lane = lax.broadcasted_iota(jnp.int32, (8, 128), 1)
    t = a + up_z(a) if how == SUM else a
    at = (2 * lane + (1 if how == ODD else 0)) & 127
    lo = jnp.take_along_axis(t[:, :128], at, 1)
    hi = jnp.take_along_axis(t[:, 128:], at, 1)
    return jnp.where(lane < 64, lo, hi)


def expand(a):
    lane = lax.broadcasted_iota(jnp.int32, (8, 128), 1)
    half = lane >> 1
    return jnp.concatenate(
        [jnp.take_along_axis(a, half, 1), jnp.take_along_axis(a, half + 64, 1)], 1
    )


def stencil(w, at):
    c = at(0, 0)
    return (
        w(0) * at(1, 0)
        + w(1) * at(-1, 0)
        + w(2) * at(0, 1)
        + w(3) * at(0, -1)
        + w(4) * up_z(c)
        + w(5) * down_z(c)
    )


def fine_level(vt, wm, cw, xl, xr, yl, yr, V, W, NW, Y1, Y2, Y3, f, over):
    V[H : H + LX, H : H + LY] = vt[...]
    for d in range(H):
        V[d, H : H + LY] = xl[d * LY : (d + 1) * LY]
        V[H + LX + d, H : H + LY] = xr[d * LY : (d + 1) * LY]
    for x in range(LX):
        for d in range(1, H + 1):
            V[x + H, H - d] = yl[x * H + d - 1]
            V[x + H, H + LY - 1 + d] = yr[x * H + d - 1]
    for w in range(3):
        W[w, H : H + LX, JW : JW + LY] = wm[w]
        for p in list(range(-H if w == 0 else -2, 0)) + [LX, LX + 1]:
            lo, hi = x_weight(xl, xr, w, p)
            W[w, p + H, JW : JW + 8] = lo
            W[w, p + H, JW + 8 : JW + 16] = hi
    for x in range(LX):
        n, i = H * LX + x, x + H
        W[0, i, JW - 2 : JW] = yl[n, 0:2]
        W[1, i, JW - 3 : JW] = yl[n, 2:5]
        W[2, i, JW - 2 : JW] = yl[n, 6:8]
        W[0, i, JW + LY : JW + LY + 2] = yr[n, 0:2]
        W[1, i, JW + LY : JW + LY + 2] = yr[n, 2:4]
        W[2, i, JW + LY : JW + LY + 2] = yr[n, 4:6]

    def norm(i, _):
        wx, lx = W[0, i], W[0, i - 1]
        wy = W[1, i]
        ly = pltpu.roll(wy, 1, 0)
        wz = W[2, i]
        lz = down_z(wz)
        deg = wx + lx + wy + ly + wz + lz
        inv = 1.0 / deg
        for a, w in enumerate((wx, lx, wy, ly, wz, lz)):
            NW[a, i] = w * inv
        NW[6, i] = deg
        return 0

    lax.fori_loop(1, LX + 5, norm, 0)

    def apply(src, dst, *parts):
        for first, step, count, low, high in parts:

            def body(n, _):
                i = H + first + step * n
                for y in range(low, high + 1):
                    r, j = y + JW, y + H
                    dst[i, j] = stencil(
                        lambda a: row(NW, a, i, r), lambda dx, dy: src[i + dx, j + dy]
                    )
                return 0

            lax.fori_loop(0, count, body, 0)

    apply(V, Y1, (1, 1, 6, -2, 17), (0, 7, 2, 0, 15), (-2, 1, 2, 1, 14), (8, 1, 2, 1, 14))
    apply(Y1, Y2, (2, 1, 4, -1, 16), (1, 5, 2, 0, 15), (0, 7, 2, 1, 14), (-1, 9, 2, 2, 13))
    apply(Y2, Y3, (2, 1, 4, 0, 15), (1, 5, 2, 1, 14), (0, 7, 2, 2, 13))

    first_row = lax.broadcasted_iota(jnp.int32, (CY, CZ), 0) == 0
    for x in range(CX):
        cx, cy, cz = cw[0, x], cw[1, x], cw[2, x]
        lcx = cw[0, x - 1] if x else x_coarse(xl, xr, 0, -1)
        edge = coarse_rows(yl, H * LX + LX + x, 1)[3:4]
        lcy = jnp.where(first_row, jnp.broadcast_to(edge, (CY, CZ)), pltpu.roll(cy, 1, 0))
        over[x] = 1.0 / (
            DIAG * (cx + lcx + cy + lcy + cz + down_z(cz)) + SHIFT * cw[3, x]
        )

    def block(x, _):
        for y in range(CY):
            ra, rb = 0.0, 0.0
            for dx in range(2):
                for dy in range(2):
                    i = H + 2 * x + dx
                    j = H + 2 * y + dy
                    ga, gb = rest(V[i, j], Y1[i, j], Y2[i, j], Y3[i, j])
                    deg = row(NW, 6, i, j - H + JW)
                    ra = ra + deg * ga
                    rb = rb + deg * gb
            inv = row(over, x, y)
            f[x, y, 0] = compress(ra) * inv
            f[x, y, 1] = compress(rb) * inv
        return 0

    lax.fori_loop(0, CX, block, 0)


def rest(v, y1, y2, y3):
    gb = G0 * v + G1 * y1 + G2 * y2
    return gb - (G0 * y1 + G1 * y2 + G2 * y3), gb


def smooth(v, y1, y2, y3):
    b = B0 * v + B1 * y1 + B2 * y2
    return v - (b - (B0 * y1 + B1 * y2 + B2 * y3)), b


def fine_corners(V, W, NW, Y1, Y2, Y3, f_, over, cl, cr, f, fix):
    f[...] = f_[...]
    for side in range(2):
        for top in range(2):
            msg = cr if top else cl

            def px(dx):
                return LX - 1 + dx if side else -dx

            def py(dy):
                return LY - 1 + dy if top else -dy

            got = {}
            for n, (dx, dy) in enumerate(CELLS):
                got[px(dx), py(dy)] = msg[len(CELLS) * side + n]

            def raw(w, x, y):
                out_x = x < 0 or x >= LX
                out_y = y < 0 or y >= LY
                if out_x and out_y:
                    n = 2 * len(CELLS) + WP.index(x)
                    if top:
                        r = (0, 2, 4)[w] + y - LY
                    else:
                        r = (2, 5, 8)[w] + y
                    return msg[n, r : r + 1]
                return W[w, x + H, y + JW : y + JW + 1]

            weights = {}

            def weight(x, y):
                if (x, y) not in weights:
                    wx, lx = raw(0, x, y), raw(0, x - 1, y)
                    wy, ly = raw(1, x, y), raw(1, x, y - 1)
                    wz = raw(2, x, y)
                    ws = (wx, lx, wy, ly, wz, down_z(wz))
                    inv = 1.0 / (wx + lx + wy + ly + wz + ws[5])
                    weights[x, y] = [jnp.broadcast_to(w * inv, (8, NZ)) for w in ws]
                return weights[x, y]

            def look(known, ref):
                def at(x, y):
                    return known[x, y] if (x, y) in known else ref[x + H, y + H]

                return at

            def run(at, cells, fresh):
                out = {}
                for dx, dy in cells:
                    x, y = px(dx), py(dy)
                    if fresh(dx, dy):
                        ws = weight(x, y)
                    else:
                        ws = [row(NW, a, x + H, y + JW) for a in range(6)]
                    out[x, y] = stencil(
                        lambda a: ws[a], lambda ex, ey: at(x + ex, y + ey)
                    )
                return out

            def fresh(dx, dy):
                return (dx > 0 and dy >= 0) or (dy > 0 and dx >= 0)

            v = look(got, V)
            y1 = look(run(v, [(1, 0), (2, 0), (1, 1), (0, 1), (0, 2)], fresh), Y1)
            y2 = look(run(y1, [(0, 0), (1, 0), (1, -1), (0, 1), (-1, 1)], fresh), Y2)
            y3 = look(run(y2, [(0, 0), (-1, 0), (0, -1)], fresh), Y3)
            ra, rb = 0.0, 0.0
            for n, (dx, dy) in enumerate(((0, 0), (-1, 0), (0, -1), (-1, -1))):
                x, y = px(dx), py(dy)
                four = (v(x, y), y1(x, y), y2(x, y), y3(x, y))
                ga, gb = rest(*four)
                deg = row(NW, 6, x + H, y + JW)
                ra = ra + deg * ga
                rb = rb + deg * gb
                p, b = smooth(*four)
                fix[2 * side + top, n, 0:8] = p
                fix[2 * side + top, n, 8:16] = b
            x, y = (CX - 1) * side, (CY - 1) * top
            inv = row(over, x, y)
            f[x, y, 0] = compress(ra) * inv
            f[x, y, 1] = compress(rb) * inv


def meanwhile(vt, NW, Y1, Y2, Y3, fix, cw, xl, xr, yl, yr, cl, cr, pb, nd, CW, R):
    def step(x, sums):
        num, den = sums
        for y in range(LY):
            v, y1 = vt[x, y], Y1[x + H, y + H]
            p, b = smooth(v, y1, Y2[x + H, y + H], Y3[x + H, y + H])
            pb[x, y, 0:8] = p
            pb[x, y, 8:16] = b
            dv = row(NW, 6, x + H, y + JW) * v
            num = num + dv * (v - y1)
            den = den + dv * v
        return num, den

    zero = jnp.zeros((8, NZ), jnp.float32)
    num, den = lax.fori_loop(0, LX, step, (zero, zero))
    nd[0] = num
    nd[1] = den
    for side in range(2):
        for top in range(2):
            for n, (dx, dy) in enumerate(((0, 0), (-1, 0), (0, -1), (-1, -1))):
                x = LX - 1 + dx if side else -dx
                y = LY - 1 + dy if top else -dy
                pb[x, y] = fix[2 * side + top, n]

    for a in range(4):
        for i in range(CX + 2 * CH):
            p = i - CH
            mid = cw[a, p] if 0 <= p < CX else x_coarse(xl, xr, a, p)
            R[a, i, JC : JC + CY] = mid
            if 0 <= p < CX:
                lo = coarse_rows(yl, H * LX + LX + p, a)
                hi = coarse_rows(yr, H * LX + LX + p, a)
            elif p in CWP:
                n = 2 * len(CELLS) + len(WP) + CWP.index(p)
                lo, hi = coarse_rows(cl, n, a), coarse_rows(cr, n, a)
            else:
                continue
            R[a, i, JC - 4 : JC] = lo
            R[a, i, JC + CY : JC + CY + 4] = hi
    for i in range(1, CX + 2 * CH - 1):
        cx, lcx, cy, cz = R[0, i], R[0, i - 1], R[1, i], R[2, i]
        ws = (cx, lcx, cy, pltpu.roll(cy, 1, 0), cz, down_z(cz))
        total = ws[0] + ws[1] + ws[2] + ws[3] + ws[4] + ws[5]
        inv = OMEGA / (DIAG * total + SHIFT * R[3, i])
        for a in range(6):
            CW[a, i] = ws[a] * inv


JC = 8
CCELLS = [(dx, dy) for dx in (1, 2, 3) for dy in range(1, CH + 1 - dx)]


def coarse_corner_send(left, right, cu, cd):
    n = 0
    for side in range(2):
        for dx, dy in CCELLS:
            x = dx - 1 if side else CX - dx
            src = right if side else left
            for half in range(2):
                cu[n] = src[x, CY - dy, half]
                cd[n] = src[x, dy - 1, half]
                n += 1


def coarse_level(own, left, right, yl, yr, cl, cr, CW, pb, NW, nd, po, bo, sums, F, EA, EB, EX):
    def put(i, j, half, f):
        f = OMEGA * f
        F[i, j, half] = f
        EA[i, j, half] = f

    for x in range(CX):
        for half in range(2):
            for y in range(CY):
                put(x, y + CH, half, left[x, y, half])
                put(x + CH, y + CH, half, own[x, y, half])
                put(x + CH + CX, y + CH, half, right[x, y, half])
            for y in range(CH):
                put(x + CH, y, half, yl[x, y, half])
                put(x + CH, y + CH + CY, half, yr[x, y, half])
    n = 0
    for side in range(2):
        for dx, dy in CCELLS:
            i = CH + CX - 1 + dx if side else CH - dx
            for half in range(2):
                put(i, CH - dy, half, cl[n])
                put(i, CH + CY - 1 + dy, half, cr[n])
                n += 1

    def sweep(src, dst):
        def body(i, reach):
            for j in range(CH - reach, CH + CY + reach):
                r = j - CH + JC
                ws = [row(CW, a, i, r) for a in range(6)]
                for half in range(2):
                    c = src[i, j, half]
                    dst[i, j, half] = (
                        (1.0 - OMEGA) * c
                        + F[i, j, half]
                        + ws[0] * src[i + 1, j, half]
                        + ws[1] * src[i - 1, j, half]
                        + ws[2] * src[i, j + 1, half]
                        + ws[3] * src[i, j - 1, half]
                        + ws[4] * up_z(c)
                        + ws[5] * down_z(c)
                    )

        return body

    planes(3, sweep(EA, EB), CX, CH)
    planes(2, sweep(EB, EA), CX, CH)
    planes(1, sweep(EA, EB), CX, CH)

    def spread(i, reach):
        for j in range(CH - reach, CH + CY + reach):
            for half in range(2):
                EX[i, j, half] = expand(EB[i, j, half])

    planes(1, spread, CX, CH)

    def block(x, _):
        for y in range(CY):
            for half in range(2):
                e = EX[x + CH, y + CH, half]
                ez = (up_z(e), down_z(e))
                ke = KEEP * e
                ce = C * e
                for dx in range(2):
                    ex = C * EX[x + CH + 2 * dx - 1, y + CH, half]
                    for dy in range(2):
                        ey = C * EX[x + CH, y + CH + 2 * dy - 1, half]
                        xx, yy = 2 * x + dx, 2 * y + dy
                        nw = [row(NW, a, xx + H, yy + JW) for a in range(6)]
                        s = (
                            ke
                            + (nw[dx] + nw[2 + dy]) * ce
                            + nw[1 - dx] * ex
                            + nw[3 - dy] * ey
                            + C * (nw[4] * ez[0] + nw[5] * ez[1])
                        )
                        if half == 0:
                            po[xx, yy] = pb[xx, yy, 0:8] - s
                        else:
                            bo[xx, yy] = pb[xx, yy, 8:16] + s
        return 0

    lax.fori_loop(0, CX, block, 0)

    def gram(n, acc):
        x = n >> 2
        acc = list(acc)
        for q in range(4):
            yy = (n & 3) * 4 + q
            deg = row(NW, 6, x + H, yy + JW)
            for h in range(0, NZ, 128):
                z = slice(h, h + 128)
                p = po[x, yy, :, z]
                b = bo[x, yy, :, z]
                dp = deg[:, z] * p
                db = deg[:, z] * b
                for s in range(8):
                    rb = pltpu.roll(db, s, 0) if s else db
                    if s < 5:
                        rp = pltpu.roll(dp, s, 0) if s else dp
                        acc[s] = acc[s] + p * rp
                        acc[5 + s] = acc[5 + s] + b * rb
                    acc[10 + s] = acc[10 + s] + p * rb
        return tuple(acc)

    zero = jnp.zeros((8, 128), jnp.float32)
    acc = list(lax.fori_loop(0, 4 * LX, gram, (zero,) * 18))
    for q in range(2):
        acc.append(nd[q, :, :128] + nd[q, :, 128:])
    ones = jnp.ones((8, 128), jnp.float32)

    def over_lanes(m):
        return lax.dot_general(
            ones,
            m,
            (((1,), (1,)), ((), ())),
            precision=lax.Precision.HIGHEST,
            preferred_element_type=jnp.float32,
        )

    t0 = over_lanes(jnp.concatenate(acc[:16], 0))
    t1 = over_lanes(jnp.concatenate(acc[16:] + [zero] * 12, 0))
    both = jnp.concatenate([t0[0:1], t1[0:1]], 0)
    sums[...] = jnp.broadcast_to(both[None], sums.shape)


def finish(parts, po, bo, out, eig, SP):
    t = parts[...]
    n = t.shape[0]
    while n > 1:
        n //= 2
        t = t[:n] + t[n:]
    t = t[0]
    eye = lax.broadcasted_iota(jnp.int32, (128, 128), 0) == lax.broadcasted_iota(
        jnp.int32, (128, 128), 1
    )
    ones = jnp.ones((128, 128), jnp.float32)
    for q in range(2):
        m = jnp.where(eye, jnp.broadcast_to(t[q : q + 1], (128, 128)), 0.0)
        SP[128 * q : 128 * (q + 1)] = jnp.dot(
            m, ones, precision=lax.Precision.HIGHEST, preferred_element_type=jnp.float32
        )
    lams = t[1:2] / pltpu.roll(t[1:2], 120, 1)
    eig[...] = pltpu.roll(lams, 112, 1)[:, :K]

    def entry(block, k):
        return row(SP, 8 * block + k)

    def sym(base, a, b):
        s = (a - b) % 8
        return entry(base + s, a) if s < 5 else entry(base + 8 - s, b)

    def cross(a, b):
        return entry(10 + (a - b) % 8, a)

    lam = [entry(18, k) / entry(19, k) for k in range(K)]
    voxels = LX * LY * NZ * lax.axis_size("gx") * lax.axis_size("gy")
    g = {}
    for a in range(K):
        for b in range(a + 1):
            g[a, b] = (
                sym(0, a, b) + lam[b] * cross(a, b) + lam[a] * (cross(b, a) + lam[b] * sym(5, a, b))
            ) * (1.0 / voxels)
    low, inv = {}, []
    for j in range(K):
        d = g[j, j]
        r = lax.rsqrt(d)
        r = r * (1.5 - 0.5 * d * r * r)
        inv.append(r)
        for a in range(j + 1, K):
            low[a, j] = g[a, j] * r
        for a in range(j + 1, K):
            for b in range(j + 1, a + 1):
                g[a, b] = g[a, b] - low[a, j] * low[b, j]

    for k in range(K):
        SP[8 * k : 8 * k + 8] = lam[k]
        SP[64 + 8 * k : 72 + 8 * k] = inv[k]
    at = {}
    for n, (a, b) in enumerate(sorted(low)):
        at[a, b] = 128 + 8 * n
        SP[128 + 8 * n : 136 + 8 * n] = low[a, b]

    def body(x, _):
        for t in range(0, LY, 8):
            for h in range(0, NZ, 128):
                z = slice(h, h + 128)
                p = jnp.swapaxes(po[x, t : t + 8, :, z], 0, 1)
                b = jnp.swapaxes(bo[x, t : t + 8, :, z], 0, 1)
                done = []
                for k in range(K):
                    u = p[k] + SP[8 * k : 8 * k + 8] * b[k]
                    for j in range(k):
                        u = u - SP[at[k, j] : at[k, j] + 8] * done[j]
                    u = u * SP[64 + 8 * k : 72 + 8 * k]
                    done.append(u)
                    out[k, x, t : t + 8, z] = u
        return 0

    lax.fori_loop(0, LX, body, 0)


def both_ways(up, down, axis):
    n = lax.axis_size(axis)
    fwd = [(i, (i + 1) % n) for i in range(n)]
    back = [((i + 1) % n, i) for i in range(n)]
    return lax.ppermute(up, axis, fwd), lax.ppermute(down, axis, back)


def per_device(vectors, weight_x, weight_y, weight_z):
    vt, wm, cw, xu, xd, yu, yd = call(
        prepare,
        [
            (LX, LY, K, NZ),
            (3, LX, LY, NZ),
            (4, CX, CY, CZ),
            (NXU, 8, NZ),
            (NXD, 8, NZ),
            (NYB, 8, NZ),
            (NYB, 8, NZ),
        ],
        (vectors, weight_x, weight_y, weight_z),
        [
            (K, LX, LY, NZ),
            (LX, LY, NZ),
            (LX, LY, NZ),
            (LX, LY, NZ),
            (5, CX * LY, CZ),
            pltpu.SemaphoreType.DMA((4,)),
        ],
        where=HBM,
        limit=56,
    )
    xl, xr = both_ways(xu, xd, "gx")
    yl, yr = both_ways(yu, yd, "gy")
    cu, cd = call(corner_send, [(NCB, 8, NZ)] * 2, (xl, xr))
    cl, cr = both_ways(cu, cd, "gy")
    ext = (LX + 2 * H, LY + 2 * H, K, NZ)
    V, W, NW, Y1, Y2, Y3, f, over = call(
        fine_level,
        [
            ext,
            (3, LX + 2 * H, 32, NZ),
            (7, LX + 2 * H, 32, NZ),
            ext,
            ext,
            ext,
            (CX, CY, 2, 8, CZ),
            (CX, CY, CZ),
        ],
        (vt, wm, cw, xl, xr, yl, yr),
        us=6,
    )
    f, fix = call(
        fine_corners,
        [(CX, CY, 2, 8, CZ), (4, 4, 16, NZ)],
        (V, W, NW, Y1, Y2, Y3, f, over, cl, cr),
    )
    left, right = both_ways(f, f, "gx")
    fl, fr = both_ways(f[:, CY - CH :], f[:, :CH], "gy")
    pb, nd, CW = call(
        meanwhile,
        [(LX, LY, 16, NZ), (2, 8, NZ), (6, CX + 2 * CH, 24, CZ)],
        (vt, NW, Y1, Y2, Y3, fix, cw, xl, xr, yl, yr, cl, cr),
        [(4, CX + 2 * CH, 24, CZ)],
        us=2,
    )
    cu, cd = call(coarse_corner_send, [(4 * len(CCELLS), 8, CZ)] * 2, (left, right))
    cl, cr = both_ways(cu, cd, "gy")
    n = lax.axis_size("gx") * lax.axis_size("gy")
    cext = (CX + 2 * CH, CY + 2 * CH, 2, 8, CZ)
    po, bo, sums = call(
        coarse_level,
        [(LX, LY, K, NZ), (LX, LY, K, NZ), (n, 2, 128)],
        (f, left, right, fl, fr, cl, cr, CW, pb, NW, nd),
        [cext, cext, cext, (CX + 2 * CH, CY + 2 * CH, 2, 8, NZ)],
        limit=12,
    )
    parts = lax.all_to_all(sums, ("gx", "gy"), 0, 0)
    refined, eig = call(
        finish,
        [(K, LX, LY, NZ), (1, K)],
        (parts, po, bo),
        [(384, 128)],
    )
    return refined, eig.reshape(K)


def solution(mesh):
    return jax.shard_map(
        per_device,
        mesh=mesh,
        in_specs=(
            P(None, "gx", "gy", None),
            P("gx", "gy", None),
            P("gx", "gy", None),
            P("gx", "gy", None),
        ),
        out_specs=(P(None, "gx", "gy", None), P()),
        check_vma=False,
    )
```

```python
import jax
import jax.numpy as jnp
from jax import lax
from jax.experimental import pallas as pl
from jax.experimental.pallas import tpu as pltpu
from jax.sharding import PartitionSpec as P

OMEGA = 0.8
SHIFT = 0.1
DIAG = 1.0 + SHIFT
C = OMEGA / DIAG
Z0 = 2.0 * C - DIAG * C * C
Z1 = C * C
G0, G1, G2 = 1.0 - DIAG * Z0, Z0 - DIAG * Z1, Z1
KEEP = 1.0 - DIAG * C
B0, B1, B2 = KEEP * Z0 + C, KEEP * Z1 + C * Z0, C * Z1

K = 8
LX, LY, NZ = 8, 16, 256
CX, CY, CZ = LX // 2, LY // 2, NZ // 2
H = 3
CH = 4
JW = 8
MIB = 1024 * 1024
VMEM = pl.BlockSpec(memory_space=pltpu.VMEM)


ANY = pl.BlockSpec(memory_space=pl.ANY)


def call(body, outs, ins, scratch=(), limit=8, where=VMEM, us=1):
    return pl.pallas_call(
        body,
        out_shape=[jax.ShapeDtypeStruct(s, jnp.float32) for s in outs],
        in_specs=[where] * len(ins),
        out_specs=[where] * len(outs),
        scratch_shapes=[pltpu.VMEM(s, jnp.float32) if isinstance(s, tuple) else s for s in scratch],
        compiler_params=pltpu.CompilerParams(vmem_limit_bytes=limit * MIB),
        cost_estimate=pl.CostEstimate(
            flops=0, bytes_accessed=us * 3_000_000, transcendentals=0
        ),
    )(*ins)


def row(ref, *at):
    *lead, r = at
    r_ = ref[(*lead, pl.ds(r, 1), slice(None))]
    return jnp.broadcast_to(r_, (8, r_.shape[-1]))


def up_z(a):
    return pltpu.roll(a, a.shape[-1] - 1, a.ndim - 1)


def down_z(a):
    return pltpu.roll(a, 1, a.ndim - 1)


UP_W = [(0, 5), (0, 6), (0, 7), (1, 6), (1, 7), (2, 6), (2, 7)]
DN_W = [(0, 0), (0, 1), (1, 0), (1, 1), (2, 0), (2, 1)]
NV = H * LY
NXU = K * H + len(UP_W)
NXD = K * H + len(DN_W)
NXB = NV + 2 * len(UP_W)
NYB = H * LX + LX + CX
CELLS = [(1, 1), (1, 2), (2, 1)]
WP = [-2, -1, LX, LX + 1]
CWP = [-3, -2, -1, CX, CX + 1, CX + 2]
NCB = 2 * len(CELLS) + len(WP)


def put_rows(up, down, n, lows, highs):
    up[n, 0:2] = highs[0][6:8]
    up[n, 2:5] = highs[1][5:8]
    up[n, 5:8] = highs[2][5:8]
    down[n, 0:2] = lows[0][0:2]
    down[n, 2:4] = lows[1][0:2]
    down[n, 4:8] = lows[2][0:4]


def put_coarse_rows(up, down, n, arrays):
    for a, w in enumerate(arrays):
        r, z = 4 * (a & 1), 128 * (a >> 1)
        up[n, r : r + 4, z : z + 128] = w[4:8]
        down[n, r : r + 4, z : z + 128] = w[0:4]


def coarse_rows(msg, n, a):
    r, z = 4 * (a & 1), 128 * (a >> 1)
    return msg[n, r : r + 4, z : z + 128]


def x_send(v, wx, wy, wz, xu, xd, sem):
    pairs = []
    for k in range(K):
        pairs.append((v.at[k, LX - H : LX], xu.at[H * k : H * k + H]))
        pairs.append((v.at[k, 0:H], xd.at[H * k : H * k + H]))
    for msg, side in ((xu, UP_W), (xd, DN_W)):
        at = K * H
        for w, ref in enumerate((wx, wy, wz)):
            p = [x for q, x in side if q == w]
            pairs.append((ref.at[p[0] : p[-1] + 1], msg.at[at : at + len(p)]))
            at += len(p)
    copies = [pltpu.make_async_copy(a, b, sem.at[n]) for n, (a, b) in enumerate(pairs)]
    for c in copies:
        c.start()
    for c in copies:
        c.wait()


def local(v, wx, wy, wz, vt, wm, cw, yu, yd, Q):
    last_x = lax.axis_index("gx") == lax.axis_size("gx") - 1
    last_y = lax.axis_index("gy") == lax.axis_size("gy") - 1
    keep_x = jnp.where(last_x, 0.0, 1.0)
    keep_y = jnp.where(last_y, 0.0, 1.0)
    wm[0] = wx[...]
    wm[0, LX - 1] = wx[LX - 1] * keep_x
    sub = lax.broadcasted_iota(jnp.int32, (LX, LY, NZ), 1)
    wm[1] = jnp.where(sub == LY - 1, wy[...] * keep_y, wy[...])
    lane = lax.broadcasted_iota(jnp.int32, (LX, LY, NZ), 2)
    wm[2] = jnp.where(lane == NZ - 1, 0.0, wz[...])

    for x in range(CX):
        i = 2 * x
        wyp = wm[1, i] + wm[1, i + 1]
        wzp = wm[2, i] + wm[2, i + 1]
        parts = (
            (wm[0, i + 1], SUM),
            (wm[0, i], SUM),
            (wyp, SUM),
            (wzp, ODD),
            (wzp, EVEN),
        )
        for q, (a, how) in enumerate(parts):
            Q[q, x * LY : x * LY + 8] = compress(a[0:8], how)
            Q[q, x * LY + 8 : x * LY + 16] = compress(a[8:16], how)
    ri = lax.broadcasted_iota(jnp.int32, (CX * CY, CX * LY), 0)
    ci = lax.broadcasted_iota(jnp.int32, (CX * CY, CX * LY), 1)
    both = jnp.where((ci >> 1) == ri, 1.0, 0.0)
    first = jnp.where(ci == 2 * ri, 1.0, 0.0)
    second = jnp.where(ci == 2 * ri + 1, 1.0, 0.0)

    def rows(m, q):
        return jnp.dot(m, Q[q], precision=lax.Precision.HIGHEST, preferred_element_type=jnp.float32)

    inside = 2.0 * (rows(both, 1) + rows(first, 2) + rows(both, 4))
    for a, w in enumerate((rows(both, 0), rows(second, 2), rows(both, 3), inside)):
        for x in range(CX):
            cw[a, x] = w[x * CY : (x + 1) * CY]

    for x in range(LX):
        put_rows(
            yu,
            yd,
            H * LX + x,
            [wm[w, x, 0:8] for w in range(3)],
            [wm[w, x, 8:16] for w in range(3)],
        )
    for x in range(CX):
        put_coarse_rows(yu, yd, H * LX + LX + x, [cw[a, x] for a in range(4)])

    for x in range(LX):
        for t in range(0, LY, 8):
            vt[x, t : t + 8] = jnp.swapaxes(v[:, x, t : t + 8, :], 0, 1)
    for x in range(LX):
        for d in range(1, H + 1):
            yu[x * H + d - 1] = vt[x, LY - d]
            yd[x * H + d - 1] = vt[x, d - 1]


def x_cell(xl, xr, p, y):
    return xl[(p + H) * LY + y] if p < 0 else xr[(p - LX) * LY + y]


def x_weight(xl, xr, w, p):
    if p < 0:
        at = NV + 2 * UP_W.index((w, p + LX))
        return xl[at], xl[at + 1]
    at = NV + 2 * DN_W.index((w, p - LX))
    return xr[at], xr[at + 1]


def x_receive(rl, rr, after, xl, xr, cu, cd):
    first_x = lax.axis_index("gx") == 0
    last_y = lax.axis_index("gy") == lax.axis_size("gy") - 1
    keep_x = jnp.where(first_x, 0.0, 1.0)
    keep_y = jnp.where(last_y, 0.0, 1.0)
    sub = lax.broadcasted_iota(jnp.int32, (8, NZ), 0)
    lane = lax.broadcasted_iota(jnp.int32, (8, NZ), 1)
    for src, dst, side in ((rl, xl, UP_W), (rr, xr, DN_W)):
        for d in range(H):
            for t in range(0, LY, 8):
                block = jnp.stack([src[H * k + d, t : t + 8] for k in range(K)])
                dst[d * LY + t : d * LY + t + 8] = jnp.swapaxes(block, 0, 1)
        for n, (w, x) in enumerate(side):
            lo, hi = src[K * H + n, 0:8], src[K * H + n, 8:16]
            if w == 0 and x == LX - 1:
                lo, hi = lo * keep_x, hi * keep_x
            if w == 1:
                hi = jnp.where(sub == 7, hi * keep_y, hi)
            if w == 2:
                lo = jnp.where(lane == NZ - 1, 0.0, lo)
                hi = jnp.where(lane == NZ - 1, 0.0, hi)
            dst[NV + 2 * n] = lo
            dst[NV + 2 * n + 1] = hi
    n = 0
    for side in (-1, 1):
        for dx, dy in CELLS:
            p = -dx if side < 0 else LX - 1 + dx
            cu[n] = x_cell(xl, xr, p, LY - dy)
            cd[n] = x_cell(xl, xr, p, dy - 1)
            n += 1
    for p in WP:
        tiles = [x_weight(xl, xr, w, p) for w in range(3)]
        put_rows(cu, cd, n, [t[0] for t in tiles], [t[1] for t in tiles])
        n += 1


def planes(radius, body, own, halo):
    def step(n, _):
        body(n + halo, radius)
        return 0

    lax.fori_loop(0, own, step, 0)
    for d in range(1, radius + 1):
        body(halo - d, radius - d)
        body(halo + own - 1 + d, radius - d)


SUM, EVEN, ODD = 0, 1, 2


def compress(a, how=SUM):
    lane = lax.broadcasted_iota(jnp.int32, (8, 128), 1)
    t = a + up_z(a) if how == SUM else a
    at = (2 * lane + (1 if how == ODD else 0)) & 127
    lo = jnp.take_along_axis(t[:, :128], at, 1)
    hi = jnp.take_along_axis(t[:, 128:], at, 1)
    return jnp.where(lane < 64, lo, hi)


def expand(a):
    lane = lax.broadcasted_iota(jnp.int32, (8, 128), 1)
    half = lane >> 1
    return jnp.concatenate(
        [jnp.take_along_axis(a, half, 1), jnp.take_along_axis(a, half + 64, 1)], 1
    )


def stencil(w, at):
    c = at(0, 0)
    return (
        w(0) * at(1, 0)
        + w(1) * at(-1, 0)
        + w(2) * at(0, 1)
        + w(3) * at(0, -1)
        + w(4) * up_z(c)
        + w(5) * down_z(c)
    )


NH = [-2, -1, 0, 8, 9]
Y1E = [-2, -1, 0, 7, 8, 9]
Y2E = [-1, 0, 1, 6, 7, 8]
Y3E = [0, 1, 2, 5, 6, 7]


def pick(near, edge, planes_):
    first = next(p for p in range(LX) if p not in planes_)

    def cell(p, y):
        if p in planes_:
            return edge[planes_.index(p), y + H]
        return near[p - first, y + H]

    return cell


def v_cell(vt, xl, xr, yl, yr):
    def cell(p, y):
        if not isinstance(p, int) or 0 <= p < LX:
            if y < 0:
                return yl[p * H - y - 1]
            if y >= LY:
                return yr[p * H + y - LY]
            return vt[p, y]
        return x_cell(xl, xr, p, y)

    return cell


def w_row(NW, NE, a, p, y):
    if p in NH:
        return row(NE, a, NH.index(p), y)
    return row(NW, a, p - 1, y + JW)


def normalise(dst, i, wx, lx, wy, ly, wz):
    lz = down_z(wz)
    deg = wx + lx + wy + ly + wz + lz
    inv = 1.0 / deg
    for a, w in enumerate((wx, lx, wy, ly, wz, lz)):
        dst[a, i] = w * inv
    dst[6, i] = deg


def fine_inner(vt, wm, cw, yl, yr, W, NW, Y1, Y2, Y3):
    for w in range(3):
        W[w, :, JW : JW + LY] = wm[w]
    for x in range(LX):
        n = H * LX + x
        W[0, x, JW - 2 : JW] = yl[n, 0:2]
        W[1, x, JW - 3 : JW] = yl[n, 2:5]
        W[2, x, JW - 2 : JW] = yl[n, 6:8]
        W[0, x, JW + LY : JW + LY + 2] = yr[n, 0:2]
        W[1, x, JW + LY : JW + LY + 2] = yr[n, 2:4]
        W[2, x, JW + LY : JW + LY + 2] = yr[n, 4:6]

    def norm(x, _):
        wy = W[1, x]
        normalise(NW, x - 1, W[0, x], W[0, x - 1], wy, pltpu.roll(wy, 1, 0), W[2, x])
        return 0

    lax.fori_loop(1, LX, norm, 0)
    v = v_cell(vt, None, None, yl, yr)

    def power(at, dst, first, count, low, high):
        def body(n, _):
            p = first + n
            for y in range(low, high + 1):
                dst[n, y + H] = stencil(
                    lambda a: row(NW, a, p - 1, y + JW), lambda dx, dy: at(p + dx, y + dy)
                )
            return 0

        lax.fori_loop(0, count, body, 0)

    power(v, Y1, 1, 6, -2, 17)
    power(lambda p, y: Y1[p - 1, y + H], Y2, 2, 4, -1, 16)
    power(lambda p, y: Y2[p - 2, y + H], Y3, 3, 2, 0, 15)


def fine_outer(vt, wm, cw, xl, xr, yl, yr, W, NW, Y1, Y2, Y3, NE, Y1X, Y2X, Y3X, f, over):
    def own(w, p):
        if 0 <= p < LX:
            return wm[w, p]
        return jnp.concatenate(x_weight(xl, xr, w, p), 0)

    top = lax.broadcasted_iota(jnp.int32, (LY, NZ), 0) == 0
    for n, p in enumerate(NH):
        wy = own(1, p)
        ly = pltpu.roll(wy, 1, 0)
        if p == 0:
            ly = jnp.where(top, jnp.broadcast_to(W[1, 0, JW - 1 : JW], (LY, NZ)), ly)
        normalise(NE, n, own(0, p), own(0, p - 1), wy, ly, own(2, p))

    def power(at, dst, planes_, rows_):
        for n, p in enumerate(planes_):
            low, high = rows_[n if n < 3 else 5 - n]
            for y in range(low, high + 1):
                dst[n, y + H] = stencil(
                    lambda a: w_row(NW, NE, a, p, y), lambda dx, dy: at(p + dx, y + dy)
                )

    v = v_cell(vt, xl, xr, yl, yr)
    y1, y2, y3 = pick(Y1, Y1X, Y1E), pick(Y2, Y2X, Y2E), pick(Y3, Y3X, Y3E)
    power(v, Y1X, Y1E, ((1, 14), (1, 14), (0, 15)))
    power(y1, Y2X, Y2E, ((2, 13), (1, 14), (0, 15)))
    power(y2, Y3X, Y3E, ((2, 13), (1, 14), (0, 15)))

    first_row = lax.broadcasted_iota(jnp.int32, (CY, CZ), 0) == 0
    for x in range(CX):
        cx, cy, cz = cw[0, x], cw[1, x], cw[2, x]
        if x:
            lcx = cw[0, x - 1]
        else:
            both = pair_rows()
            flat = jnp.concatenate(
                [compress(t) for t in x_weight(xl, xr, 0, -1)], 0
            )
            lcx = jnp.dot(
                both, flat, precision=lax.Precision.HIGHEST, preferred_element_type=jnp.float32
            )
        edge = coarse_rows(yl, H * LX + LX + x, 1)[3:4]
        lcy = jnp.where(first_row, jnp.broadcast_to(edge, (CY, CZ)), pltpu.roll(cy, 1, 0))
        over[x] = 1.0 / (
            DIAG * (cx + lcx + cy + lcy + cz + down_z(cz)) + SHIFT * cw[3, x]
        )

    for x in range(CX):
        for y in range(CY):
            if x in (0, CX - 1) and y in (0, CY - 1):
                continue
            ra, rb = 0.0, 0.0
            for dx in range(2):
                for dy in range(2):
                    p, q = 2 * x + dx, 2 * y + dy
                    ga, gb = rest(v(p, q), y1(p, q), y2(p, q), y3(p, q))
                    deg = w_row(NW, NE, 6, p, q)
                    ra = ra + deg * ga
                    rb = rb + deg * gb
            inv = row(over, x, y)
            at = 2 * (x * CY + y)
            f[at] = compress(ra) * inv
            f[at + 1] = compress(rb) * inv
    for a in range(4):
        for x in range(CX):
            f[NF + 4 * a + x] = cw[a, x]


NF = 2 * CX * CY


def pair_rows():
    ri = lax.broadcasted_iota(jnp.int32, (CY, LY), 0)
    ci = lax.broadcasted_iota(jnp.int32, (CY, LY), 1)
    return jnp.where((ci >> 1) == ri, 1.0, 0.0)


def rest(v, y1, y2, y3):
    gb = G0 * v + G1 * y1 + G2 * y2
    return gb - (G0 * y1 + G1 * y2 + G2 * y3), gb


def smooth(v, y1, y2, y3):
    b = B0 * v + B1 * y1 + B2 * y2
    return v - (b - (B0 * y1 + B1 * y2 + B2 * y3)), b


def fine_corners(
    vt, xl, xr, yl, yr, W, NW, Y1, Y2, Y3, NE, Y1X, Y2X, Y3X, f_, over, cl, cr, f, fu, fd, fix
):
    f[...] = f_[...]
    old = (
        v_cell(vt, xl, xr, yl, yr),
        pick(Y1, Y1X, Y1E),
        pick(Y2, Y2X, Y2E),
        pick(Y3, Y3X, Y3E),
    )
    for side in range(2):
        for top in range(2):
            msg = cr if top else cl

            def px(dx):
                return LX - 1 + dx if side else -dx

            def py(dy):
                return LY - 1 + dy if top else -dy

            got = {}
            for n, (dx, dy) in enumerate(CELLS):
                got[px(dx), py(dy)] = msg[len(CELLS) * side + n]

            def raw(w, x, y):
                out_x = x < 0 or x >= LX
                out_y = y < 0 or y >= LY
                if out_x and out_y:
                    n = 2 * len(CELLS) + WP.index(x)
                    if top:
                        r = (0, 2, 4)[w] + y - LY
                    else:
                        r = (2, 5, 8)[w] + y
                    return msg[n, r : r + 1]
                if out_x:
                    tile = x_weight(xl, xr, w, x)[y >> 3]
                    return tile[y & 7 : (y & 7) + 1]
                return W[w, x, y + JW : y + JW + 1]

            weights = {}

            def weight(x, y):
                if (x, y) not in weights:
                    wx, lx = raw(0, x, y), raw(0, x - 1, y)
                    wy, ly = raw(1, x, y), raw(1, x, y - 1)
                    wz = raw(2, x, y)
                    ws = (wx, lx, wy, ly, wz, down_z(wz))
                    inv = 1.0 / (wx + lx + wy + ly + wz + ws[5])
                    weights[x, y] = [jnp.broadcast_to(w * inv, (8, NZ)) for w in ws]
                return weights[x, y]

            def look(known, cell):
                def at(x, y):
                    return known[x, y] if (x, y) in known else cell(x, y)

                return at

            def run(at, cells, fresh):
                out = {}
                for dx, dy in cells:
                    x, y = px(dx), py(dy)
                    if fresh(dx, dy):
                        ws = weight(x, y)
                    else:
                        ws = [w_row(NW, NE, a, x, y) for a in range(6)]
                    out[x, y] = stencil(
                        lambda a: ws[a], lambda ex, ey: at(x + ex, y + ey)
                    )
                return out

            def fresh(dx, dy):
                return (dx > 0 and dy >= 0) or (dy > 0 and dx >= 0)

            v = look(got, old[0])
            y1 = look(run(v, [(1, 0), (2, 0), (1, 1), (0, 1), (0, 2)], fresh), old[1])
            y2 = look(run(y1, [(0, 0), (1, 0), (1, -1), (0, 1), (-1, 1)], fresh), old[2])
            y3 = look(run(y2, [(0, 0), (-1, 0), (0, -1)], fresh), old[3])
            ra, rb = 0.0, 0.0
            for n, (dx, dy) in enumerate(((0, 0), (-1, 0), (0, -1), (-1, -1))):
                x, y = px(dx), py(dy)
                four = (v(x, y), y1(x, y), y2(x, y), y3(x, y))
                ga, gb = rest(*four)
                deg = w_row(NW, NE, 6, x, y)
                ra = ra + deg * ga
                rb = rb + deg * gb
                p, b = smooth(*four)
                fix[2 * side + top, n, 0:8] = p
                fix[2 * side + top, n, 8:16] = b
            x, y = (CX - 1) * side, (CY - 1) * top
            inv = row(over, x, y)
            at = 2 * (x * CY + y)
            f[at] = compress(ra) * inv
            f[at + 1] = compress(rb) * inv
    for x in range(CX):
        at = 2 * x * CY
        fd[8 * x : 8 * x + 8] = f[at : at + 8]
        fu[8 * x : 8 * x + 8] = f[at + 8 : at + 16]


def meanwhile(vt, NW, NE, Y1, Y2, Y3, Y1X, Y2X, Y3X, fix, pb, nd):
    y1, y2, y3 = pick(Y1, Y1X, Y1E), pick(Y2, Y2X, Y2E), pick(Y3, Y3X, Y3E)
    num = den = jnp.zeros((8, NZ), jnp.float32)
    corner = {}
    for side in range(2):
        for top in range(2):
            for n, (dx, dy) in enumerate(((0, 0), (-1, 0), (0, -1), (-1, -1))):
                x = LX - 1 + dx if side else -dx
                y = LY - 1 + dy if top else -dy
                corner[x, y] = 2 * side + top, n
    for x in range(LX):
        for y in range(LY):
            v, nv = vt[x, y], y1(x, y)
            if (x, y) in corner:
                pb[x, y] = fix[corner[x, y]]
            else:
                p, b = smooth(v, nv, y2(x, y), y3(x, y))
                pb[x, y, 0:8] = p
                pb[x, y, 8:16] = b
            dv = w_row(NW, NE, 6, x, y) * v
            num = num + dv * (v - nv)
            den = den + dv * v
    nd[0] = num
    nd[1] = den


JC = 8
CCELLS = [(dx, dy) for dx in (1, 2, 3) for dy in range(1, CH + 1 - dx)]


NCC = 4 * len(CCELLS) + 2 * len(CWP)


def coarse_corner_send(left, right, after, yl, yr, cu, cd):
    n = 0
    for side in range(2):
        for dx, dy in CCELLS:
            x = dx - 1 if side else CX - dx
            src = right if side else left
            for half in range(2):
                cu[n] = src[2 * (x * CY + CY - dy) + half]
                cd[n] = src[2 * (x * CY + dy - 1) + half]
                n += 1
    for p in CWP:
        src, x = (left, p + CX) if p < 0 else (right, p - CX)
        for a in range(4):
            w = src[NF + 4 * a + x]
            m, r = n + (a >> 1), 4 * (a & 1)
            cu[m, r : r + 4] = w[4:8]
            cd[m, r : r + 4] = w[0:4]
        n += 2


def coarse_level(
    own, left, right, yl, yr, cl, cr, gl, gr, pb, NW, NE, nd, po, bo, mine, other, F, EA, EB, EX, CW, R
):
    def put(i, j, half, f):
        f = OMEGA * f
        F[i, j, half] = f
        EA[i, j, half] = f

    for x in range(CX):
        for half in range(2):
            for y in range(CY):
                at = 2 * (x * CY + y) + half
                put(x, y + CH, half, left[at])
                put(x + CH, y + CH, half, own[at])
                put(x + CH + CX, y + CH, half, right[at])
            for y in range(CH):
                put(x + CH, y, half, yl[2 * (x * CH + y) + half])
                put(x + CH, y + CH + CY, half, yr[2 * (x * CH + y) + half])
    n = 0
    for side in range(2):
        for dx, dy in CCELLS:
            i = CH + CX - 1 + dx if side else CH - dx
            for half in range(2):
                put(i, CH - dy, half, cl[n])
                put(i, CH + CY - 1 + dy, half, cr[n])
                n += 1

    for a in range(4):
        for i in range(CX + 2 * CH):
            p = i - CH
            src, x = (left, p + CX) if p < 0 else (own, p) if p < CX else (right, p - CX)
            R[a, i, JC : JC + CY] = src[NF + 4 * a + x]
            if 0 <= p < CX:
                lo = coarse_rows(gl, H * LX + LX + p, a)
                hi = coarse_rows(gr, H * LX + LX + p, a)
            elif p in CWP:
                m, r = n + 2 * CWP.index(p) + (a >> 1), 4 * (a & 1)
                lo, hi = cl[m, r : r + 4], cr[m, r : r + 4]
            else:
                continue
            R[a, i, JC - 4 : JC] = lo
            R[a, i, JC + CY : JC + CY + 4] = hi
    for i in range(1, CX + 2 * CH - 1):
        cx, lcx, cy, cz = R[0, i], R[0, i - 1], R[1, i], R[2, i]
        ws = (cx, lcx, cy, pltpu.roll(cy, 1, 0), cz, down_z(cz))
        total = ws[0] + ws[1] + ws[2] + ws[3] + ws[4] + ws[5]
        inv = OMEGA / (DIAG * total + SHIFT * R[3, i])
        for a in range(6):
            CW[a, i] = ws[a] * inv

    def sweep(src, dst):
        def body(i, reach):
            for j in range(CH - reach, CH + CY + reach):
                r = j - CH + JC
                ws = [row(CW, a, i, r) for a in range(6)]
                for half in range(2):
                    c = src[i, j, half]
                    dst[i, j, half] = (
                        (1.0 - OMEGA) * c
                        + F[i, j, half]
                        + ws[0] * src[i + 1, j, half]
                        + ws[1] * src[i - 1, j, half]
                        + ws[2] * src[i, j + 1, half]
                        + ws[3] * src[i, j - 1, half]
                        + ws[4] * up_z(c)
                        + ws[5] * down_z(c)
                    )

        return body

    planes(3, sweep(EA, EB), CX, CH)
    planes(2, sweep(EB, EA), CX, CH)
    planes(1, sweep(EA, EB), CX, CH)

    def spread(i, reach):
        for j in range(CH - reach, CH + CY + reach):
            for half in range(2):
                EX[i, j, half] = expand(EB[i, j, half])

    planes(1, spread, CX, CH)

    for x in range(CX):
        for y in range(CY):
            for half in range(2):
                e = EX[x + CH, y + CH, half]
                ez = (up_z(e), down_z(e))
                ke = KEEP * e
                ce = C * e
                for dx in range(2):
                    ex = C * EX[x + CH + 2 * dx - 1, y + CH, half]
                    for dy in range(2):
                        ey = C * EX[x + CH, y + CH + 2 * dy - 1, half]
                        xx, yy = 2 * x + dx, 2 * y + dy
                        nw = [w_row(NW, NE, a, xx, yy) for a in range(6)]
                        s = (
                            ke
                            + (nw[dx] + nw[2 + dy]) * ce
                            + nw[1 - dx] * ex
                            + nw[3 - dy] * ey
                            + C * (nw[4] * ez[0] + nw[5] * ez[1])
                        )
                        if half == 0:
                            po[xx, yy] = pb[xx, yy, 0:8] - s
                        else:
                            bo[xx, yy] = pb[xx, yy, 8:16] + s

    def gram(x, edge, acc):
        acc = list(acc)
        for yy in range(LY):
            deg = row(NE, 6, NH.index(0), yy) if edge else row(NW, 6, x - 1, yy + JW)
            for h in range(0, NZ, 128):
                z = slice(h, h + 128)
                p = po[x, yy, :, z]
                b = bo[x, yy, :, z]
                dp = deg[:, z] * p
                db = deg[:, z] * b
                for s in range(8):
                    rb = pltpu.roll(db, s, 0) if s else db
                    if s < 5:
                        rp = pltpu.roll(dp, s, 0) if s else dp
                        acc[s] = acc[s] + p * rp
                        acc[5 + s] = acc[5 + s] + b * rb
                    acc[10 + s] = acc[10 + s] + p * rb
        return tuple(acc)

    zero = jnp.zeros((8, 128), jnp.float32)
    acc = gram(0, True, (zero,) * 18)
    acc = list(lax.fori_loop(1, LX, lambda x, acc: gram(x, False, acc), acc))
    for q in range(2):
        acc.append(nd[q, :, :128] + nd[q, :, 128:])
    ones = jnp.ones((8, 128), jnp.float32)

    def over_lanes(m):
        return lax.dot_general(
            ones,
            m,
            (((1,), (1,)), ((), ())),
            precision=lax.Precision.HIGHEST,
            preferred_element_type=jnp.float32,
        )

    t0 = over_lanes(jnp.concatenate(acc[:16], 0))
    t1 = over_lanes(jnp.concatenate(acc[16:] + [zero] * 12, 0))
    even = lax.axis_index("gy") % 2 == 0
    mine[...] = jnp.where(even, t0[0:1], t1[0:1])
    other[...] = jnp.where(even, t1[0:1], t0[0:1])


def spread_sums(a, b, out):
    out[...] = jnp.broadcast_to((a[...] + b[...])[None], out.shape)


def finish(parts, po, bo, out, eig, SP):
    t = parts[...]
    n = t.shape[0]
    while n > 2:
        n //= 2
        t = t[:n] + t[n:]
    t = t[:, 0]
    eye = lax.broadcasted_iota(jnp.int32, (128, 128), 0) == lax.broadcasted_iota(
        jnp.int32, (128, 128), 1
    )
    ones = jnp.ones((128, 128), jnp.float32)
    for q in range(2):
        m = jnp.where(eye, jnp.broadcast_to(t[q : q + 1], (128, 128)), 0.0)
        SP[128 * q : 128 * (q + 1)] = jnp.dot(
            m, ones, precision=lax.Precision.HIGHEST, preferred_element_type=jnp.float32
        )
    lams = t[1:2] / pltpu.roll(t[1:2], 120, 1)
    eig[...] = pltpu.roll(lams, 112, 1)[:, :K]

    def entry(block, k):
        return row(SP, 8 * block + k)

    def sym(base, a, b):
        s = (a - b) % 8
        return entry(base + s, a) if s < 5 else entry(base + 8 - s, b)

    def cross(a, b):
        return entry(10 + (a - b) % 8, a)

    lam = [entry(18, k) / entry(19, k) for k in range(K)]
    voxels = LX * LY * NZ * lax.axis_size("gx") * lax.axis_size("gy")
    g = {}
    for a in range(K):
        for b in range(a + 1):
            g[a, b] = (
                sym(0, a, b) + lam[b] * cross(a, b) + lam[a] * (cross(b, a) + lam[b] * sym(5, a, b))
            ) * (1.0 / voxels)
    low, inv = {}, []
    for j in range(K):
        d = g[j, j]
        r = lax.rsqrt(d)
        r = r * (1.5 - 0.5 * d * r * r)
        inv.append(r)
        for a in range(j + 1, K):
            low[a, j] = g[a, j] * r
        for a in range(j + 1, K):
            for b in range(j + 1, a + 1):
                g[a, b] = g[a, b] - low[a, j] * low[b, j]

    for k in range(K):
        SP[8 * k : 8 * k + 8] = lam[k]
        SP[64 + 8 * k : 72 + 8 * k] = inv[k]
    at = {}
    for n, (a, b) in enumerate(sorted(low)):
        at[a, b] = 128 + 8 * n
        SP[128 + 8 * n : 136 + 8 * n] = low[a, b]

    def body(x, _):
        for t in range(0, LY, 8):
            for h in range(0, NZ, 128):
                z = slice(h, h + 128)
                p = jnp.swapaxes(po[x, t : t + 8, :, z], 0, 1)
                b = jnp.swapaxes(bo[x, t : t + 8, :, z], 0, 1)
                done = []
                for k in range(K):
                    u = p[k] + SP[8 * k : 8 * k + 8] * b[k]
                    for j in range(k):
                        u = u - SP[at[k, j] : at[k, j] + 8] * done[j]
                    u = u * SP[64 + 8 * k : 72 + 8 * k]
                    done.append(u)
                    out[k, x, t : t + 8, z] = u
        return 0

    lax.fori_loop(0, LX, body, 0)


def both_ways(up, down, axis):
    n = lax.axis_size(axis)
    fwd = [(i, (i + 1) % n) for i in range(n)]
    back = [((i + 1) % n, i) for i in range(n)]
    return lax.ppermute(up, axis, fwd), lax.ppermute(down, axis, back)


def per_device(vectors, weight_x, weight_y, weight_z):
    args = (vectors, weight_x, weight_y, weight_z)
    xu, xd = call(
        x_send,
        [(NXU, LY, NZ), (NXD, LY, NZ)],
        args,
        [pltpu.SemaphoreType.DMA((2 * K + 6,))],
        limit=56,
        where=ANY,
    )
    rl, rr = both_ways(xu, xd, "gx")
    vt, wm, cw, yu, yd = call(
        local,
        [
            (LX, LY, K, NZ),
            (3, LX, LY, NZ),
            (4, CX, CY, CZ),
            (NYB, 8, NZ),
            (NYB, 8, NZ),
        ],
        args,
        [(5, CX * LY, CZ)],
    )
    yl, yr = both_ways(yu, yd, "gy")
    tall = LY + 2 * H
    W, NW, Y1, Y2, Y3 = call(
        fine_inner,
        [
            (3, LX, 32, NZ),
            (7, LX - 1, 32, NZ),
            (6, tall, K, NZ),
            (4, tall, K, NZ),
            (2, tall, K, NZ),
        ],
        (vt, wm, cw, yl, yr),
        us=3,
    )
    xl, xr, cu, cd = call(
        x_receive, [(NXB, 8, NZ), (NXB, 8, NZ), (NCB, 8, NZ), (NCB, 8, NZ)], (rl, rr, Y3)
    )
    cl, cr = both_ways(cu, cd, "gy")
    NE, Y1X, Y2X, Y3X, f, over = call(
        fine_outer,
        [
            (7, len(NH), LY, NZ),
            (6, tall, K, NZ),
            (6, tall, K, NZ),
            (6, tall, K, NZ),
            (NF + 4 * CX, 8, CZ),
            (CX, CY, CZ),
        ],
        (vt, wm, cw, xl, xr, yl, yr, W, NW, Y1, Y2, Y3),
        us=4,
    )
    f, fu, fd, fix = call(
        fine_corners,
        [(NF + 4 * CX, 8, CZ), (NF // 2, 8, CZ), (NF // 2, 8, CZ), (4, 4, 16, NZ)],
        (vt, xl, xr, yl, yr, W, NW, Y1, Y2, Y3, NE, Y1X, Y2X, Y3X, f, over, cl, cr),
    )
    left, right = both_ways(f, f, "gx")
    fl, fr = both_ways(fu, fd, "gy")
    pb, nd = call(
        meanwhile,
        [(LX, LY, 16, NZ), (2, 8, NZ)],
        (vt, NW, NE, Y1, Y2, Y3, Y1X, Y2X, Y3X, fix),
    )
    cu, cd = call(coarse_corner_send, [(NCC, 8, CZ)] * 2, (left, right, nd, fl, fr))
    cl, cr = both_ways(cu, cd, "gy")
    cext = (CX + 2 * CH, CY + 2 * CH, 2, 8, CZ)
    po, bo, mine, other = call(
        coarse_level,
        [(LX, LY, K, NZ), (LX, LY, K, NZ), (1, 128), (1, 128)],
        (f, left, right, fl, fr, cl, cr, yl, yr, pb, NW, NE, nd),
        [
            cext,
            cext,
            cext,
            (CX + 2 * CH, CY + 2 * CH, 2, 8, NZ),
            (6, CX + 2 * CH, 24, CZ),
            (4, CX + 2 * CH, 24, CZ),
        ],
        limit=12,
    )
    n = lax.axis_size("gy")
    theirs = lax.ppermute(other, "gy", [(i, i ^ 1) for i in range(n)])
    (sums,) = call(spread_sums, [(n * lax.axis_size("gx"), 1, 128)], (mine, theirs))
    parts = lax.all_to_all(sums, ("gx", "gy"), 0, 0)
    refined, eig = call(
        finish,
        [(K, LX, LY, NZ), (1, K)],
        (parts, po, bo),
        [(384, 128)],
    )
    return refined, eig.reshape(K)


def solution(mesh):
    return jax.shard_map(
        per_device,
        mesh=mesh,
        in_specs=(
            P(None, "gx", "gy", None),
            P("gx", "gy", None),
            P("gx", "gy", None),
            P("gx", "gy", None),
        ),
        out_specs=(P(None, "gx", "gy", None), P()),
        check_vma=False,
    )
```

```python
import jax
import jax.numpy as jnp
from jax import lax
from jax.experimental import pallas as pl
from jax.experimental.pallas import tpu as pltpu
from jax.sharding import PartitionSpec as P

OMEGA = 0.8
SHIFT = 0.1
DIAG = 1.0 + SHIFT
C = OMEGA / DIAG
Z0 = 2.0 * C - DIAG * C * C
Z1 = C * C
G0, G1, G2 = 1.0 - DIAG * Z0, Z0 - DIAG * Z1, Z1
KEEP = 1.0 - DIAG * C
B0, B1, B2 = KEEP * Z0 + C, KEEP * Z1 + C * Z0, C * Z1

K = 8
LX, LY, NZ = 8, 16, 256
CX, CY, CZ = LX // 2, LY // 2, NZ // 2
H = 3
CH = 4
JW = 8
MIB = 1024 * 1024
VMEM = pl.BlockSpec(memory_space=pltpu.VMEM)


ANY = pl.BlockSpec(memory_space=pl.ANY)


def call(body, outs, ins, scratch=(), limit=8, where=VMEM, us=1, out_where=None):
    return pl.pallas_call(
        body,
        out_shape=[jax.ShapeDtypeStruct(s, jnp.float32) for s in outs],
        in_specs=[where] * len(ins),
        out_specs=out_where or [where] * len(outs),
        scratch_shapes=[pltpu.VMEM(s, jnp.float32) if isinstance(s, tuple) else s for s in scratch],
        compiler_params=pltpu.CompilerParams(vmem_limit_bytes=limit * MIB),
        cost_estimate=pl.CostEstimate(
            flops=0, bytes_accessed=us * 3_000_000, transcendentals=0
        ),
    )(*ins)


def row(ref, *at):
    *lead, r = at
    r_ = ref[(*lead, pl.ds(r, 1), slice(None))]
    return jnp.broadcast_to(r_, (8, r_.shape[-1]))


def up_z(a):
    return pltpu.roll(a, a.shape[-1] - 1, a.ndim - 1)


def down_z(a):
    return pltpu.roll(a, 1, a.ndim - 1)


UP_W = [(0, 5), (0, 6), (0, 7), (1, 6), (1, 7), (2, 6), (2, 7)]
DN_W = [(0, 0), (0, 1), (1, 0), (1, 1), (2, 0), (2, 1)]
NV = H * LY
NXU = K * H + len(UP_W)
NXD = K * H + len(DN_W)
NXB = NV + 2 * len(UP_W)
NYB = H * LX + LX + CX
CELLS = [(1, 1), (1, 2), (2, 1)]
WP = [-2, -1, LX, LX + 1]
CWP = [-3, -2, -1, CX, CX + 1, CX + 2]
NCB = 2 * len(CELLS) + len(WP)


def put_rows(up, down, n, lows, highs):
    up[n, 0:2] = highs[0][6:8]
    up[n, 2:5] = highs[1][5:8]
    up[n, 5:8] = highs[2][5:8]
    down[n, 0:2] = lows[0][0:2]
    down[n, 2:4] = lows[1][0:2]
    down[n, 4:8] = lows[2][0:4]


def put_coarse_rows(up, down, n, arrays):
    for a, w in enumerate(arrays):
        r, z = 4 * (a & 1), 128 * (a >> 1)
        up[n, r : r + 4, z : z + 128] = w[4:8]
        down[n, r : r + 4, z : z + 128] = w[0:4]


def coarse_rows(msg, n, a):
    r, z = 4 * (a & 1), 128 * (a >> 1)
    return msg[n, r : r + 4, z : z + 128]


def x_send(v, wx, wy, wz, xu, xd, bu, bd, sem):
    pairs = []
    for k in range(K):
        pairs.append((v.at[k, LX - H : LX], bu.at[H * k : H * k + H], xu.at[H * k : H * k + H]))
        pairs.append((v.at[k, 0:H], bd.at[H * k : H * k + H], xd.at[H * k : H * k + H]))
    for buf, msg, side in ((bu, xu, UP_W), (bd, xd, DN_W)):
        at = K * H
        for w, ref in enumerate((wx, wy, wz)):
            p = [x for q, x in side if q == w]
            here = slice(at, at + len(p))
            pairs.append((ref.at[p[0] : p[-1] + 1], buf.at[here], msg.at[here]))
            at += len(p)
    n = len(pairs)
    ins = [pltpu.make_async_copy(a, b, sem.at[i]) for i, (a, b, _) in enumerate(pairs)]
    outs = [pltpu.make_async_copy(b, c, sem.at[n + i]) for i, (_, b, c) in enumerate(pairs)]
    for c in ins:
        c.start()
    for i, o in zip(ins, outs):
        i.wait()
        o.start()
    for o in outs:
        o.wait()


def local(v, wx, wy, wz, vt, wm, cw, yu, yd, Q):
    last_x = lax.axis_index("gx") == lax.axis_size("gx") - 1
    last_y = lax.axis_index("gy") == lax.axis_size("gy") - 1
    keep_x = jnp.where(last_x, 0.0, 1.0)
    keep_y = jnp.where(last_y, 0.0, 1.0)
    wm[0] = wx[...]
    wm[0, LX - 1] = wx[LX - 1] * keep_x
    sub = lax.broadcasted_iota(jnp.int32, (LX, LY, NZ), 1)
    wm[1] = jnp.where(sub == LY - 1, wy[...] * keep_y, wy[...])
    lane = lax.broadcasted_iota(jnp.int32, (LX, LY, NZ), 2)
    wm[2] = jnp.where(lane == NZ - 1, 0.0, wz[...])

    for x in range(CX):
        i = 2 * x
        wyp = wm[1, i] + wm[1, i + 1]
        wzp = wm[2, i] + wm[2, i + 1]
        parts = (
            (wm[0, i + 1], SUM),
            (wm[0, i], SUM),
            (wyp, SUM),
            (wzp, ODD),
            (wzp, EVEN),
        )
        for q, (a, how) in enumerate(parts):
            Q[q, x * LY : x * LY + 8] = compress(a[0:8], how)
            Q[q, x * LY + 8 : x * LY + 16] = compress(a[8:16], how)
    ri = lax.broadcasted_iota(jnp.int32, (CX * CY, CX * LY), 0)
    ci = lax.broadcasted_iota(jnp.int32, (CX * CY, CX * LY), 1)
    both = jnp.where((ci >> 1) == ri, 1.0, 0.0)
    first = jnp.where(ci == 2 * ri, 1.0, 0.0)
    second = jnp.where(ci == 2 * ri + 1, 1.0, 0.0)

    def rows(m, q):
        return jnp.dot(m, Q[q], precision=lax.Precision.HIGHEST, preferred_element_type=jnp.float32)

    inside = 2.0 * (rows(both, 1) + rows(first, 2) + rows(both, 4))
    for a, w in enumerate((rows(both, 0), rows(second, 2), rows(both, 3), inside)):
        for x in range(CX):
            cw[a, x] = w[x * CY : (x + 1) * CY]

    for x in range(LX):
        put_rows(
            yu,
            yd,
            H * LX + x,
            [wm[w, x, 0:8] for w in range(3)],
            [wm[w, x, 8:16] for w in range(3)],
        )
    for x in range(CX):
        put_coarse_rows(yu, yd, H * LX + LX + x, [cw[a, x] for a in range(4)])

    for x in range(LX):
        for t in range(0, LY, 8):
            vt[x, t : t + 8] = jnp.swapaxes(v[:, x, t : t + 8, :], 0, 1)
    for x in range(LX):
        for d in range(1, H + 1):
            yu[x * H + d - 1] = vt[x, LY - d]
            yd[x * H + d - 1] = vt[x, d - 1]


def x_cell(xl, xr, p, y):
    return xl[(p + H) * LY + y] if p < 0 else xr[(p - LX) * LY + y]


def x_weight(xl, xr, w, p):
    if p < 0:
        at = NV + 2 * UP_W.index((w, p + LX))
        return xl[at], xl[at + 1]
    at = NV + 2 * DN_W.index((w, p - LX))
    return xr[at], xr[at + 1]


def x_receive(rl, rr, after, xl, xr, cu, cd):
    first_x = lax.axis_index("gx") == 0
    last_y = lax.axis_index("gy") == lax.axis_size("gy") - 1
    keep_x = jnp.where(first_x, 0.0, 1.0)
    keep_y = jnp.where(last_y, 0.0, 1.0)
    sub = lax.broadcasted_iota(jnp.int32, (8, NZ), 0)
    lane = lax.broadcasted_iota(jnp.int32, (8, NZ), 1)
    for src, dst, side in ((rl, xl, UP_W), (rr, xr, DN_W)):
        for d in range(H):
            for t in range(0, LY, 8):
                block = jnp.stack([src[H * k + d, t : t + 8] for k in range(K)])
                dst[d * LY + t : d * LY + t + 8] = jnp.swapaxes(block, 0, 1)
        for n, (w, x) in enumerate(side):
            lo, hi = src[K * H + n, 0:8], src[K * H + n, 8:16]
            if w == 0 and x == LX - 1:
                lo, hi = lo * keep_x, hi * keep_x
            if w == 1:
                hi = jnp.where(sub == 7, hi * keep_y, hi)
            if w == 2:
                lo = jnp.where(lane == NZ - 1, 0.0, lo)
                hi = jnp.where(lane == NZ - 1, 0.0, hi)
            dst[NV + 2 * n] = lo
            dst[NV + 2 * n + 1] = hi
    n = 0
    for side in (-1, 1):
        for dx, dy in CELLS:
            p = -dx if side < 0 else LX - 1 + dx
            cu[n] = x_cell(xl, xr, p, LY - dy)
            cd[n] = x_cell(xl, xr, p, dy - 1)
            n += 1
    for p in WP:
        tiles = [x_weight(xl, xr, w, p) for w in range(3)]
        put_rows(cu, cd, n, [t[0] for t in tiles], [t[1] for t in tiles])
        n += 1


def planes(radius, body, own, halo):
    def step(n, _):
        body(n + halo, radius)
        return 0

    lax.fori_loop(0, own, step, 0)
    for d in range(1, radius + 1):
        body(halo - d, radius - d)
        body(halo + own - 1 + d, radius - d)


SUM, EVEN, ODD = 0, 1, 2


def compress(a, how=SUM):
    lane = lax.broadcasted_iota(jnp.int32, (8, 128), 1)
    t = a + up_z(a) if how == SUM else a
    at = (2 * lane + (1 if how == ODD else 0)) & 127
    lo = jnp.take_along_axis(t[:, :128], at, 1)
    hi = jnp.take_along_axis(t[:, 128:], at, 1)
    return jnp.where(lane < 64, lo, hi)


def expand(a):
    lane = lax.broadcasted_iota(jnp.int32, (8, 128), 1)
    half = lane >> 1
    return jnp.concatenate(
        [jnp.take_along_axis(a, half, 1), jnp.take_along_axis(a, half + 64, 1)], 1
    )


def stencil(w, at):
    c = at(0, 0)
    return (
        w(0) * at(1, 0)
        + w(1) * at(-1, 0)
        + w(2) * at(0, 1)
        + w(3) * at(0, -1)
        + w(4) * up_z(c)
        + w(5) * down_z(c)
    )


NH = [-2, -1, 0, 8, 9]
Y1E = [-2, -1, 0, 7, 8, 9]
Y2E = [-1, 0, 1, 6, 7, 8]
Y3E = [0, 1, 2, 5, 6, 7]


def pick(near, edge, planes_):
    first = next(p for p in range(LX) if p not in planes_)

    def cell(p, y):
        if p in planes_:
            return edge[planes_.index(p), y + H]
        return near[p - first, y + H]

    return cell


def v_cell(vt, xl, xr, yl, yr):
    def cell(p, y):
        if not isinstance(p, int) or 0 <= p < LX:
            if y < 0:
                return yl[p * H - y - 1]
            if y >= LY:
                return yr[p * H + y - LY]
            return vt[p, y]
        return x_cell(xl, xr, p, y)

    return cell


def w_row(NW, NE, a, p, y):
    if p in NH:
        return row(NE, a, NH.index(p), y)
    return row(NW, a, p - 1, y + JW)


def normalise(dst, i, wx, lx, wy, ly, wz):
    lz = down_z(wz)
    deg = wx + lx + wy + ly + wz + lz
    inv = 1.0 / deg
    for a, w in enumerate((wx, lx, wy, ly, wz, lz)):
        dst[a, i] = w * inv
    dst[6, i] = deg


def fine_inner(vt, wm, cw, yl, yr, W, NW, Y1, Y2, Y3):
    for w in range(3):
        W[w, :, JW : JW + LY] = wm[w]
    for x in range(LX):
        n = H * LX + x
        W[0, x, JW - 2 : JW] = yl[n, 0:2]
        W[1, x, JW - 3 : JW] = yl[n, 2:5]
        W[2, x, JW - 2 : JW] = yl[n, 6:8]
        W[0, x, JW + LY : JW + LY + 2] = yr[n, 0:2]
        W[1, x, JW + LY : JW + LY + 2] = yr[n, 2:4]
        W[2, x, JW + LY : JW + LY + 2] = yr[n, 4:6]

    def norm(x, _):
        wy = W[1, x]
        normalise(NW, x - 1, W[0, x], W[0, x - 1], wy, pltpu.roll(wy, 1, 0), W[2, x])
        return 0

    lax.fori_loop(1, LX, norm, 0)
    v = v_cell(vt, None, None, yl, yr)

    def power(at, dst, first, count, low, high):
        def body(n, _):
            p = first + n
            for y in range(low, high + 1):
                dst[n, y + H] = stencil(
                    lambda a: row(NW, a, p - 1, y + JW), lambda dx, dy: at(p + dx, y + dy)
                )
            return 0

        lax.fori_loop(0, count, body, 0)

    power(v, Y1, 1, 6, -2, 17)
    power(lambda p, y: Y1[p - 1, y + H], Y2, 2, 4, -1, 16)
    power(lambda p, y: Y2[p - 2, y + H], Y3, 3, 2, 0, 15)


def fine_outer(vt, wm, cw, xl, xr, yl, yr, W, NW, Y1, Y2, Y3, NE, Y1X, Y2X, Y3X, f, over):
    def own(w, p):
        if 0 <= p < LX:
            return wm[w, p]
        return jnp.concatenate(x_weight(xl, xr, w, p), 0)

    top = lax.broadcasted_iota(jnp.int32, (LY, NZ), 0) == 0
    for n, p in enumerate(NH):
        wy = own(1, p)
        ly = pltpu.roll(wy, 1, 0)
        if p == 0:
            ly = jnp.where(top, jnp.broadcast_to(W[1, 0, JW - 1 : JW], (LY, NZ)), ly)
        normalise(NE, n, own(0, p), own(0, p - 1), wy, ly, own(2, p))

    def power(at, dst, planes_, rows_):
        for n, p in enumerate(planes_):
            low, high = rows_[n if n < 3 else 5 - n]
            for y in range(low, high + 1):
                dst[n, y + H] = stencil(
                    lambda a: w_row(NW, NE, a, p, y), lambda dx, dy: at(p + dx, y + dy)
                )

    v = v_cell(vt, xl, xr, yl, yr)
    y1, y2, y3 = pick(Y1, Y1X, Y1E), pick(Y2, Y2X, Y2E), pick(Y3, Y3X, Y3E)
    power(v, Y1X, Y1E, ((1, 14), (1, 14), (0, 15)))
    power(y1, Y2X, Y2E, ((2, 13), (1, 14), (0, 15)))
    power(y2, Y3X, Y3E, ((2, 13), (1, 14), (0, 15)))

    first_row = lax.broadcasted_iota(jnp.int32, (CY, CZ), 0) == 0
    for x in range(CX):
        cx, cy, cz = cw[0, x], cw[1, x], cw[2, x]
        if x:
            lcx = cw[0, x - 1]
        else:
            both = pair_rows()
            flat = jnp.concatenate(
                [compress(t) for t in x_weight(xl, xr, 0, -1)], 0
            )
            lcx = jnp.dot(
                both, flat, precision=lax.Precision.HIGHEST, preferred_element_type=jnp.float32
            )
        edge = coarse_rows(yl, H * LX + LX + x, 1)[3:4]
        lcy = jnp.where(first_row, jnp.broadcast_to(edge, (CY, CZ)), pltpu.roll(cy, 1, 0))
        over[x] = 1.0 / (
            DIAG * (cx + lcx + cy + lcy + cz + down_z(cz)) + SHIFT * cw[3, x]
        )

    for x in range(CX):
        for y in range(CY):
            if x in (0, CX - 1) and y in (0, CY - 1):
                continue
            ra, rb = 0.0, 0.0
            for dx in range(2):
                for dy in range(2):
                    p, q = 2 * x + dx, 2 * y + dy
                    ga, gb = rest(v(p, q), y1(p, q), y2(p, q), y3(p, q))
                    deg = w_row(NW, NE, 6, p, q)
                    ra = ra + deg * ga
                    rb = rb + deg * gb
            inv = row(over, x, y)
            at = 2 * (x * CY + y)
            f[at] = compress(ra) * inv
            f[at + 1] = compress(rb) * inv
    for a in range(4):
        for x in range(CX):
            f[NF + 4 * a + x] = cw[a, x]


NF = 2 * CX * CY


def pair_rows():
    ri = lax.broadcasted_iota(jnp.int32, (CY, LY), 0)
    ci = lax.broadcasted_iota(jnp.int32, (CY, LY), 1)
    return jnp.where((ci >> 1) == ri, 1.0, 0.0)


def rest(v, y1, y2, y3):
    gb = G0 * v + G1 * y1 + G2 * y2
    return gb - (G0 * y1 + G1 * y2 + G2 * y3), gb


def smooth(v, y1, y2, y3):
    b = B0 * v + B1 * y1 + B2 * y2
    return v - (b - (B0 * y1 + B1 * y2 + B2 * y3)), b


def fine_corners(
    vt, xl, xr, yl, yr, W, NW, Y1, Y2, Y3, NE, Y1X, Y2X, Y3X, f_, over, cl, cr, f, fu, fd, fix
):
    f[...] = f_[...]
    old = (
        v_cell(vt, xl, xr, yl, yr),
        pick(Y1, Y1X, Y1E),
        pick(Y2, Y2X, Y2E),
        pick(Y3, Y3X, Y3E),
    )
    for side in range(2):
        for top in range(2):
            msg = cr if top else cl

            def px(dx):
                return LX - 1 + dx if side else -dx

            def py(dy):
                return LY - 1 + dy if top else -dy

            got = {}
            for n, (dx, dy) in enumerate(CELLS):
                got[px(dx), py(dy)] = msg[len(CELLS) * side + n]

            def raw(w, x, y):
                out_x = x < 0 or x >= LX
                out_y = y < 0 or y >= LY
                if out_x and out_y:
                    n = 2 * len(CELLS) + WP.index(x)
                    if top:
                        r = (0, 2, 4)[w] + y - LY
                    else:
                        r = (2, 5, 8)[w] + y
                    return msg[n, r : r + 1]
                if out_x:
                    tile = x_weight(xl, xr, w, x)[y >> 3]
                    return tile[y & 7 : (y & 7) + 1]
                return W[w, x, y + JW : y + JW + 1]

            weights = {}

            def weight(x, y):
                if (x, y) not in weights:
                    wx, lx = raw(0, x, y), raw(0, x - 1, y)
                    wy, ly = raw(1, x, y), raw(1, x, y - 1)
                    wz = raw(2, x, y)
                    ws = (wx, lx, wy, ly, wz, down_z(wz))
                    inv = 1.0 / (wx + lx + wy + ly + wz + ws[5])
                    weights[x, y] = [jnp.broadcast_to(w * inv, (8, NZ)) for w in ws]
                return weights[x, y]

            def look(known, cell):
                def at(x, y):
                    return known[x, y] if (x, y) in known else cell(x, y)

                return at

            def run(at, cells, fresh):
                out = {}
                for dx, dy in cells:
                    x, y = px(dx), py(dy)
                    if fresh(dx, dy):
                        ws = weight(x, y)
                    else:
                        ws = [w_row(NW, NE, a, x, y) for a in range(6)]
                    out[x, y] = stencil(
                        lambda a: ws[a], lambda ex, ey: at(x + ex, y + ey)
                    )
                return out

            def fresh(dx, dy):
                return (dx > 0 and dy >= 0) or (dy > 0 and dx >= 0)

            v = look(got, old[0])
            y1 = look(run(v, [(1, 0), (2, 0), (1, 1), (0, 1), (0, 2)], fresh), old[1])
            y2 = look(run(y1, [(0, 0), (1, 0), (1, -1), (0, 1), (-1, 1)], fresh), old[2])
            y3 = look(run(y2, [(0, 0), (-1, 0), (0, -1)], fresh), old[3])
            ra, rb = 0.0, 0.0
            for n, (dx, dy) in enumerate(((0, 0), (-1, 0), (0, -1), (-1, -1))):
                x, y = px(dx), py(dy)
                four = (v(x, y), y1(x, y), y2(x, y), y3(x, y))
                ga, gb = rest(*four)
                deg = w_row(NW, NE, 6, x, y)
                ra = ra + deg * ga
                rb = rb + deg * gb
                p, b = smooth(*four)
                fix[2 * side + top, n, 0:8] = p
                fix[2 * side + top, n, 8:16] = b
            x, y = (CX - 1) * side, (CY - 1) * top
            inv = row(over, x, y)
            at = 2 * (x * CY + y)
            f[at] = compress(ra) * inv
            f[at + 1] = compress(rb) * inv
    for x in range(CX):
        at = 2 * x * CY
        fd[8 * x : 8 * x + 8] = f[at : at + 8]
        fu[8 * x : 8 * x + 8] = f[at + 8 : at + 16]


def meanwhile(vt, NW, NE, Y1, Y2, Y3, Y1X, Y2X, Y3X, fix, pb, nd):
    y1, y2, y3 = pick(Y1, Y1X, Y1E), pick(Y2, Y2X, Y2E), pick(Y3, Y3X, Y3E)
    num = den = jnp.zeros((8, NZ), jnp.float32)
    corner = {}
    for side in range(2):
        for top in range(2):
            for n, (dx, dy) in enumerate(((0, 0), (-1, 0), (0, -1), (-1, -1))):
                x = LX - 1 + dx if side else -dx
                y = LY - 1 + dy if top else -dy
                corner[x, y] = 2 * side + top, n
    for x in range(LX):
        for y in range(LY):
            v, nv = vt[x, y], y1(x, y)
            if (x, y) in corner:
                pb[x, y] = fix[corner[x, y]]
            else:
                p, b = smooth(v, nv, y2(x, y), y3(x, y))
                pb[x, y, 0:8] = p
                pb[x, y, 8:16] = b
            dv = w_row(NW, NE, 6, x, y) * v
            num = num + dv * (v - nv)
            den = den + dv * v
    nd[0] = num
    nd[1] = den


JC = 8
CCELLS = [(dx, dy) for dx in (1, 2, 3) for dy in range(1, CH + 1 - dx)]


NCC = 4 * len(CCELLS) + 2 * len(CWP)


def coarse_corner_send(left, right, after, yl, yr, cu, cd):
    n = 0
    for side in range(2):
        for dx, dy in CCELLS:
            x = dx - 1 if side else CX - dx
            src = right if side else left
            for half in range(2):
                cu[n] = src[2 * (x * CY + CY - dy) + half]
                cd[n] = src[2 * (x * CY + dy - 1) + half]
                n += 1
    for p in CWP:
        src, x = (left, p + CX) if p < 0 else (right, p - CX)
        for a in range(4):
            w = src[NF + 4 * a + x]
            m, r = n + (a >> 1), 4 * (a & 1)
            cu[m, r : r + 4] = w[4:8]
            cd[m, r : r + 4] = w[0:4]
        n += 2


def coarse_level(
    own, left, right, yl, yr, cl, cr, gl, gr, pb, NW, NE, nd, po, bo, mine, other, F, EA, EB, EX, CW, R
):
    def put(i, j, half, f):
        f = OMEGA * f
        F[i, j, half] = f
        EA[i, j, half] = f

    for x in range(CX):
        for half in range(2):
            for y in range(CY):
                at = 2 * (x * CY + y) + half
                put(x, y + CH, half, left[at])
                put(x + CH, y + CH, half, own[at])
                put(x + CH + CX, y + CH, half, right[at])
            for y in range(CH):
                put(x + CH, y, half, yl[2 * (x * CH + y) + half])
                put(x + CH, y + CH + CY, half, yr[2 * (x * CH + y) + half])
    n = 0
    for side in range(2):
        for dx, dy in CCELLS:
            i = CH + CX - 1 + dx if side else CH - dx
            for half in range(2):
                put(i, CH - dy, half, cl[n])
                put(i, CH + CY - 1 + dy, half, cr[n])
                n += 1

    for a in range(4):
        for i in range(CX + 2 * CH):
            p = i - CH
            src, x = (left, p + CX) if p < 0 else (own, p) if p < CX else (right, p - CX)
            R[a, i, JC : JC + CY] = src[NF + 4 * a + x]
            if 0 <= p < CX:
                lo = coarse_rows(gl, H * LX + LX + p, a)
                hi = coarse_rows(gr, H * LX + LX + p, a)
            elif p in CWP:
                m, r = n + 2 * CWP.index(p) + (a >> 1), 4 * (a & 1)
                lo, hi = cl[m, r : r + 4], cr[m, r : r + 4]
            else:
                continue
            R[a, i, JC - 4 : JC] = lo
            R[a, i, JC + CY : JC + CY + 4] = hi
    for i in range(1, CX + 2 * CH - 1):
        cx, lcx, cy, cz = R[0, i], R[0, i - 1], R[1, i], R[2, i]
        ws = (cx, lcx, cy, pltpu.roll(cy, 1, 0), cz, down_z(cz))
        total = ws[0] + ws[1] + ws[2] + ws[3] + ws[4] + ws[5]
        inv = OMEGA / (DIAG * total + SHIFT * R[3, i])
        for a in range(6):
            CW[a, i] = ws[a] * inv

    def sweep(src, dst):
        def body(i, reach):
            for j in range(CH - reach, CH + CY + reach):
                r = j - CH + JC
                ws = [row(CW, a, i, r) for a in range(6)]
                for half in range(2):
                    c = src[i, j, half]
                    dst[i, j, half] = (
                        (1.0 - OMEGA) * c
                        + F[i, j, half]
                        + ws[0] * src[i + 1, j, half]
                        + ws[1] * src[i - 1, j, half]
                        + ws[2] * src[i, j + 1, half]
                        + ws[3] * src[i, j - 1, half]
                        + ws[4] * up_z(c)
                        + ws[5] * down_z(c)
                    )

        return body

    planes(3, sweep(EA, EB), CX, CH)
    planes(2, sweep(EB, EA), CX, CH)
    planes(1, sweep(EA, EB), CX, CH)

    def spread(i, reach):
        for j in range(CH - reach, CH + CY + reach):
            for half in range(2):
                EX[i, j, half] = expand(EB[i, j, half])

    planes(1, spread, CX, CH)

    for x in range(CX):
        for y in range(CY):
            for half in range(2):
                e = EX[x + CH, y + CH, half]
                ez = (up_z(e), down_z(e))
                ke = KEEP * e
                ce = C * e
                for dx in range(2):
                    ex = C * EX[x + CH + 2 * dx - 1, y + CH, half]
                    for dy in range(2):
                        ey = C * EX[x + CH, y + CH + 2 * dy - 1, half]
                        xx, yy = 2 * x + dx, 2 * y + dy
                        nw = [w_row(NW, NE, a, xx, yy) for a in range(6)]
                        s = (
                            ke
                            + (nw[dx] + nw[2 + dy]) * ce
                            + nw[1 - dx] * ex
                            + nw[3 - dy] * ey
                            + C * (nw[4] * ez[0] + nw[5] * ez[1])
                        )
                        if half == 0:
                            po[xx, yy] = pb[xx, yy, 0:8] - s
                        else:
                            bo[xx, yy] = pb[xx, yy, 8:16] + s

    def gram(x, edge, acc):
        acc = list(acc)
        for yy in range(LY):
            deg = row(NE, 6, NH.index(0), yy) if edge else row(NW, 6, x - 1, yy + JW)
            for h in range(0, NZ, 128):
                z = slice(h, h + 128)
                p = po[x, yy, :, z]
                b = bo[x, yy, :, z]
                dp = deg[:, z] * p
                db = deg[:, z] * b
                for s in range(8):
                    rb = pltpu.roll(db, s, 0) if s else db
                    if s < 5:
                        rp = pltpu.roll(dp, s, 0) if s else dp
                        acc[s] = acc[s] + p * rp
                        acc[5 + s] = acc[5 + s] + b * rb
                    acc[10 + s] = acc[10 + s] + p * rb
        return tuple(acc)

    zero = jnp.zeros((8, 128), jnp.float32)
    acc = gram(0, True, (zero,) * 18)
    acc = list(lax.fori_loop(1, LX, lambda x, acc: gram(x, False, acc), acc))
    for q in range(2):
        acc.append(nd[q, :, :128] + nd[q, :, 128:])
    ones = jnp.ones((8, 128), jnp.float32)

    def over_lanes(m):
        return lax.dot_general(
            ones,
            m,
            (((1,), (1,)), ((), ())),
            precision=lax.Precision.HIGHEST,
            preferred_element_type=jnp.float32,
        )

    t0 = over_lanes(jnp.concatenate(acc[:16], 0))
    t1 = over_lanes(jnp.concatenate(acc[16:] + [zero] * 12, 0))
    even = lax.axis_index("gy") % 2 == 0
    mine[...] = jnp.where(even, t0[0:1], t1[0:1])
    other[...] = jnp.where(even, t1[0:1], t0[0:1])


def spread_sums(a, b, out):
    out[...] = jnp.broadcast_to((a[...] + b[...])[None], out.shape)


def finish(parts, po, bo, out, eig, SP, buf, sem):
    t = parts[...]
    n = t.shape[0]
    while n > 2:
        n //= 2
        t = t[:n] + t[n:]
    t = t[:, 0]
    eye = lax.broadcasted_iota(jnp.int32, (128, 128), 0) == lax.broadcasted_iota(
        jnp.int32, (128, 128), 1
    )
    ones = jnp.ones((128, 128), jnp.float32)
    for q in range(2):
        m = jnp.where(eye, jnp.broadcast_to(t[q : q + 1], (128, 128)), 0.0)
        SP[128 * q : 128 * (q + 1)] = jnp.dot(
            m, ones, precision=lax.Precision.HIGHEST, preferred_element_type=jnp.float32
        )
    lams = t[1:2] / pltpu.roll(t[1:2], 120, 1)
    eig[...] = pltpu.roll(lams, 112, 1)[:, :K]

    def entry(block, k):
        return row(SP, 8 * block + k)

    def sym(base, a, b):
        s = (a - b) % 8
        return entry(base + s, a) if s < 5 else entry(base + 8 - s, b)

    def cross(a, b):
        return entry(10 + (a - b) % 8, a)

    lam = [entry(18, k) / entry(19, k) for k in range(K)]
    voxels = LX * LY * NZ * lax.axis_size("gx") * lax.axis_size("gy")
    g = {}
    for a in range(K):
        for b in range(a + 1):
            g[a, b] = (
                sym(0, a, b) + lam[b] * cross(a, b) + lam[a] * (cross(b, a) + lam[b] * sym(5, a, b))
            ) * (1.0 / voxels)
    low, inv = {}, []
    for j in range(K):
        d = g[j, j]
        r = lax.rsqrt(d)
        r = r * (1.5 - 0.5 * d * r * r)
        inv.append(r)
        for a in range(j + 1, K):
            low[a, j] = g[a, j] * r
        for a in range(j + 1, K):
            for b in range(j + 1, a + 1):
                g[a, b] = g[a, b] - low[a, j] * low[b, j]

    for k in range(K):
        SP[8 * k : 8 * k + 8] = lam[k]
        SP[64 + 8 * k : 72 + 8 * k] = inv[k]
    at = {}
    for n, (a, b) in enumerate(sorted(low)):
        at[a, b] = 128 + 8 * n
        SP[128 + 8 * n : 136 + 8 * n] = low[a, b]

    def body(x, _):
        for t in range(0, LY, 8):
            for h in range(0, NZ, 128):
                z = slice(h, h + 128)
                p = jnp.swapaxes(po[x, t : t + 8, :, z], 0, 1)
                b = jnp.swapaxes(bo[x, t : t + 8, :, z], 0, 1)
                done = []
                for k in range(K):
                    u = p[k] + SP[8 * k : 8 * k + 8] * b[k]
                    for j in range(k):
                        u = u - SP[at[k, j] : at[k, j] + 8] * done[j]
                    u = u * SP[64 + 8 * k : 72 + 8 * k]
                    done.append(u)
                    buf[k, x, t : t + 8, z] = u
        copy(x).start()
        return 0

    def copy(x):
        here = pl.ds(x, 1)
        return pltpu.make_async_copy(buf.at[:, here], out.at[:, here], sem.at[x])

    lax.fori_loop(0, LX, body, 0)
    for x in range(LX):
        copy(x).wait()


def both_ways(up, down, axis):
    n = lax.axis_size(axis)
    fwd = [(i, (i + 1) % n) for i in range(n)]
    back = [((i + 1) % n, i) for i in range(n)]
    return lax.ppermute(up, axis, fwd), lax.ppermute(down, axis, back)


def per_device(vectors, weight_x, weight_y, weight_z):
    args = (vectors, weight_x, weight_y, weight_z)
    xu, xd = call(
        x_send,
        [(NXU, LY, NZ), (NXD, LY, NZ)],
        args,
        [(NXU, LY, NZ), (NXD, LY, NZ), pltpu.SemaphoreType.DMA((4 * K + 12,))],
        limit=56,
        where=ANY,
    )
    rl, rr = both_ways(xu, xd, "gx")
    vt, wm, cw, yu, yd = call(
        local,
        [
            (LX, LY, K, NZ),
            (3, LX, LY, NZ),
            (4, CX, CY, CZ),
            (NYB, 8, NZ),
            (NYB, 8, NZ),
        ],
        args,
        [(5, CX * LY, CZ)],
    )
    yl, yr = both_ways(yu, yd, "gy")
    tall = LY + 2 * H
    W, NW, Y1, Y2, Y3 = call(
        fine_inner,
        [
            (3, LX, 32, NZ),
            (7, LX - 1, 32, NZ),
            (6, tall, K, NZ),
            (4, tall, K, NZ),
            (2, tall, K, NZ),
        ],
        (vt, wm, cw, yl, yr),
        us=3,
    )
    xl, xr, cu, cd = call(
        x_receive, [(NXB, 8, NZ), (NXB, 8, NZ), (NCB, 8, NZ), (NCB, 8, NZ)], (rl, rr, Y3)
    )
    cl, cr = both_ways(cu, cd, "gy")
    NE, Y1X, Y2X, Y3X, f, over = call(
        fine_outer,
        [
            (7, len(NH), LY, NZ),
            (6, tall, K, NZ),
            (6, tall, K, NZ),
            (6, tall, K, NZ),
            (NF + 4 * CX, 8, CZ),
            (CX, CY, CZ),
        ],
        (vt, wm, cw, xl, xr, yl, yr, W, NW, Y1, Y2, Y3),
        us=4,
    )
    f, fu, fd, fix = call(
        fine_corners,
        [(NF + 4 * CX, 8, CZ), (NF // 2, 8, CZ), (NF // 2, 8, CZ), (4, 4, 16, NZ)],
        (vt, xl, xr, yl, yr, W, NW, Y1, Y2, Y3, NE, Y1X, Y2X, Y3X, f, over, cl, cr),
    )
    left, right = both_ways(f, f, "gx")
    fl, fr = both_ways(fu, fd, "gy")
    pb, nd = call(
        meanwhile,
        [(LX, LY, 16, NZ), (2, 8, NZ)],
        (vt, NW, NE, Y1, Y2, Y3, Y1X, Y2X, Y3X, fix),
    )
    cu, cd = call(coarse_corner_send, [(NCC, 8, CZ)] * 2, (left, right, nd, fl, fr))
    cl, cr = both_ways(cu, cd, "gy")
    cext = (CX + 2 * CH, CY + 2 * CH, 2, 8, CZ)
    po, bo, mine, other = call(
        coarse_level,
        [(LX, LY, K, NZ), (LX, LY, K, NZ), (1, 128), (1, 128)],
        (f, left, right, fl, fr, cl, cr, yl, yr, pb, NW, NE, nd),
        [
            cext,
            cext,
            cext,
            (CX + 2 * CH, CY + 2 * CH, 2, 8, NZ),
            (6, CX + 2 * CH, 24, CZ),
            (4, CX + 2 * CH, 24, CZ),
        ],
        limit=12,
    )
    n = lax.axis_size("gy")
    theirs = lax.ppermute(other, "gy", [(i, i ^ 1) for i in range(n)])
    (sums,) = call(spread_sums, [(n * lax.axis_size("gx"), 1, 128)], (mine, theirs))
    parts = lax.all_to_all(sums, ("gx", "gy"), 0, 0)
    refined, eig = call(
        finish,
        [(K, LX, LY, NZ), (1, K)],
        (parts, po, bo),
        [(384, 128), (K, LX, LY, NZ), pltpu.SemaphoreType.DMA((LX,))],
        out_where=[ANY, VMEM],
    )
    return refined, eig.reshape(K)


def solution(mesh):
    return jax.shard_map(
        per_device,
        mesh=mesh,
        in_specs=(
            P(None, "gx", "gy", None),
            P("gx", "gy", None),
            P("gx", "gy", None),
            P("gx", "gy", None),
        ),
        out_specs=(P(None, "gx", "gy", None), P()),
        check_vma=False,
    )
```

```python
import jax
import jax.numpy as jnp
from jax import lax
from jax.experimental import pallas as pl
from jax.experimental.pallas import tpu as pltpu
from jax.sharding import PartitionSpec as P

OMEGA = 0.8
SHIFT = 0.1
DIAG = 1.0 + SHIFT
C = OMEGA / DIAG
Z0 = 2.0 * C - DIAG * C * C
Z1 = C * C
G0, G1, G2 = 1.0 - DIAG * Z0, Z0 - DIAG * Z1, Z1
KEEP = 1.0 - DIAG * C
B0, B1, B2 = KEEP * Z0 + C, KEEP * Z1 + C * Z0, C * Z1

K = 8
LX, LY, NZ = 8, 16, 256
CX, CY, CZ = LX // 2, LY // 2, NZ // 2
H = 3
CH = 4
JW = 8
MIB = 1024 * 1024
VMEM = pl.BlockSpec(memory_space=pltpu.VMEM)


ANY = pl.BlockSpec(memory_space=pl.ANY)


def call(body, outs, ins, scratch=(), limit=8, where=VMEM, us=1, out_where=None):
    return pl.pallas_call(
        body,
        out_shape=[jax.ShapeDtypeStruct(s, jnp.float32) for s in outs],
        in_specs=[where] * len(ins),
        out_specs=out_where or [where] * len(outs),
        scratch_shapes=[pltpu.VMEM(s, jnp.float32) if isinstance(s, tuple) else s for s in scratch],
        compiler_params=pltpu.CompilerParams(vmem_limit_bytes=limit * MIB),
        cost_estimate=pl.CostEstimate(
            flops=0, bytes_accessed=us * 3_000_000, transcendentals=0
        ),
    )(*ins)


def row(ref, *at):
    *lead, r = at
    r_ = ref[(*lead, pl.ds(r, 1), slice(None))]
    return jnp.broadcast_to(r_, (8, r_.shape[-1]))


def up_z(a):
    return pltpu.roll(a, a.shape[-1] - 1, a.ndim - 1)


def down_z(a):
    return pltpu.roll(a, 1, a.ndim - 1)


UP_W = [(0, 5), (0, 6), (0, 7), (1, 6), (1, 7), (2, 6), (2, 7)]
DN_W = [(0, 0), (0, 1), (1, 0), (1, 1), (2, 0), (2, 1)]
NV = H * LY
NXU = K * H + len(UP_W)
NXD = K * H + len(DN_W)
NXB = NV + 2 * len(UP_W)
NYB = H * LX + LX + CX
CELLS = [(1, 1), (1, 2), (2, 1)]
WP = [-2, -1, LX, LX + 1]
CWP = [-3, -2, -1, CX, CX + 1, CX + 2]
NCB = 2 * len(CELLS) + len(WP)


def put_rows(up, down, n, lows, highs):
    up[n, 0:2] = highs[0][6:8]
    up[n, 2:5] = highs[1][5:8]
    up[n, 5:8] = highs[2][5:8]
    down[n, 0:2] = lows[0][0:2]
    down[n, 2:4] = lows[1][0:2]
    down[n, 4:8] = lows[2][0:4]


def put_coarse_rows(up, down, n, arrays):
    for a, w in enumerate(arrays):
        r, z = 4 * (a & 1), 128 * (a >> 1)
        up[n, r : r + 4, z : z + 128] = w[4:8]
        down[n, r : r + 4, z : z + 128] = w[0:4]


def coarse_rows(msg, n, a):
    r, z = 4 * (a & 1), 128 * (a >> 1)
    return msg[n, r : r + 4, z : z + 128]


def x_send(v, wx, wy, wz, xu, xd, bu, bd, sem):
    pairs = []
    for k in range(K):
        pairs.append((v.at[k, LX - H : LX], bu.at[H * k : H * k + H], xu.at[H * k : H * k + H]))
        pairs.append((v.at[k, 0:H], bd.at[H * k : H * k + H], xd.at[H * k : H * k + H]))
    for buf, msg, side in ((bu, xu, UP_W), (bd, xd, DN_W)):
        at = K * H
        for w, ref in enumerate((wx, wy, wz)):
            p = [x for q, x in side if q == w]
            here = slice(at, at + len(p))
            pairs.append((ref.at[p[0] : p[-1] + 1], buf.at[here], msg.at[here]))
            at += len(p)
    n = len(pairs)
    ins = [pltpu.make_async_copy(a, b, sem.at[i]) for i, (a, b, _) in enumerate(pairs)]
    outs = [pltpu.make_async_copy(b, c, sem.at[n + i]) for i, (_, b, c) in enumerate(pairs)]
    for c in ins:
        c.start()
    for i, o in zip(ins, outs):
        i.wait()
        o.start()
    for o in outs:
        o.wait()


def local(v, wx, wy, wz, vt, wm, cw, yu, yd, Q):
    last_x = lax.axis_index("gx") == lax.axis_size("gx") - 1
    last_y = lax.axis_index("gy") == lax.axis_size("gy") - 1
    keep_x = jnp.where(last_x, 0.0, 1.0)
    keep_y = jnp.where(last_y, 0.0, 1.0)
    wm[0] = wx[...]
    wm[0, LX - 1] = wx[LX - 1] * keep_x
    sub = lax.broadcasted_iota(jnp.int32, (LX, LY, NZ), 1)
    wm[1] = jnp.where(sub == LY - 1, wy[...] * keep_y, wy[...])
    lane = lax.broadcasted_iota(jnp.int32, (LX, LY, NZ), 2)
    wm[2] = jnp.where(lane == NZ - 1, 0.0, wz[...])

    for x in range(CX):
        i = 2 * x
        wyp = wm[1, i] + wm[1, i + 1]
        wzp = wm[2, i] + wm[2, i + 1]
        parts = (
            (wm[0, i + 1], SUM),
            (wm[0, i], SUM),
            (wyp, SUM),
            (wzp, ODD),
            (wzp, EVEN),
        )
        for q, (a, how) in enumerate(parts):
            Q[q, x * LY : x * LY + 8] = compress(a[0:8], how)
            Q[q, x * LY + 8 : x * LY + 16] = compress(a[8:16], how)
    ri = lax.broadcasted_iota(jnp.int32, (CX * CY, CX * LY), 0)
    ci = lax.broadcasted_iota(jnp.int32, (CX * CY, CX * LY), 1)
    both = jnp.where((ci >> 1) == ri, 1.0, 0.0)
    first = jnp.where(ci == 2 * ri, 1.0, 0.0)
    second = jnp.where(ci == 2 * ri + 1, 1.0, 0.0)

    def rows(m, q):
        return jnp.dot(m, Q[q], precision=lax.Precision.HIGHEST, preferred_element_type=jnp.float32)

    inside = 2.0 * (rows(both, 1) + rows(first, 2) + rows(both, 4))
    for a, w in enumerate((rows(both, 0), rows(second, 2), rows(both, 3), inside)):
        for x in range(CX):
            cw[a, x] = w[x * CY : (x + 1) * CY]

    for x in range(LX):
        put_rows(
            yu,
            yd,
            H * LX + x,
            [wm[w, x, 0:8] for w in range(3)],
            [wm[w, x, 8:16] for w in range(3)],
        )
    for x in range(CX):
        put_coarse_rows(yu, yd, H * LX + LX + x, [cw[a, x] for a in range(4)])

    for x in range(LX):
        for t in range(0, LY, 8):
            vt[x, t : t + 8] = jnp.swapaxes(v[:, x, t : t + 8, :], 0, 1)
    for x in range(LX):
        for d in range(1, H + 1):
            yu[x * H + d - 1] = vt[x, LY - d]
            yd[x * H + d - 1] = vt[x, d - 1]


def x_cell(xl, xr, p, y):
    return xl[(p + H) * LY + y] if p < 0 else xr[(p - LX) * LY + y]


def x_weight(xl, xr, w, p):
    if p < 0:
        at = NV + 2 * UP_W.index((w, p + LX))
        return xl[at], xl[at + 1]
    at = NV + 2 * DN_W.index((w, p - LX))
    return xr[at], xr[at + 1]


def x_receive(rl, rr, after, xl, xr, cu, cd):
    first_x = lax.axis_index("gx") == 0
    last_y = lax.axis_index("gy") == lax.axis_size("gy") - 1
    keep_x = jnp.where(first_x, 0.0, 1.0)
    keep_y = jnp.where(last_y, 0.0, 1.0)
    sub = lax.broadcasted_iota(jnp.int32, (8, NZ), 0)
    lane = lax.broadcasted_iota(jnp.int32, (8, NZ), 1)
    for src, dst, side in ((rl, xl, UP_W), (rr, xr, DN_W)):
        for d in range(H):
            for t in range(0, LY, 8):
                block = jnp.stack([src[H * k + d, t : t + 8] for k in range(K)])
                dst[d * LY + t : d * LY + t + 8] = jnp.swapaxes(block, 0, 1)
        for n, (w, x) in enumerate(side):
            lo, hi = src[K * H + n, 0:8], src[K * H + n, 8:16]
            if w == 0 and x == LX - 1:
                lo, hi = lo * keep_x, hi * keep_x
            if w == 1:
                hi = jnp.where(sub == 7, hi * keep_y, hi)
            if w == 2:
                lo = jnp.where(lane == NZ - 1, 0.0, lo)
                hi = jnp.where(lane == NZ - 1, 0.0, hi)
            dst[NV + 2 * n] = lo
            dst[NV + 2 * n + 1] = hi
    n = 0
    for side in (-1, 1):
        for dx, dy in CELLS:
            p = -dx if side < 0 else LX - 1 + dx
            cu[n] = x_cell(xl, xr, p, LY - dy)
            cd[n] = x_cell(xl, xr, p, dy - 1)
            n += 1
    for p in WP:
        tiles = [x_weight(xl, xr, w, p) for w in range(3)]
        put_rows(cu, cd, n, [t[0] for t in tiles], [t[1] for t in tiles])
        n += 1


def planes(radius, body, own, halo):
    def step(n, _):
        body(n + halo, radius)
        return 0

    lax.fori_loop(0, own, step, 0)
    for d in range(1, radius + 1):
        body(halo - d, radius - d)
        body(halo + own - 1 + d, radius - d)


SUM, EVEN, ODD = 0, 1, 2


def compress(a, how=SUM):
    lane = lax.broadcasted_iota(jnp.int32, (8, 128), 1)
    t = a + up_z(a) if how == SUM else a
    at = (2 * lane + (1 if how == ODD else 0)) & 127
    lo = jnp.take_along_axis(t[:, :128], at, 1)
    hi = jnp.take_along_axis(t[:, 128:], at, 1)
    return jnp.where(lane < 64, lo, hi)


def expand(a):
    lane = lax.broadcasted_iota(jnp.int32, (8, 128), 1)
    half = lane >> 1
    return jnp.concatenate(
        [jnp.take_along_axis(a, half, 1), jnp.take_along_axis(a, half + 64, 1)], 1
    )


def stencil(w, at):
    c = at(0, 0)
    return (
        w(0) * at(1, 0)
        + w(1) * at(-1, 0)
        + w(2) * at(0, 1)
        + w(3) * at(0, -1)
        + w(4) * up_z(c)
        + w(5) * down_z(c)
    )


NH = [-2, -1, 0, 8, 9]
Y1E = [-2, -1, 0, 7, 8, 9]
Y2E = [-1, 0, 1, 6, 7, 8]
Y3E = [0, 1, 2, 5, 6, 7]


def pick(near, edge, planes_):
    first = next(p for p in range(LX) if p not in planes_)

    def cell(p, y):
        if p in planes_:
            return edge[planes_.index(p), y + H]
        return near[p - first, y + H]

    return cell


def v_cell(vt, xl, xr, yl, yr):
    def cell(p, y):
        if not isinstance(p, int) or 0 <= p < LX:
            if y < 0:
                return yl[p * H - y - 1]
            if y >= LY:
                return yr[p * H + y - LY]
            return vt[p, y]
        return x_cell(xl, xr, p, y)

    return cell


def w_row(NW, NE, a, p, y):
    if p in NH:
        return row(NE, a, NH.index(p), y)
    return row(NW, a, p - 1, y + JW)


def normalise(dst, i, wx, lx, wy, ly, wz):
    lz = down_z(wz)
    deg = wx + lx + wy + ly + wz + lz
    inv = 1.0 / deg
    for a, w in enumerate((wx, lx, wy, ly, wz, lz)):
        dst[a, i] = w * inv
    dst[6, i] = deg


def fine_inner(vt, wm, cw, yl, yr, W, NW, Y1, Y2, Y3):
    for w in range(3):
        W[w, :, JW : JW + LY] = wm[w]
    for x in range(LX):
        n = H * LX + x
        W[0, x, JW - 2 : JW] = yl[n, 0:2]
        W[1, x, JW - 3 : JW] = yl[n, 2:5]
        W[2, x, JW - 2 : JW] = yl[n, 6:8]
        W[0, x, JW + LY : JW + LY + 2] = yr[n, 0:2]
        W[1, x, JW + LY : JW + LY + 2] = yr[n, 2:4]
        W[2, x, JW + LY : JW + LY + 2] = yr[n, 4:6]

    def norm(x, _):
        wy = W[1, x]
        normalise(NW, x - 1, W[0, x], W[0, x - 1], wy, pltpu.roll(wy, 1, 0), W[2, x])
        return 0

    lax.fori_loop(1, LX, norm, 0)
    v = v_cell(vt, None, None, yl, yr)

    def power(at, dst, first, count, low, high):
        def body(n, _):
            p = first + n
            for y in range(low, high + 1):
                dst[n, y + H] = stencil(
                    lambda a: row(NW, a, p - 1, y + JW), lambda dx, dy: at(p + dx, y + dy)
                )
            return 0

        lax.fori_loop(0, count, body, 0)

    power(v, Y1, 1, 6, -2, 17)
    power(lambda p, y: Y1[p - 1, y + H], Y2, 2, 4, -1, 16)
    power(lambda p, y: Y2[p - 2, y + H], Y3, 3, 2, 0, 15)


def fine_outer(vt, wm, cw, xl, xr, yl, yr, W, NW, Y1, Y2, Y3, NE, Y1X, Y2X, Y3X, f, over):
    def own(w, p):
        if 0 <= p < LX:
            return wm[w, p]
        return jnp.concatenate(x_weight(xl, xr, w, p), 0)

    top = lax.broadcasted_iota(jnp.int32, (LY, NZ), 0) == 0
    for n, p in enumerate(NH):
        wy = own(1, p)
        ly = pltpu.roll(wy, 1, 0)
        if p == 0:
            ly = jnp.where(top, jnp.broadcast_to(W[1, 0, JW - 1 : JW], (LY, NZ)), ly)
        normalise(NE, n, own(0, p), own(0, p - 1), wy, ly, own(2, p))

    def power(at, dst, planes_, rows_):
        for n, p in enumerate(planes_):
            low, high = rows_[n if n < 3 else 5 - n]
            for y in range(low, high + 1):
                dst[n, y + H] = stencil(
                    lambda a: w_row(NW, NE, a, p, y), lambda dx, dy: at(p + dx, y + dy)
                )

    v = v_cell(vt, xl, xr, yl, yr)
    y1, y2, y3 = pick(Y1, Y1X, Y1E), pick(Y2, Y2X, Y2E), pick(Y3, Y3X, Y3E)
    power(v, Y1X, Y1E, ((1, 14), (1, 14), (0, 15)))
    power(y1, Y2X, Y2E, ((2, 13), (1, 14), (0, 15)))
    power(y2, Y3X, Y3E, ((2, 13), (1, 14), (0, 15)))

    first_row = lax.broadcasted_iota(jnp.int32, (CY, CZ), 0) == 0
    for x in range(CX):
        cx, cy, cz = cw[0, x], cw[1, x], cw[2, x]
        if x:
            lcx = cw[0, x - 1]
        else:
            both = pair_rows()
            flat = jnp.concatenate(
                [compress(t) for t in x_weight(xl, xr, 0, -1)], 0
            )
            lcx = jnp.dot(
                both, flat, precision=lax.Precision.HIGHEST, preferred_element_type=jnp.float32
            )
        edge = coarse_rows(yl, H * LX + LX + x, 1)[3:4]
        lcy = jnp.where(first_row, jnp.broadcast_to(edge, (CY, CZ)), pltpu.roll(cy, 1, 0))
        over[x] = 1.0 / (
            DIAG * (cx + lcx + cy + lcy + cz + down_z(cz)) + SHIFT * cw[3, x]
        )

    for x in range(CX):
        for y in range(CY):
            if x in (0, CX - 1) and y in (0, CY - 1):
                continue
            ra, rb = 0.0, 0.0
            for dx in range(2):
                for dy in range(2):
                    p, q = 2 * x + dx, 2 * y + dy
                    ga, gb = rest(v(p, q), y1(p, q), y2(p, q), y3(p, q))
                    deg = w_row(NW, NE, 6, p, q)
                    ra = ra + deg * ga
                    rb = rb + deg * gb
            inv = row(over, x, y)
            at = 2 * (x * CY + y)
            f[at] = compress(ra) * inv
            f[at + 1] = compress(rb) * inv
    for a in range(4):
        for x in range(CX):
            f[NF + 4 * a + x] = cw[a, x]


NF = 2 * CX * CY


def pair_rows():
    ri = lax.broadcasted_iota(jnp.int32, (CY, LY), 0)
    ci = lax.broadcasted_iota(jnp.int32, (CY, LY), 1)
    return jnp.where((ci >> 1) == ri, 1.0, 0.0)


def rest(v, y1, y2, y3):
    gb = G0 * v + G1 * y1 + G2 * y2
    return gb - (G0 * y1 + G1 * y2 + G2 * y3), gb


def smooth(v, y1, y2, y3):
    b = B0 * v + B1 * y1 + B2 * y2
    return v - (b - (B0 * y1 + B1 * y2 + B2 * y3)), b


def fine_corners(
    vt, xl, xr, yl, yr, W, NW, Y1, Y2, Y3, NE, Y1X, Y2X, Y3X, f_, over, cl, cr, f, fu, fd, fix
):
    f[...] = f_[...]
    old = (
        v_cell(vt, xl, xr, yl, yr),
        pick(Y1, Y1X, Y1E),
        pick(Y2, Y2X, Y2E),
        pick(Y3, Y3X, Y3E),
    )
    for side in range(2):
        for top in range(2):
            msg = cr if top else cl

            def px(dx):
                return LX - 1 + dx if side else -dx

            def py(dy):
                return LY - 1 + dy if top else -dy

            got = {}
            for n, (dx, dy) in enumerate(CELLS):
                got[px(dx), py(dy)] = msg[len(CELLS) * side + n]

            def raw(w, x, y):
                out_x = x < 0 or x >= LX
                out_y = y < 0 or y >= LY
                if out_x and out_y:
                    n = 2 * len(CELLS) + WP.index(x)
                    if top:
                        r = (0, 2, 4)[w] + y - LY
                    else:
                        r = (2, 5, 8)[w] + y
                    return msg[n, r : r + 1]
                if out_x:
                    tile = x_weight(xl, xr, w, x)[y >> 3]
                    return tile[y & 7 : (y & 7) + 1]
                return W[w, x, y + JW : y + JW + 1]

            weights = {}

            def weight(x, y):
                if (x, y) not in weights:
                    wx, lx = raw(0, x, y), raw(0, x - 1, y)
                    wy, ly = raw(1, x, y), raw(1, x, y - 1)
                    wz = raw(2, x, y)
                    ws = (wx, lx, wy, ly, wz, down_z(wz))
                    inv = 1.0 / (wx + lx + wy + ly + wz + ws[5])
                    weights[x, y] = [jnp.broadcast_to(w * inv, (8, NZ)) for w in ws]
                return weights[x, y]

            def look(known, cell):
                def at(x, y):
                    return known[x, y] if (x, y) in known else cell(x, y)

                return at

            def run(at, cells, fresh):
                out = {}
                for dx, dy in cells:
                    x, y = px(dx), py(dy)
                    if fresh(dx, dy):
                        ws = weight(x, y)
                    else:
                        ws = [w_row(NW, NE, a, x, y) for a in range(6)]
                    out[x, y] = stencil(
                        lambda a: ws[a], lambda ex, ey: at(x + ex, y + ey)
                    )
                return out

            def fresh(dx, dy):
                return (dx > 0 and dy >= 0) or (dy > 0 and dx >= 0)

            v = look(got, old[0])
            y1 = look(run(v, [(1, 0), (2, 0), (1, 1), (0, 1), (0, 2)], fresh), old[1])
            y2 = look(run(y1, [(0, 0), (1, 0), (1, -1), (0, 1), (-1, 1)], fresh), old[2])
            y3 = look(run(y2, [(0, 0), (-1, 0), (0, -1)], fresh), old[3])
            ra, rb = 0.0, 0.0
            for n, (dx, dy) in enumerate(((0, 0), (-1, 0), (0, -1), (-1, -1))):
                x, y = px(dx), py(dy)
                four = (v(x, y), y1(x, y), y2(x, y), y3(x, y))
                ga, gb = rest(*four)
                deg = w_row(NW, NE, 6, x, y)
                ra = ra + deg * ga
                rb = rb + deg * gb
                p, b = smooth(*four)
                fix[2 * side + top, n, 0:8] = p
                fix[2 * side + top, n, 8:16] = b
            x, y = (CX - 1) * side, (CY - 1) * top
            inv = row(over, x, y)
            at = 2 * (x * CY + y)
            f[at] = compress(ra) * inv
            f[at + 1] = compress(rb) * inv
    for x in range(CX):
        at = 2 * x * CY
        fd[8 * x : 8 * x + 8] = f[at : at + 8]
        fu[8 * x : 8 * x + 8] = f[at + 8 : at + 16]


def meanwhile(vt, NW, NE, Y1, Y2, Y3, Y1X, Y2X, Y3X, fix, pb, nd):
    y1, y2, y3 = pick(Y1, Y1X, Y1E), pick(Y2, Y2X, Y2E), pick(Y3, Y3X, Y3E)
    num = den = jnp.zeros((8, NZ), jnp.float32)
    corner = {}
    for side in range(2):
        for top in range(2):
            for n, (dx, dy) in enumerate(((0, 0), (-1, 0), (0, -1), (-1, -1))):
                x = LX - 1 + dx if side else -dx
                y = LY - 1 + dy if top else -dy
                corner[x, y] = 2 * side + top, n
    for x in range(LX):
        for y in range(LY):
            v, nv = vt[x, y], y1(x, y)
            if (x, y) in corner:
                pb[x, y] = fix[corner[x, y]]
            else:
                p, b = smooth(v, nv, y2(x, y), y3(x, y))
                pb[x, y, 0:8] = p
                pb[x, y, 8:16] = b
            dv = w_row(NW, NE, 6, x, y) * v
            num = num + dv * (v - nv)
            den = den + dv * v
    nd[0] = num
    nd[1] = den


JC = 8
CCELLS = [(dx, dy) for dx in (1, 2, 3) for dy in range(1, CH + 1 - dx)]


NCC = 4 * len(CCELLS) + 2 * len(CWP)


def coarse_corner_send(left, right, after, yl, yr, cu, cd):
    n = 0
    for side in range(2):
        for dx, dy in CCELLS:
            x = dx - 1 if side else CX - dx
            src = right if side else left
            for half in range(2):
                cu[n] = src[2 * (x * CY + CY - dy) + half]
                cd[n] = src[2 * (x * CY + dy - 1) + half]
                n += 1
    for p in CWP:
        src, x = (left, p + CX) if p < 0 else (right, p - CX)
        for a in range(4):
            w = src[NF + 4 * a + x]
            m, r = n + (a >> 1), 4 * (a & 1)
            cu[m, r : r + 4] = w[4:8]
            cd[m, r : r + 4] = w[0:4]
        n += 2


def coarse_level(
    own, left, right, yl, yr, cl, cr, gl, gr, pb, NW, NE, nd, po, bo, mine, other, F, EA, EB, EX, CW, R
):
    def put(i, j, half, f):
        f = OMEGA * f
        F[i, j, half] = f

    for x in range(CX):
        for half in range(2):
            for y in range(CY):
                at = 2 * (x * CY + y) + half
                put(x, y + CH, half, left[at])
                put(x + CH, y + CH, half, own[at])
                put(x + CH + CX, y + CH, half, right[at])
            for y in range(CH):
                put(x + CH, y, half, yl[2 * (x * CH + y) + half])
                put(x + CH, y + CH + CY, half, yr[2 * (x * CH + y) + half])
    n = 0
    for side in range(2):
        for dx, dy in CCELLS:
            i = CH + CX - 1 + dx if side else CH - dx
            for half in range(2):
                put(i, CH - dy, half, cl[n])
                put(i, CH + CY - 1 + dy, half, cr[n])
                n += 1

    for a in range(4):
        for i in range(CX + 2 * CH):
            p = i - CH
            src, x = (left, p + CX) if p < 0 else (own, p) if p < CX else (right, p - CX)
            R[a, i, JC : JC + CY] = src[NF + 4 * a + x]
            if 0 <= p < CX:
                lo = coarse_rows(gl, H * LX + LX + p, a)
                hi = coarse_rows(gr, H * LX + LX + p, a)
            elif p in CWP:
                m, r = n + 2 * CWP.index(p) + (a >> 1), 4 * (a & 1)
                lo, hi = cl[m, r : r + 4], cr[m, r : r + 4]
            else:
                continue
            R[a, i, JC - 4 : JC] = lo
            R[a, i, JC + CY : JC + CY + 4] = hi
    for i in range(1, CX + 2 * CH - 1):
        cx, lcx, cy, cz = R[0, i], R[0, i - 1], R[1, i], R[2, i]
        ws = (cx, lcx, cy, pltpu.roll(cy, 1, 0), cz, down_z(cz))
        total = ws[0] + ws[1] + ws[2] + ws[3] + ws[4] + ws[5]
        inv = OMEGA / (DIAG * total + SHIFT * R[3, i])
        for a in range(6):
            CW[a, i] = ws[a] * inv

    def sweep(src, dst):
        def body(i, reach):
            for j in range(CH - reach, CH + CY + reach):
                r = j - CH + JC
                ws = [row(CW, a, i, r) for a in range(6)]
                for half in range(2):
                    c = src[i, j, half]
                    dst[i, j, half] = (
                        (1.0 - OMEGA) * c
                        + F[i, j, half]
                        + ws[0] * src[i + 1, j, half]
                        + ws[1] * src[i - 1, j, half]
                        + ws[2] * src[i, j + 1, half]
                        + ws[3] * src[i, j - 1, half]
                        + ws[4] * up_z(c)
                        + ws[5] * down_z(c)
                    )

        return body

    planes(3, sweep(F, EB), CX, CH)
    planes(2, sweep(EB, EA), CX, CH)
    planes(1, sweep(EA, EB), CX, CH)

    def spread(i, reach):
        for j in range(CH - reach, CH + CY + reach):
            for half in range(2):
                EX[i, j, half] = expand(EB[i, j, half])

    planes(1, spread, CX, CH)

    for x in range(CX):
        for y in range(CY):
            for half in range(2):
                e = EX[x + CH, y + CH, half]
                ez = (up_z(e), down_z(e))
                ke = KEEP * e
                ce = C * e
                for dx in range(2):
                    ex = C * EX[x + CH + 2 * dx - 1, y + CH, half]
                    for dy in range(2):
                        ey = C * EX[x + CH, y + CH + 2 * dy - 1, half]
                        xx, yy = 2 * x + dx, 2 * y + dy
                        nw = [w_row(NW, NE, a, xx, yy) for a in range(6)]
                        s = (
                            ke
                            + (nw[dx] + nw[2 + dy]) * ce
                            + nw[1 - dx] * ex
                            + nw[3 - dy] * ey
                            + C * (nw[4] * ez[0] + nw[5] * ez[1])
                        )
                        if half == 0:
                            po[xx, yy] = pb[xx, yy, 0:8] - s
                        else:
                            bo[xx, yy] = pb[xx, yy, 8:16] + s

    def row8(ref, x, y, m, z):
        return jnp.broadcast_to(ref[x, y, m : m + 1, z], (8, 128))

    def gram(x, edge, acc):
        acc = list(acc)
        for yy in range(LY):
            deg = row(NE, 6, NH.index(0), yy) if edge else row(NW, 6, x - 1, yy + JW)
            for h in range(0, NZ, 128):
                z = slice(h, h + 128)
                p = po[x, yy, :, z]
                b = bo[x, yy, :, z]
                dp = deg[:, z] * p
                db = deg[:, z] * b
                for m in range(8):
                    acc[m] = acc[m] + dp * row8(po, x, yy, m, z)
                    acc[13 + m] = acc[13 + m] + dp * row8(bo, x, yy, m, z)
                for s in range(5):
                    acc[8 + s] = acc[8 + s] + b * (pltpu.roll(db, s, 0) if s else db)
        return tuple(acc)

    zero = jnp.zeros((8, 128), jnp.float32)
    acc = gram(0, True, (zero,) * 21)
    acc = list(lax.fori_loop(1, LX, lambda x, acc: gram(x, False, acc), acc))
    for q in range(2):
        acc.append(nd[q, :, :128] + nd[q, :, 128:])
    lane = lax.broadcasted_iota(jnp.int32, (8, 128), 1)
    sub = lax.broadcasted_iota(jnp.int32, (8, 128), 0)

    def collect(blocks):
        x = zero
        for n, a in enumerate(blocks):
            total = jnp.broadcast_to(jnp.sum(a, axis=1, keepdims=True), (8, 128))
            x = x + jnp.where(lane == 8 * n + sub, total, 0.0)
        return jnp.sum(x, axis=0, keepdims=True)

    t0 = collect(acc[:16])
    t1 = collect(acc[16:])
    even = lax.axis_index("gy") % 2 == 0
    mine[...] = jnp.where(even, t0, t1)
    other[...] = jnp.where(even, t1, t0)


def spread_sums(a, b, out):
    out[...] = jnp.broadcast_to((a[...] + b[...])[None], out.shape)


def finish(parts, po, bo, out, eig, SP, buf, sem):
    t = parts[...]
    n = t.shape[0]
    while n > 2:
        n //= 2
        t = t[:n] + t[n:]
    t = t[:, 0]
    lams = t[1:2] / pltpu.roll(t[1:2], 120, 1)
    eig[...] = pltpu.roll(lams, 88, 1)[:, :K]
    half = [jnp.broadcast_to(t[q : q + 1], (8, 128)) for q in range(2)]

    def entry(block, k):
        at = 8 * (block % 16) + k
        return jnp.broadcast_to(half[block // 16][:, at : at + 1], (8, 128))

    def sym(a, b):
        s = (a - b) % 8
        return entry(8 + s, a) if s < 5 else entry(16 - s, b)

    def cross(a, b):
        return entry(13 + b, a)

    lam = [entry(21, k) / entry(22, k) for k in range(K)]
    voxels = LX * LY * NZ * lax.axis_size("gx") * lax.axis_size("gy")
    g = {}
    for a in range(K):
        for b in range(a + 1):
            g[a, b] = (
                entry(b, a) + lam[b] * cross(a, b) + lam[a] * (cross(b, a) + lam[b] * sym(a, b))
            ) * (1.0 / voxels)
    low, inv = {}, []
    for j in range(K):
        d = g[j, j]
        r = lax.rsqrt(d)
        r = r * (1.5 - 0.5 * d * r * r)
        inv.append(r)
        for a in range(j + 1, K):
            low[a, j] = g[a, j] * r
        for a in range(j + 1, K):
            for b in range(j + 1, a + 1):
                g[a, b] = g[a, b] - low[a, j] * low[b, j]

    for k in range(K):
        SP[8 * k : 8 * k + 8] = lam[k]
        SP[64 + 8 * k : 72 + 8 * k] = inv[k]
    at = {}
    for n, (a, b) in enumerate(sorted(low)):
        at[a, b] = 128 + 8 * n
        SP[128 + 8 * n : 136 + 8 * n] = low[a, b]

    def body(x, _):
        for t in range(0, LY, 8):
            for h in range(0, NZ, 128):
                z = slice(h, h + 128)
                p = jnp.swapaxes(po[x, t : t + 8, :, z], 0, 1)
                b = jnp.swapaxes(bo[x, t : t + 8, :, z], 0, 1)
                done = []
                for k in range(K):
                    u = p[k] + SP[8 * k : 8 * k + 8] * b[k]
                    for j in range(k):
                        u = u - SP[at[k, j] : at[k, j] + 8] * done[j]
                    u = u * SP[64 + 8 * k : 72 + 8 * k]
                    done.append(u)
                    buf[k, x, t : t + 8, z] = u
        copy(x).start()
        return 0

    def copy(x):
        here = pl.ds(x, 1)
        return pltpu.make_async_copy(buf.at[:, here], out.at[:, here], sem.at[x])

    lax.fori_loop(0, LX, body, 0)
    for x in range(LX):
        copy(x).wait()


def both_ways(up, down, axis):
    n = lax.axis_size(axis)
    fwd = [(i, (i + 1) % n) for i in range(n)]
    back = [((i + 1) % n, i) for i in range(n)]
    return lax.ppermute(up, axis, fwd), lax.ppermute(down, axis, back)


def per_device(vectors, weight_x, weight_y, weight_z):
    args = (vectors, weight_x, weight_y, weight_z)
    xu, xd = call(
        x_send,
        [(NXU, LY, NZ), (NXD, LY, NZ)],
        args,
        [(NXU, LY, NZ), (NXD, LY, NZ), pltpu.SemaphoreType.DMA((4 * K + 12,))],
        limit=56,
        where=ANY,
    )
    rl, rr = both_ways(xu, xd, "gx")
    vt, wm, cw, yu, yd = call(
        local,
        [
            (LX, LY, K, NZ),
            (3, LX, LY, NZ),
            (4, CX, CY, CZ),
            (NYB, 8, NZ),
            (NYB, 8, NZ),
        ],
        args,
        [(5, CX * LY, CZ)],
    )
    yl, yr = both_ways(yu, yd, "gy")
    tall = LY + 2 * H
    W, NW, Y1, Y2, Y3 = call(
        fine_inner,
        [
            (3, LX, 32, NZ),
            (7, LX - 1, 32, NZ),
            (6, tall, K, NZ),
            (4, tall, K, NZ),
            (2, tall, K, NZ),
        ],
        (vt, wm, cw, yl, yr),
        us=3,
    )
    xl, xr, cu, cd = call(
        x_receive, [(NXB, 8, NZ), (NXB, 8, NZ), (NCB, 8, NZ), (NCB, 8, NZ)], (rl, rr, Y3)
    )
    cl, cr = both_ways(cu, cd, "gy")
    NE, Y1X, Y2X, Y3X, f, over = call(
        fine_outer,
        [
            (7, len(NH), LY, NZ),
            (6, tall, K, NZ),
            (6, tall, K, NZ),
            (6, tall, K, NZ),
            (NF + 4 * CX, 8, CZ),
            (CX, CY, CZ),
        ],
        (vt, wm, cw, xl, xr, yl, yr, W, NW, Y1, Y2, Y3),
        us=4,
    )
    f, fu, fd, fix = call(
        fine_corners,
        [(NF + 4 * CX, 8, CZ), (NF // 2, 8, CZ), (NF // 2, 8, CZ), (4, 4, 16, NZ)],
        (vt, xl, xr, yl, yr, W, NW, Y1, Y2, Y3, NE, Y1X, Y2X, Y3X, f, over, cl, cr),
    )
    left, right = both_ways(f, f, "gx")
    fl, fr = both_ways(fu, fd, "gy")
    pb, nd = call(
        meanwhile,
        [(LX, LY, 16, NZ), (2, 8, NZ)],
        (vt, NW, NE, Y1, Y2, Y3, Y1X, Y2X, Y3X, fix),
    )
    cu, cd = call(coarse_corner_send, [(NCC, 8, CZ)] * 2, (left, right, nd, fl, fr))
    cl, cr = both_ways(cu, cd, "gy")
    cext = (CX + 2 * CH, CY + 2 * CH, 2, 8, CZ)
    po, bo, mine, other = call(
        coarse_level,
        [(LX, LY, K, NZ), (LX, LY, K, NZ), (1, 128), (1, 128)],
        (f, left, right, fl, fr, cl, cr, yl, yr, pb, NW, NE, nd),
        [
            cext,
            cext,
            cext,
            (CX + 2 * CH, CY + 2 * CH, 2, 8, NZ),
            (6, CX + 2 * CH, 24, CZ),
            (4, CX + 2 * CH, 24, CZ),
        ],
        limit=12,
    )
    n = lax.axis_size("gy")
    theirs = lax.ppermute(other, "gy", [(i, i ^ 1) for i in range(n)])
    (sums,) = call(spread_sums, [(n * lax.axis_size("gx"), 1, 128)], (mine, theirs))
    parts = lax.all_to_all(sums, ("gx", "gy"), 0, 0)
    refined, eig = call(
        finish,
        [(K, LX, LY, NZ), (1, K)],
        (parts, po, bo),
        [(384, 128), (K, LX, LY, NZ), pltpu.SemaphoreType.DMA((LX,))],
        out_where=[ANY, VMEM],
    )
    return refined, eig.reshape(K)


def solution(mesh):
    return jax.shard_map(
        per_device,
        mesh=mesh,
        in_specs=(
            P(None, "gx", "gy", None),
            P("gx", "gy", None),
            P("gx", "gy", None),
            P("gx", "gy", None),
        ),
        out_specs=(P(None, "gx", "gy", None), P()),
        check_vma=False,
    )
```

```python
import jax
import jax.numpy as jnp
from jax import lax
from jax.experimental import pallas as pl
from jax.experimental.pallas import tpu as pltpu
from jax.sharding import PartitionSpec as P

OMEGA = 0.8
SHIFT = 0.1
DIAG = 1.0 + SHIFT
C = OMEGA / DIAG
Z0 = 2.0 * C - DIAG * C * C
Z1 = C * C
G0, G1, G2 = 1.0 - DIAG * Z0, Z0 - DIAG * Z1, Z1
KEEP = 1.0 - DIAG * C
B0, B1, B2 = KEEP * Z0 + C, KEEP * Z1 + C * Z0, C * Z1

K = 8
LX, LY, NZ = 8, 16, 256
CX, CY, CZ = LX // 2, LY // 2, NZ // 2
H = 3
CH = 4
JW = 8
MIB = 1024 * 1024
VMEM = pl.BlockSpec(memory_space=pltpu.VMEM)


ANY = pl.BlockSpec(memory_space=pl.ANY)


def call(body, outs, ins, scratch=(), limit=8, where=VMEM, us=1, out_where=None):
    return pl.pallas_call(
        body,
        out_shape=[jax.ShapeDtypeStruct(s, jnp.float32) for s in outs],
        in_specs=[where] * len(ins),
        out_specs=out_where or [where] * len(outs),
        scratch_shapes=[pltpu.VMEM(s, jnp.float32) if isinstance(s, tuple) else s for s in scratch],
        compiler_params=pltpu.CompilerParams(vmem_limit_bytes=limit * MIB),
        cost_estimate=pl.CostEstimate(
            flops=0, bytes_accessed=us * 3_000_000, transcendentals=0
        ),
    )(*ins)


def row(ref, *at):
    *lead, r = at
    r_ = ref[(*lead, pl.ds(r, 1), slice(None))]
    return jnp.broadcast_to(r_, (8, r_.shape[-1]))


def up_z(a):
    return pltpu.roll(a, a.shape[-1] - 1, a.ndim - 1)


def down_z(a):
    return pltpu.roll(a, 1, a.ndim - 1)


UP_W = [(0, 5), (0, 6), (0, 7), (1, 6), (1, 7), (2, 6), (2, 7)]
DN_W = [(0, 0), (0, 1), (1, 0), (1, 1), (2, 0), (2, 1)]
NV = H * LY
NXU = K * H + len(UP_W)
NXD = K * H + len(DN_W)
NXB = NV + 2 * len(UP_W)
NYB = H * LX + LX + CX
CELLS = [(1, 1), (1, 2), (2, 1)]
WP = [-2, -1, LX, LX + 1]
CWP = [-3, -2, -1, CX, CX + 1, CX + 2]
NCB = 2 * len(CELLS) + len(WP)


def put_rows(up, down, n, lows, highs):
    up[n, 0:2] = highs[0][6:8]
    up[n, 2:5] = highs[1][5:8]
    up[n, 5:8] = highs[2][5:8]
    down[n, 0:2] = lows[0][0:2]
    down[n, 2:4] = lows[1][0:2]
    down[n, 4:8] = lows[2][0:4]


def put_coarse_rows(up, down, n, arrays):
    for a, w in enumerate(arrays):
        r, z = 4 * (a & 1), 128 * (a >> 1)
        up[n, r : r + 4, z : z + 128] = w[4:8]
        down[n, r : r + 4, z : z + 128] = w[0:4]


def coarse_rows(msg, n, a):
    r, z = 4 * (a & 1), 128 * (a >> 1)
    return msg[n, r : r + 4, z : z + 128]


def x_send(v, wx, wy, wz, xu, xd, bu, bd, sem):
    pairs = []
    for k in range(K):
        pairs.append((v.at[k, LX - H : LX], bu.at[H * k : H * k + H], xu.at[H * k : H * k + H]))
        pairs.append((v.at[k, 0:H], bd.at[H * k : H * k + H], xd.at[H * k : H * k + H]))
    for buf, msg, side in ((bu, xu, UP_W), (bd, xd, DN_W)):
        at = K * H
        for w, ref in enumerate((wx, wy, wz)):
            p = [x for q, x in side if q == w]
            here = slice(at, at + len(p))
            pairs.append((ref.at[p[0] : p[-1] + 1], buf.at[here], msg.at[here]))
            at += len(p)
    n = len(pairs)
    ins = [pltpu.make_async_copy(a, b, sem.at[i]) for i, (a, b, _) in enumerate(pairs)]
    outs = [pltpu.make_async_copy(b, c, sem.at[n + i]) for i, (_, b, c) in enumerate(pairs)]
    for c in ins:
        c.start()
    for i, o in zip(ins, outs):
        i.wait()
        o.start()
    for o in outs:
        o.wait()


def local(v, wx, wy, wz, vt, wm, cw, yu, yd, Q):
    last_x = lax.axis_index("gx") == lax.axis_size("gx") - 1
    last_y = lax.axis_index("gy") == lax.axis_size("gy") - 1
    keep_x = jnp.where(last_x, 0.0, 1.0)
    keep_y = jnp.where(last_y, 0.0, 1.0)
    wm[0] = wx[...]
    wm[0, LX - 1] = wx[LX - 1] * keep_x
    sub = lax.broadcasted_iota(jnp.int32, (LX, LY, NZ), 1)
    wm[1] = jnp.where(sub == LY - 1, wy[...] * keep_y, wy[...])
    lane = lax.broadcasted_iota(jnp.int32, (LX, LY, NZ), 2)
    wm[2] = jnp.where(lane == NZ - 1, 0.0, wz[...])

    for x in range(CX):
        i = 2 * x
        wyp = wm[1, i] + wm[1, i + 1]
        wzp = wm[2, i] + wm[2, i + 1]
        parts = (
            (wm[0, i + 1], SUM),
            (wm[0, i], SUM),
            (wyp, SUM),
            (wzp, ODD),
            (wzp, EVEN),
        )
        for q, (a, how) in enumerate(parts):
            Q[q, x * LY : x * LY + 8] = compress(a[0:8], how)
            Q[q, x * LY + 8 : x * LY + 16] = compress(a[8:16], how)
    ri = lax.broadcasted_iota(jnp.int32, (CX * CY, CX * LY), 0)
    ci = lax.broadcasted_iota(jnp.int32, (CX * CY, CX * LY), 1)
    both = jnp.where((ci >> 1) == ri, 1.0, 0.0)
    first = jnp.where(ci == 2 * ri, 1.0, 0.0)
    second = jnp.where(ci == 2 * ri + 1, 1.0, 0.0)

    def rows(m, q):
        return jnp.dot(m, Q[q], precision=lax.Precision.HIGHEST, preferred_element_type=jnp.float32)

    inside = 2.0 * (rows(both, 1) + rows(first, 2) + rows(both, 4))
    for a, w in enumerate((rows(both, 0), rows(second, 2), rows(both, 3), inside)):
        for x in range(CX):
            cw[a, x] = w[x * CY : (x + 1) * CY]

    for x in range(LX):
        put_rows(
            yu,
            yd,
            H * LX + x,
            [wm[w, x, 0:8] for w in range(3)],
            [wm[w, x, 8:16] for w in range(3)],
        )
    for x in range(CX):
        put_coarse_rows(yu, yd, H * LX + LX + x, [cw[a, x] for a in range(4)])

    for x in range(LX):
        for t in range(0, LY, 8):
            vt[x, t : t + 8] = jnp.swapaxes(v[:, x, t : t + 8, :], 0, 1)
    for x in range(LX):
        for d in range(1, H + 1):
            yu[x * H + d - 1] = vt[x, LY - d]
            yd[x * H + d - 1] = vt[x, d - 1]


def x_cell(xl, xr, p, y):
    return xl[(p + H) * LY + y] if p < 0 else xr[(p - LX) * LY + y]


def x_weight(xl, xr, w, p):
    if p < 0:
        at = NV + 2 * UP_W.index((w, p + LX))
        return xl[at], xl[at + 1]
    at = NV + 2 * DN_W.index((w, p - LX))
    return xr[at], xr[at + 1]


def x_receive(rl, rr, after, xl, xr, cu, cd):
    first_x = lax.axis_index("gx") == 0
    last_y = lax.axis_index("gy") == lax.axis_size("gy") - 1
    keep_x = jnp.where(first_x, 0.0, 1.0)
    keep_y = jnp.where(last_y, 0.0, 1.0)
    sub = lax.broadcasted_iota(jnp.int32, (8, NZ), 0)
    lane = lax.broadcasted_iota(jnp.int32, (8, NZ), 1)
    for src, dst, side in ((rl, xl, UP_W), (rr, xr, DN_W)):
        for d in range(H):
            for t in range(0, LY, 8):
                block = jnp.stack([src[H * k + d, t : t + 8] for k in range(K)])
                dst[d * LY + t : d * LY + t + 8] = jnp.swapaxes(block, 0, 1)
        for n, (w, x) in enumerate(side):
            lo, hi = src[K * H + n, 0:8], src[K * H + n, 8:16]
            if w == 0 and x == LX - 1:
                lo, hi = lo * keep_x, hi * keep_x
            if w == 1:
                hi = jnp.where(sub == 7, hi * keep_y, hi)
            if w == 2:
                lo = jnp.where(lane == NZ - 1, 0.0, lo)
                hi = jnp.where(lane == NZ - 1, 0.0, hi)
            dst[NV + 2 * n] = lo
            dst[NV + 2 * n + 1] = hi
    n = 0
    for side in (-1, 1):
        for dx, dy in CELLS:
            p = -dx if side < 0 else LX - 1 + dx
            cu[n] = x_cell(xl, xr, p, LY - dy)
            cd[n] = x_cell(xl, xr, p, dy - 1)
            n += 1
    for p in WP:
        tiles = [x_weight(xl, xr, w, p) for w in range(3)]
        put_rows(cu, cd, n, [t[0] for t in tiles], [t[1] for t in tiles])
        n += 1


SUM, EVEN, ODD = 0, 1, 2


def compress(a, how=SUM):
    lane = lax.broadcasted_iota(jnp.int32, (8, 128), 1)
    t = a + up_z(a) if how == SUM else a
    at = (2 * lane + (1 if how == ODD else 0)) & 127
    lo = jnp.take_along_axis(t[:, :128], at, 1)
    hi = jnp.take_along_axis(t[:, 128:], at, 1)
    return jnp.where(lane < 64, lo, hi)


def expand(a):
    lane = lax.broadcasted_iota(jnp.int32, (8, 128), 1)
    half = lane >> 1
    return jnp.concatenate(
        [jnp.take_along_axis(a, half, 1), jnp.take_along_axis(a, half + 64, 1)], 1
    )


def stencil(w, at):
    c = at(0, 0)
    return (
        w(0) * at(1, 0)
        + w(1) * at(-1, 0)
        + w(2) * at(0, 1)
        + w(3) * at(0, -1)
        + w(4) * up_z(c)
        + w(5) * down_z(c)
    )


NH = [-2, -1, 0, 8, 9]
Y1E = [-2, -1, 0, 7, 8, 9]
Y2E = [-1, 0, 1, 6, 7, 8]
Y3E = [0, 1, 2, 5, 6, 7]


def pick(near, edge, planes_):
    first = next(p for p in range(LX) if p not in planes_)

    def cell(p, y):
        if p in planes_:
            return edge[planes_.index(p), y + H]
        return near[p - first, y + H]

    return cell


def v_cell(vt, xl, xr, yl, yr):
    def cell(p, y):
        if not isinstance(p, int) or 0 <= p < LX:
            if y < 0:
                return yl[p * H - y - 1]
            if y >= LY:
                return yr[p * H + y - LY]
            return vt[p, y]
        return x_cell(xl, xr, p, y)

    return cell


def w_row(NW, NE, a, p, y):
    if p in NH:
        return row(NE, a, NH.index(p), y)
    return row(NW, a, p - 1, y + JW)


def normalise(dst, i, wx, lx, wy, ly, wz):
    lz = down_z(wz)
    deg = wx + lx + wy + ly + wz + lz
    inv = 1.0 / deg
    for a, w in enumerate((wx, lx, wy, ly, wz, lz)):
        dst[a, i] = w * inv
    dst[6, i] = deg


def fine_inner(vt, wm, cw, yl, yr, W, NW, Y1, Y2, Y3):
    for w in range(3):
        W[w, :, JW : JW + LY] = wm[w]
    for x in range(LX):
        n = H * LX + x
        W[0, x, JW - 2 : JW] = yl[n, 0:2]
        W[1, x, JW - 3 : JW] = yl[n, 2:5]
        W[2, x, JW - 2 : JW] = yl[n, 6:8]
        W[0, x, JW + LY : JW + LY + 2] = yr[n, 0:2]
        W[1, x, JW + LY : JW + LY + 2] = yr[n, 2:4]
        W[2, x, JW + LY : JW + LY + 2] = yr[n, 4:6]

    def norm(x, _):
        wy = W[1, x]
        normalise(NW, x - 1, W[0, x], W[0, x - 1], wy, pltpu.roll(wy, 1, 0), W[2, x])
        return 0

    lax.fori_loop(1, LX, norm, 0)
    v = v_cell(vt, None, None, yl, yr)

    def power(at, dst, first, count, low, high):
        def body(n, _):
            p = first + n
            for y in range(low, high + 1):
                dst[n, y + H] = stencil(
                    lambda a: row(NW, a, p - 1, y + JW), lambda dx, dy: at(p + dx, y + dy)
                )
            return 0

        lax.fori_loop(0, count, body, 0)

    power(v, Y1, 1, 6, -2, 17)
    power(lambda p, y: Y1[p - 1, y + H], Y2, 2, 4, -1, 16)
    power(lambda p, y: Y2[p - 2, y + H], Y3, 3, 2, 0, 15)


def fine_outer(vt, wm, cw, xl, xr, yl, yr, W, NW, Y1, Y2, Y3, NE, Y1X, Y2X, Y3X, f, over):
    def own(w, p):
        if 0 <= p < LX:
            return wm[w, p]
        return jnp.concatenate(x_weight(xl, xr, w, p), 0)

    top = lax.broadcasted_iota(jnp.int32, (LY, NZ), 0) == 0
    for n, p in enumerate(NH):
        wy = own(1, p)
        ly = pltpu.roll(wy, 1, 0)
        if p == 0:
            ly = jnp.where(top, jnp.broadcast_to(W[1, 0, JW - 1 : JW], (LY, NZ)), ly)
        normalise(NE, n, own(0, p), own(0, p - 1), wy, ly, own(2, p))

    def power(at, dst, planes_, rows_):
        for n, p in enumerate(planes_):
            low, high = rows_[n if n < 3 else 5 - n]
            for y in range(low, high + 1):
                dst[n, y + H] = stencil(
                    lambda a: w_row(NW, NE, a, p, y), lambda dx, dy: at(p + dx, y + dy)
                )

    v = v_cell(vt, xl, xr, yl, yr)
    y1, y2, y3 = pick(Y1, Y1X, Y1E), pick(Y2, Y2X, Y2E), pick(Y3, Y3X, Y3E)
    power(v, Y1X, Y1E, ((1, 14), (1, 14), (0, 15)))
    power(y1, Y2X, Y2E, ((2, 13), (1, 14), (0, 15)))
    power(y2, Y3X, Y3E, ((2, 13), (1, 14), (0, 15)))

    first_row = lax.broadcasted_iota(jnp.int32, (CY, CZ), 0) == 0
    for x in range(CX):
        cx, cy, cz = cw[0, x], cw[1, x], cw[2, x]
        if x:
            lcx = cw[0, x - 1]
        else:
            both = pair_rows()
            flat = jnp.concatenate(
                [compress(t) for t in x_weight(xl, xr, 0, -1)], 0
            )
            lcx = jnp.dot(
                both, flat, precision=lax.Precision.HIGHEST, preferred_element_type=jnp.float32
            )
        edge = coarse_rows(yl, H * LX + LX + x, 1)[3:4]
        lcy = jnp.where(first_row, jnp.broadcast_to(edge, (CY, CZ)), pltpu.roll(cy, 1, 0))
        over[x] = 1.0 / (
            DIAG * (cx + lcx + cy + lcy + cz + down_z(cz)) + SHIFT * cw[3, x]
        )

    for x in range(CX):
        for y in range(CY):
            if x in (0, CX - 1) and y in (0, CY - 1):
                continue
            ra, rb = 0.0, 0.0
            for dx in range(2):
                for dy in range(2):
                    p, q = 2 * x + dx, 2 * y + dy
                    ga, gb = rest(v(p, q), y1(p, q), y2(p, q), y3(p, q))
                    deg = w_row(NW, NE, 6, p, q)
                    ra = ra + deg * ga
                    rb = rb + deg * gb
            inv = row(over, x, y)
            at = 2 * (x * CY + y)
            f[at] = compress(ra) * inv
            f[at + 1] = compress(rb) * inv
    for a in range(4):
        for x in range(CX):
            f[NF + 4 * a + x] = cw[a, x]


NF = 2 * CX * CY


def pair_rows():
    ri = lax.broadcasted_iota(jnp.int32, (CY, LY), 0)
    ci = lax.broadcasted_iota(jnp.int32, (CY, LY), 1)
    return jnp.where((ci >> 1) == ri, 1.0, 0.0)


def rest(v, y1, y2, y3):
    gb = G0 * v + G1 * y1 + G2 * y2
    return gb - (G0 * y1 + G1 * y2 + G2 * y3), gb


def smooth(v, y1, y2, y3):
    b = B0 * v + B1 * y1 + B2 * y2
    return v - (b - (B0 * y1 + B1 * y2 + B2 * y3)), b


def fine_corners(
    vt, xl, xr, yl, yr, W, NW, Y1, Y2, Y3, NE, Y1X, Y2X, Y3X, f_, over, cl, cr, f, fu, fd, fix
):
    f[...] = f_[...]
    old = (
        v_cell(vt, xl, xr, yl, yr),
        pick(Y1, Y1X, Y1E),
        pick(Y2, Y2X, Y2E),
        pick(Y3, Y3X, Y3E),
    )
    for side in range(2):
        for top in range(2):
            msg = cr if top else cl

            def px(dx):
                return LX - 1 + dx if side else -dx

            def py(dy):
                return LY - 1 + dy if top else -dy

            got = {}
            for n, (dx, dy) in enumerate(CELLS):
                got[px(dx), py(dy)] = msg[len(CELLS) * side + n]

            def raw(w, x, y):
                out_x = x < 0 or x >= LX
                out_y = y < 0 or y >= LY
                if out_x and out_y:
                    n = 2 * len(CELLS) + WP.index(x)
                    if top:
                        r = (0, 2, 4)[w] + y - LY
                    else:
                        r = (2, 5, 8)[w] + y
                    return msg[n, r : r + 1]
                if out_x:
                    tile = x_weight(xl, xr, w, x)[y >> 3]
                    return tile[y & 7 : (y & 7) + 1]
                return W[w, x, y + JW : y + JW + 1]

            weights = {}

            def weight(x, y):
                if (x, y) not in weights:
                    wx, lx = raw(0, x, y), raw(0, x - 1, y)
                    wy, ly = raw(1, x, y), raw(1, x, y - 1)
                    wz = raw(2, x, y)
                    ws = (wx, lx, wy, ly, wz, down_z(wz))
                    inv = 1.0 / (wx + lx + wy + ly + wz + ws[5])
                    weights[x, y] = [jnp.broadcast_to(w * inv, (8, NZ)) for w in ws]
                return weights[x, y]

            def look(known, cell):
                def at(x, y):
                    return known[x, y] if (x, y) in known else cell(x, y)

                return at

            def run(at, cells, fresh):
                out = {}
                for dx, dy in cells:
                    x, y = px(dx), py(dy)
                    if fresh(dx, dy):
                        ws = weight(x, y)
                    else:
                        ws = [w_row(NW, NE, a, x, y) for a in range(6)]
                    out[x, y] = stencil(
                        lambda a: ws[a], lambda ex, ey: at(x + ex, y + ey)
                    )
                return out

            def fresh(dx, dy):
                return (dx > 0 and dy >= 0) or (dy > 0 and dx >= 0)

            v = look(got, old[0])
            y1 = look(run(v, [(1, 0), (2, 0), (1, 1), (0, 1), (0, 2)], fresh), old[1])
            y2 = look(run(y1, [(0, 0), (1, 0), (1, -1), (0, 1), (-1, 1)], fresh), old[2])
            y3 = look(run(y2, [(0, 0), (-1, 0), (0, -1)], fresh), old[3])
            ra, rb = 0.0, 0.0
            for n, (dx, dy) in enumerate(((0, 0), (-1, 0), (0, -1), (-1, -1))):
                x, y = px(dx), py(dy)
                four = (v(x, y), y1(x, y), y2(x, y), y3(x, y))
                ga, gb = rest(*four)
                deg = w_row(NW, NE, 6, x, y)
                ra = ra + deg * ga
                rb = rb + deg * gb
                p, b = smooth(*four)
                fix[2 * side + top, n, 0:8] = p
                fix[2 * side + top, n, 8:16] = b
            x, y = (CX - 1) * side, (CY - 1) * top
            inv = row(over, x, y)
            at = 2 * (x * CY + y)
            f[at] = compress(ra) * inv
            f[at + 1] = compress(rb) * inv
    for x in range(CX):
        at = 2 * x * CY
        fd[8 * x : 8 * x + 8] = f[at : at + 8]
        fu[8 * x : 8 * x + 8] = f[at + 8 : at + 16]


def meanwhile(vt, NW, NE, Y1, Y2, Y3, Y1X, Y2X, Y3X, fix, pb, nd):
    y1, y2, y3 = pick(Y1, Y1X, Y1E), pick(Y2, Y2X, Y2E), pick(Y3, Y3X, Y3E)
    num = den = jnp.zeros((8, NZ), jnp.float32)
    corner = {}
    for side in range(2):
        for top in range(2):
            for n, (dx, dy) in enumerate(((0, 0), (-1, 0), (0, -1), (-1, -1))):
                x = LX - 1 + dx if side else -dx
                y = LY - 1 + dy if top else -dy
                corner[x, y] = 2 * side + top, n
    for x in range(LX):
        for y in range(LY):
            v, nv = vt[x, y], y1(x, y)
            if (x, y) in corner:
                pb[x, y] = fix[corner[x, y]]
            else:
                p, b = smooth(v, nv, y2(x, y), y3(x, y))
                pb[x, y, 0:8] = p
                pb[x, y, 8:16] = b
            dv = w_row(NW, NE, 6, x, y) * v
            num = num + dv * (v - nv)
            den = den + dv * v
    nd[0] = num
    nd[1] = den


JC = 8
CCELLS = [(dx, dy) for dx in (1, 2, 3) for dy in range(1, CH + 1 - dx)]


NCC = 4 * len(CCELLS) + 2 * len(CWP)


def coarse_corner_send(left, right, after, yl, yr, cu, cd):
    n = 0
    for side in range(2):
        for dx, dy in CCELLS:
            x = dx - 1 if side else CX - dx
            src = right if side else left
            for half in range(2):
                cu[n] = src[2 * (x * CY + CY - dy) + half]
                cd[n] = src[2 * (x * CY + dy - 1) + half]
                n += 1
    for p in CWP:
        src, x = (left, p + CX) if p < 0 else (right, p - CX)
        for a in range(4):
            w = src[NF + 4 * a + x]
            m, r = n + (a >> 1), 4 * (a & 1)
            cu[m, r : r + 4] = w[4:8]
            cd[m, r : r + 4] = w[0:4]
        n += 2


def beyond(i, j):
    return max(CH - i, i - CH - CX + 1, 0), max(CH - j, j - CH - CY + 1, 0)


def cells_within(radius):
    every = [(i, j) for i in range(CX + 2 * CH) for j in range(CY + 2 * CH)]
    return [c for c in every if sum(beyond(*c)) <= radius]


def early(before, radius):
    out = set()
    for i, j in cells_within(radius):
        dx, dy = beyond(i, j)
        if dx and not CH < j < CH + CY - 1 or dy and not CH < i < CH + CX - 1:
            continue
        if {(i, j), (i + 1, j), (i - 1, j), (i, j + 1), (i, j - 1)} <= before:
            out.add((i, j))
    return out


EARLY0 = {c for c in cells_within(CH) if 0 in beyond(*c)}
EARLY1 = early(EARLY0, 3)
EARLY2 = early(EARLY1, 2)
EARLY3 = early(EARLY2, 1)


def coarse_weights(own, left, right, gl, gr, corner, CW, R):
    for a in range(4):
        for i in range(CX + 2 * CH):
            p = i - CH
            src, x = (left, p + CX) if p < 0 else (own, p) if p < CX else (right, p - CX)
            R[a, i, JC : JC + CY] = src[NF + 4 * a + x]
            if 0 <= p < CX:
                lo = coarse_rows(gl, H * LX + LX + p, a)
                hi = coarse_rows(gr, H * LX + LX + p, a)
            elif corner and p in CWP:
                m, r = 4 * len(CCELLS) + 2 * CWP.index(p) + (a >> 1), 4 * (a & 1)
                lo, hi = corner[0][m, r : r + 4], corner[1][m, r : r + 4]
            else:
                continue
            R[a, i, JC - 4 : JC] = lo
            R[a, i, JC + CY : JC + CY + 4] = hi
    for i in range(1, CX + 2 * CH - 1):
        cx, lcx, cy, cz = R[0, i], R[0, i - 1], R[1, i], R[2, i]
        ws = (cx, lcx, cy, pltpu.roll(cy, 1, 0), cz, down_z(cz))
        total = ws[0] + ws[1] + ws[2] + ws[3] + ws[4] + ws[5]
        inv = OMEGA / (DIAG * total + SHIFT * R[3, i])
        for a in range(6):
            CW[a, i] = ws[a] * inv


def sweep(cells, at, f, CW, dst):
    for i, j in cells:
        ws = [row(CW, a, i, j - CH + JC) for a in range(6)]
        for half in range(2):
            c = at(i, j, half)
            dst[i, j, half] = (
                (1.0 - OMEGA) * c
                + f(i, j, half)
                + ws[0] * at(i + 1, j, half)
                + ws[1] * at(i - 1, j, half)
                + ws[2] * at(i, j + 1, half)
                + ws[3] * at(i, j - 1, half)
                + ws[4] * up_z(c)
                + ws[5] * down_z(c)
            )


def coarse_early(own, left, right, yl, yr, gl, gr, F, E1, E2, E3, CW, R):
    for x in range(CX):
        for half in range(2):
            for y in range(CY):
                at = 2 * (x * CY + y) + half
                F[x, y + CH, half] = OMEGA * left[at]
                F[x + CH, y + CH, half] = OMEGA * own[at]
                F[x + CH + CX, y + CH, half] = OMEGA * right[at]
            for y in range(CH):
                F[x + CH, y, half] = OMEGA * yl[2 * (x * CH + y) + half]
                F[x + CH, y + CH + CY, half] = OMEGA * yr[2 * (x * CH + y) + half]
    coarse_weights(own, left, right, gl, gr, None, CW, R)

    def of(ref):
        return lambda i, j, half: ref[i, j, half]

    sweep(sorted(EARLY1), of(F), of(F), CW, E1)
    sweep(sorted(EARLY2), of(E1), of(F), CW, E2)
    sweep(sorted(EARLY3), of(E2), of(F), CW, E3)


def coarse_level(
    own,
    left,
    right,
    cl,
    cr,
    gl,
    gr,
    F,
    E1,
    E2,
    E3,
    pb,
    NW,
    NE,
    nd,
    po,
    bo,
    mine,
    other,
    X1,
    X2,
    X3,
    EX,
    CW,
    R,
):
    coarse_weights(own, left, right, gl, gr, (cl, cr), CW, R)
    corner = {}
    n = 0
    for side in range(2):
        for dx, dy in CCELLS:
            i = CH + CX - 1 + dx if side else CH - dx
            for half in range(2):
                corner[i, CH - dy, half] = cl, n
                corner[i, CH + CY - 1 + dy, half] = cr, n
                n += 1

    def f(i, j, half):
        if (i, j, half) in corner:
            msg, n = corner[i, j, half]
            return OMEGA * msg[n]
        return F[i, j, half]

    def both(first, cells, then):
        return lambda i, j, half: (first if (i, j) in cells else then)[i, j, half]

    e1, e2, e3 = both(E1, EARLY1, X1), both(E2, EARLY2, X2), both(E3, EARLY3, X3)
    sweep([c for c in cells_within(3) if c not in EARLY1], f, f, CW, X1)
    sweep([c for c in cells_within(2) if c not in EARLY2], e1, f, CW, X2)
    sweep([c for c in cells_within(1) if c not in EARLY3], e2, f, CW, X3)
    for i, j in cells_within(1):
        for half in range(2):
            EX[i, j, half] = expand(e3(i, j, half))

    for x in range(CX):
        for y in range(CY):
            for half in range(2):
                e = EX[x + CH, y + CH, half]
                ez = (up_z(e), down_z(e))
                ke = KEEP * e
                ce = C * e
                for dx in range(2):
                    ex = C * EX[x + CH + 2 * dx - 1, y + CH, half]
                    for dy in range(2):
                        ey = C * EX[x + CH, y + CH + 2 * dy - 1, half]
                        xx, yy = 2 * x + dx, 2 * y + dy
                        nw = [w_row(NW, NE, a, xx, yy) for a in range(6)]
                        s = (
                            ke
                            + (nw[dx] + nw[2 + dy]) * ce
                            + nw[1 - dx] * ex
                            + nw[3 - dy] * ey
                            + C * (nw[4] * ez[0] + nw[5] * ez[1])
                        )
                        if half == 0:
                            po[xx, yy] = pb[xx, yy, 0:8] - s
                        else:
                            bo[xx, yy] = pb[xx, yy, 8:16] + s

    def row8(ref, x, y, m, z):
        return jnp.broadcast_to(ref[x, y, m : m + 1, z], (8, 128))

    def gram(x, edge, acc):
        acc = list(acc)
        for yy in range(LY):
            deg = row(NE, 6, NH.index(0), yy) if edge else row(NW, 6, x - 1, yy + JW)
            for h in range(0, NZ, 128):
                z = slice(h, h + 128)
                p = po[x, yy, :, z]
                b = bo[x, yy, :, z]
                dp = deg[:, z] * p
                db = deg[:, z] * b
                for m in range(8):
                    acc[m] = acc[m] + dp * row8(po, x, yy, m, z)
                    acc[13 + m] = acc[13 + m] + dp * row8(bo, x, yy, m, z)
                for s in range(5):
                    acc[8 + s] = acc[8 + s] + b * (pltpu.roll(db, s, 0) if s else db)
        return tuple(acc)

    zero = jnp.zeros((8, 128), jnp.float32)
    acc = gram(0, True, (zero,) * 21)
    acc = list(lax.fori_loop(1, LX, lambda x, acc: gram(x, False, acc), acc))
    for q in range(2):
        acc.append(nd[q, :, :128] + nd[q, :, 128:])
    lane = lax.broadcasted_iota(jnp.int32, (8, 128), 1)
    sub = lax.broadcasted_iota(jnp.int32, (8, 128), 0)

    def collect(blocks):
        x = zero
        for n, a in enumerate(blocks):
            total = jnp.broadcast_to(jnp.sum(a, axis=1, keepdims=True), (8, 128))
            x = x + jnp.where(lane == 8 * n + sub, total, 0.0)
        return jnp.sum(x, axis=0, keepdims=True)

    t0 = collect(acc[:16])
    t1 = collect(acc[16:])
    even = lax.axis_index("gy") % 2 == 0
    mine[...] = jnp.where(even, t0, t1)
    other[...] = jnp.where(even, t1, t0)


def spread_sums(a, b, out):
    out[...] = jnp.broadcast_to((a[...] + b[...])[None], out.shape)


def finish(parts, po, bo, out, eig, SP, buf, sem):
    t = parts[...]
    n = t.shape[0]
    while n > 2:
        n //= 2
        t = t[:n] + t[n:]
    t = t[:, 0]
    lams = t[1:2] / pltpu.roll(t[1:2], 120, 1)
    eig[...] = pltpu.roll(lams, 88, 1)[:, :K]
    half = [jnp.broadcast_to(t[q : q + 1], (8, 128)) for q in range(2)]

    def entry(block, k):
        at = 8 * (block % 16) + k
        return jnp.broadcast_to(half[block // 16][:, at : at + 1], (8, 128))

    def sym(a, b):
        s = (a - b) % 8
        return entry(8 + s, a) if s < 5 else entry(16 - s, b)

    def cross(a, b):
        return entry(13 + b, a)

    lam = [entry(21, k) / entry(22, k) for k in range(K)]
    voxels = LX * LY * NZ * lax.axis_size("gx") * lax.axis_size("gy")
    g = {}
    for a in range(K):
        for b in range(a + 1):
            g[a, b] = (
                entry(b, a) + lam[b] * cross(a, b) + lam[a] * (cross(b, a) + lam[b] * sym(a, b))
            ) * (1.0 / voxels)
    low, inv = {}, []
    for j in range(K):
        d = g[j, j]
        r = lax.rsqrt(d)
        r = r * (1.5 - 0.5 * d * r * r)
        inv.append(r)
        for a in range(j + 1, K):
            low[a, j] = g[a, j] * r
        for a in range(j + 1, K):
            for b in range(j + 1, a + 1):
                g[a, b] = g[a, b] - low[a, j] * low[b, j]

    sub = lax.broadcasted_iota(jnp.int32, (8, 128), 0)
    lam_rows = jnp.zeros((8, 128), jnp.float32)
    for k in range(K):
        lam_rows = jnp.where(sub == k, lam[k], lam_rows)
        SP[64 + 8 * k : 72 + 8 * k] = inv[k]
    at = {}
    for n, (a, b) in enumerate(sorted(low)):
        at[a, b] = 128 + 8 * n
        SP[128 + 8 * n : 136 + 8 * n] = low[a, b]

    def body(x, _):
        for t in range(0, LY, 8):
            for h in range(0, NZ, 128):
                z = slice(h, h + 128)
                upd = po[x, t : t + 8, :, z] + lam_rows[None] * bo[x, t : t + 8, :, z]
                upd = jnp.swapaxes(upd, 0, 1)
                done = []
                for k in range(K):
                    u = upd[k]
                    for j in range(k):
                        u = u - SP[at[k, j] : at[k, j] + 8] * done[j]
                    u = u * SP[64 + 8 * k : 72 + 8 * k]
                    done.append(u)
                    buf[k, x, t : t + 8, z] = u
        copy(x).start()
        return 0

    def copy(x):
        here = pl.ds(x, 1)
        return pltpu.make_async_copy(buf.at[:, here], out.at[:, here], sem.at[x])

    lax.fori_loop(0, LX, body, 0)
    for x in range(LX):
        copy(x).wait()


def both_ways(up, down, axis):
    n = lax.axis_size(axis)
    fwd = [(i, (i + 1) % n) for i in range(n)]
    back = [((i + 1) % n, i) for i in range(n)]
    return lax.ppermute(up, axis, fwd), lax.ppermute(down, axis, back)


def per_device(vectors, weight_x, weight_y, weight_z):
    args = (vectors, weight_x, weight_y, weight_z)
    xu, xd = call(
        x_send,
        [(NXU, LY, NZ), (NXD, LY, NZ)],
        args,
        [(NXU, LY, NZ), (NXD, LY, NZ), pltpu.SemaphoreType.DMA((4 * K + 12,))],
        limit=56,
        where=ANY,
    )
    rl, rr = both_ways(xu, xd, "gx")
    vt, wm, cw, yu, yd = call(
        local,
        [
            (LX, LY, K, NZ),
            (3, LX, LY, NZ),
            (4, CX, CY, CZ),
            (NYB, 8, NZ),
            (NYB, 8, NZ),
        ],
        args,
        [(5, CX * LY, CZ)],
    )
    yl, yr = both_ways(yu, yd, "gy")
    tall = LY + 2 * H
    W, NW, Y1, Y2, Y3 = call(
        fine_inner,
        [
            (3, LX, 32, NZ),
            (7, LX - 1, 32, NZ),
            (6, tall, K, NZ),
            (4, tall, K, NZ),
            (2, tall, K, NZ),
        ],
        (vt, wm, cw, yl, yr),
        us=3,
    )
    xl, xr, cu, cd = call(
        x_receive, [(NXB, 8, NZ), (NXB, 8, NZ), (NCB, 8, NZ), (NCB, 8, NZ)], (rl, rr, Y3)
    )
    cl, cr = both_ways(cu, cd, "gy")
    NE, Y1X, Y2X, Y3X, f, over = call(
        fine_outer,
        [
            (7, len(NH), LY, NZ),
            (6, tall, K, NZ),
            (6, tall, K, NZ),
            (6, tall, K, NZ),
            (NF + 4 * CX, 8, CZ),
            (CX, CY, CZ),
        ],
        (vt, wm, cw, xl, xr, yl, yr, W, NW, Y1, Y2, Y3),
        us=4,
    )
    f, fu, fd, fix = call(
        fine_corners,
        [(NF + 4 * CX, 8, CZ), (NF // 2, 8, CZ), (NF // 2, 8, CZ), (4, 4, 16, NZ)],
        (vt, xl, xr, yl, yr, W, NW, Y1, Y2, Y3, NE, Y1X, Y2X, Y3X, f, over, cl, cr),
    )
    left, right = both_ways(f, f, "gx")
    fl, fr = both_ways(fu, fd, "gy")
    pb, nd = call(
        meanwhile,
        [(LX, LY, 16, NZ), (2, 8, NZ)],
        (vt, NW, NE, Y1, Y2, Y3, Y1X, Y2X, Y3X, fix),
    )
    cu, cd = call(coarse_corner_send, [(NCC, 8, CZ)] * 2, (left, right, nd, fl, fr))
    cl, cr = both_ways(cu, cd, "gy")
    cext = (CX + 2 * CH, CY + 2 * CH, 2, 8, CZ)
    weights = [(6, CX + 2 * CH, 24, CZ), (4, CX + 2 * CH, 24, CZ)]
    early_ = call(
        coarse_early, [cext] * 4, (f, left, right, fl, fr, yl, yr), weights, us=2
    )
    po, bo, mine, other = call(
        coarse_level,
        [(LX, LY, K, NZ), (LX, LY, K, NZ), (1, 128), (1, 128)],
        (f, left, right, cl, cr, yl, yr, *early_, pb, NW, NE, nd),
        [cext, cext, cext, (CX + 2 * CH, CY + 2 * CH, 2, 8, NZ)] + weights,
        limit=12,
    )
    n = lax.axis_size("gy")
    theirs = lax.ppermute(other, "gy", [(i, i ^ 1) for i in range(n)])
    (sums,) = call(spread_sums, [(n * lax.axis_size("gx"), 1, 128)], (mine, theirs))
    parts = lax.all_to_all(sums, ("gx", "gy"), 0, 0)
    refined, eig = call(
        finish,
        [(K, LX, LY, NZ), (1, K)],
        (parts, po, bo),
        [(384, 128), (K, LX, LY, NZ), pltpu.SemaphoreType.DMA((LX,))],
        out_where=[ANY, VMEM],
    )
    return refined, eig.reshape(K)


def solution(mesh):
    return jax.shard_map(
        per_device,
        mesh=mesh,
        in_specs=(
            P(None, "gx", "gy", None),
            P("gx", "gy", None),
            P("gx", "gy", None),
            P("gx", "gy", None),
        ),
        out_specs=(P(None, "gx", "gy", None), P()),
        check_vma=False,
    )
```

```python
import jax
import jax.numpy as jnp
from jax import lax
from jax.experimental import pallas as pl
from jax.experimental.pallas import tpu as pltpu
from jax.sharding import PartitionSpec as P

OMEGA = 0.8
SHIFT = 0.1
DIAG = 1.0 + SHIFT
C = OMEGA / DIAG
Z0 = 2.0 * C - DIAG * C * C
Z1 = C * C
G0, G1, G2 = 1.0 - DIAG * Z0, Z0 - DIAG * Z1, Z1
KEEP = 1.0 - DIAG * C
B0, B1, B2 = KEEP * Z0 + C, KEEP * Z1 + C * Z0, C * Z1

K = 8
LX, LY, NZ = 8, 16, 256
CX, CY, CZ = LX // 2, LY // 2, NZ // 2
H = 3
CH = 4
JW = 8
MIB = 1024 * 1024
VMEM = pl.BlockSpec(memory_space=pltpu.VMEM)


ANY = pl.BlockSpec(memory_space=pl.ANY)


def call(body, outs, ins, scratch=(), limit=8, where=VMEM, us=1):
    return pl.pallas_call(
        body,
        out_shape=[jax.ShapeDtypeStruct(s, jnp.float32) for s in outs],
        in_specs=[where] * len(ins),
        out_specs=[where] * len(outs),
        scratch_shapes=[pltpu.VMEM(s, jnp.float32) if isinstance(s, tuple) else s for s in scratch],
        compiler_params=pltpu.CompilerParams(vmem_limit_bytes=limit * MIB),
        cost_estimate=pl.CostEstimate(
            flops=0, bytes_accessed=us * 3_000_000, transcendentals=0
        ),
    )(*ins)


def row(ref, *at):
    *lead, r = at
    r_ = ref[(*lead, pl.ds(r, 1), slice(None))]
    return jnp.broadcast_to(r_, (8, r_.shape[-1]))


def up_z(a):
    return pltpu.roll(a, a.shape[-1] - 1, a.ndim - 1)


def down_z(a):
    return pltpu.roll(a, 1, a.ndim - 1)


UP_W = [(0, 5), (0, 6), (0, 7), (1, 6), (1, 7), (2, 6), (2, 7)]
DN_W = [(0, 0), (0, 1), (1, 0), (1, 1), (2, 0), (2, 1)]
NV = H * LY
NXU = K * H + len(UP_W)
NXD = K * H + len(DN_W)
NXB = NV + 2 * len(UP_W)
NYB = H * LX + LX + CX
CELLS = [(1, 1), (1, 2), (2, 1)]
WP = [-2, -1, LX, LX + 1]
CWP = [-3, -2, -1, CX, CX + 1, CX + 2]
NCB = 2 * len(CELLS) + len(WP)


def put_rows(up, down, n, lows, highs):
    up[n, 0:2] = highs[0][6:8]
    up[n, 2:5] = highs[1][5:8]
    up[n, 5:8] = highs[2][5:8]
    down[n, 0:2] = lows[0][0:2]
    down[n, 2:4] = lows[1][0:2]
    down[n, 4:8] = lows[2][0:4]


def put_coarse_rows(up, down, n, arrays):
    for a, w in enumerate(arrays):
        r, z = 4 * (a & 1), 128 * (a >> 1)
        up[n, r : r + 4, z : z + 128] = w[4:8]
        down[n, r : r + 4, z : z + 128] = w[0:4]


def coarse_rows(msg, n, a):
    r, z = 4 * (a & 1), 128 * (a >> 1)
    return msg[n, r : r + 4, z : z + 128]


def x_send(v, wx, wy, wz, xu, xd, bu, bd, sem):
    pairs = []
    for k in range(K):
        pairs.append((v.at[k, LX - H : LX], bu.at[H * k : H * k + H], xu.at[H * k : H * k + H]))
        pairs.append((v.at[k, 0:H], bd.at[H * k : H * k + H], xd.at[H * k : H * k + H]))
    for buf, msg, side in ((bu, xu, UP_W), (bd, xd, DN_W)):
        at = K * H
        for w, ref in enumerate((wx, wy, wz)):
            p = [x for q, x in side if q == w]
            here = slice(at, at + len(p))
            pairs.append((ref.at[p[0] : p[-1] + 1], buf.at[here], msg.at[here]))
            at += len(p)
    n = len(pairs)
    ins = [pltpu.make_async_copy(a, b, sem.at[i]) for i, (a, b, _) in enumerate(pairs)]
    outs = [pltpu.make_async_copy(b, c, sem.at[n + i]) for i, (_, b, c) in enumerate(pairs)]
    for c in ins:
        c.start()
    for i, o in zip(ins, outs):
        i.wait()
        o.start()
    for o in outs:
        o.wait()


def local(v, w_, vt, wm, cw, yu, yd, Q):
    last_x = lax.axis_index("gx") == lax.axis_size("gx") - 1
    last_y = lax.axis_index("gy") == lax.axis_size("gy") - 1
    keep_x = jnp.where(last_x, 0.0, 1.0)
    keep_y = jnp.where(last_y, 0.0, 1.0)
    wm[0] = w_[0]
    wm[0, LX - 1] = w_[0, LX - 1] * keep_x
    sub = lax.broadcasted_iota(jnp.int32, (LX, LY, NZ), 1)
    wm[1] = jnp.where(sub == LY - 1, w_[1] * keep_y, w_[1])
    lane = lax.broadcasted_iota(jnp.int32, (LX, LY, NZ), 2)
    wm[2] = jnp.where(lane == NZ - 1, 0.0, w_[2])

    for x in range(CX):
        i = 2 * x
        wyp = wm[1, i] + wm[1, i + 1]
        wzp = wm[2, i] + wm[2, i + 1]
        parts = (
            (wm[0, i + 1], SUM),
            (wm[0, i], SUM),
            (wyp, SUM),
            (wzp, ODD),
            (wzp, EVEN),
        )
        for q, (a, how) in enumerate(parts):
            Q[q, x * LY : x * LY + 8] = compress(a[0:8], how)
            Q[q, x * LY + 8 : x * LY + 16] = compress(a[8:16], how)
    ri = lax.broadcasted_iota(jnp.int32, (CX * CY, CX * LY), 0)
    ci = lax.broadcasted_iota(jnp.int32, (CX * CY, CX * LY), 1)
    both = jnp.where((ci >> 1) == ri, 1.0, 0.0)
    first = jnp.where(ci == 2 * ri, 1.0, 0.0)
    second = jnp.where(ci == 2 * ri + 1, 1.0, 0.0)

    def rows(m, q):
        return jnp.dot(m, Q[q], precision=lax.Precision.HIGHEST, preferred_element_type=jnp.float32)

    inside = 2.0 * (rows(both, 1) + rows(first, 2) + rows(both, 4))
    for a, w in enumerate((rows(both, 0), rows(second, 2), rows(both, 3), inside)):
        for x in range(CX):
            cw[a, x] = w[x * CY : (x + 1) * CY]

    for x in range(LX):
        put_rows(
            yu,
            yd,
            H * LX + x,
            [wm[w, x, 0:8] for w in range(3)],
            [wm[w, x, 8:16] for w in range(3)],
        )
    for x in range(CX):
        put_coarse_rows(yu, yd, H * LX + LX + x, [cw[a, x] for a in range(4)])

    for x in range(LX):
        for t in range(0, LY, 8):
            vt[x, t : t + 8] = jnp.swapaxes(v[:, x, t : t + 8, :], 0, 1)
    for x in range(LX):
        for d in range(1, H + 1):
            yu[x * H + d - 1] = vt[x, LY - d]
            yd[x * H + d - 1] = vt[x, d - 1]


def x_cell(xl, xr, p, y):
    return xl[(p + H) * LY + y] if p < 0 else xr[(p - LX) * LY + y]


def x_weight(xl, xr, w, p):
    if p < 0:
        at = NV + 2 * UP_W.index((w, p + LX))
        return xl[at], xl[at + 1]
    at = NV + 2 * DN_W.index((w, p - LX))
    return xr[at], xr[at + 1]


def x_receive(rl, rr, after, xl, xr, cu, cd):
    first_x = lax.axis_index("gx") == 0
    last_y = lax.axis_index("gy") == lax.axis_size("gy") - 1
    keep_x = jnp.where(first_x, 0.0, 1.0)
    keep_y = jnp.where(last_y, 0.0, 1.0)
    sub = lax.broadcasted_iota(jnp.int32, (8, NZ), 0)
    lane = lax.broadcasted_iota(jnp.int32, (8, NZ), 1)
    for src, dst, side in ((rl, xl, UP_W), (rr, xr, DN_W)):
        for d in range(H):
            for t in range(0, LY, 8):
                block = jnp.stack([src[H * k + d, t : t + 8] for k in range(K)])
                dst[d * LY + t : d * LY + t + 8] = jnp.swapaxes(block, 0, 1)
        for n, (w, x) in enumerate(side):
            lo, hi = src[K * H + n, 0:8], src[K * H + n, 8:16]
            if w == 0 and x == LX - 1:
                lo, hi = lo * keep_x, hi * keep_x
            if w == 1:
                hi = jnp.where(sub == 7, hi * keep_y, hi)
            if w == 2:
                lo = jnp.where(lane == NZ - 1, 0.0, lo)
                hi = jnp.where(lane == NZ - 1, 0.0, hi)
            dst[NV + 2 * n] = lo
            dst[NV + 2 * n + 1] = hi
    n = 0
    for side in (-1, 1):
        for dx, dy in CELLS:
            p = -dx if side < 0 else LX - 1 + dx
            cu[n] = x_cell(xl, xr, p, LY - dy)
            cd[n] = x_cell(xl, xr, p, dy - 1)
            n += 1
    for p in WP:
        tiles = [x_weight(xl, xr, w, p) for w in range(3)]
        put_rows(cu, cd, n, [t[0] for t in tiles], [t[1] for t in tiles])
        n += 1


SUM, EVEN, ODD = 0, 1, 2


def compress(a, how=SUM):
    lane = lax.broadcasted_iota(jnp.int32, (8, 128), 1)
    t = a + up_z(a) if how == SUM else a
    at = (2 * lane + (1 if how == ODD else 0)) & 127
    lo = jnp.take_along_axis(t[:, :128], at, 1)
    hi = jnp.take_along_axis(t[:, 128:], at, 1)
    return jnp.where(lane < 64, lo, hi)


def expand(a):
    lane = lax.broadcasted_iota(jnp.int32, (8, 128), 1)
    half = lane >> 1
    return jnp.concatenate(
        [jnp.take_along_axis(a, half, 1), jnp.take_along_axis(a, half + 64, 1)], 1
    )


def stencil(w, at, without=None):
    c = at(0, 0)
    total = w(2) * at(0, 1) + w(3) * at(0, -1) + w(4) * up_z(c) + w(5) * down_z(c)
    for a, dx in ((0, 1), (1, -1)):
        if a != without:
            total = total + w(a) * at(dx, 0)
    return total


NH = [-2, -1, 0, 8, 9]
Y1E = [-2, -1, 0, 7, 8, 9]
Y2E = [-1, 0, 1, 6, 7, 8]
Y3E = [0, 1, 2, 5, 6, 7]
LACK = {(1, 7): 0, (2, 1): 1, (2, 6): 0, (3, 2): 1, (3, 5): 0}


def pick(near, edge, planes_):
    first = next(p for p in range(LX) if p not in planes_)

    def cell(p, y):
        if p in planes_:
            return edge[planes_.index(p), y + H]
        return near[p - first, y + H]

    return cell


def v_cell(vt, xl, xr, yl, yr):
    def cell(p, y):
        if not isinstance(p, int) or 0 <= p < LX:
            if y < 0:
                return yl[p * H - y - 1]
            if y >= LY:
                return yr[p * H + y - LY]
            return vt[p, y]
        return x_cell(xl, xr, p, y)

    return cell


def w_row(NW, NE, a, p, y):
    if p in NH:
        return row(NE, a, NH.index(p), y)
    return row(NW, a, p - 1, y + JW)


def normalise(dst, i, wx, lx, wy, ly, wz):
    lz = down_z(wz)
    deg = wx + lx + wy + ly + wz + lz
    inv = 1.0 / deg
    for a, w in enumerate((wx, lx, wy, ly, wz, lz)):
        dst[a, i] = w * inv
    dst[6, i] = deg


def fine_inner(vt, wm, cw, yl, yr, W, NW, Y1, Y2, Y3, PX):
    for w in range(3):
        W[w, :, JW : JW + LY] = wm[w]
    for x in range(LX):
        n = H * LX + x
        W[0, x, JW - 2 : JW] = yl[n, 0:2]
        W[1, x, JW - 3 : JW] = yl[n, 2:5]
        W[2, x, JW - 2 : JW] = yl[n, 6:8]
        W[0, x, JW + LY : JW + LY + 2] = yr[n, 0:2]
        W[1, x, JW + LY : JW + LY + 2] = yr[n, 2:4]
        W[2, x, JW + LY : JW + LY + 2] = yr[n, 4:6]

    def norm(x, _):
        wy = W[1, x]
        normalise(NW, x - 1, W[0, x], W[0, x - 1], wy, pltpu.roll(wy, 1, 0), W[2, x])
        return 0

    lax.fori_loop(1, LX, norm, 0)
    v = v_cell(vt, None, None, yl, yr)

    def power(at, dst, first, count, low, high):
        def body(n, _):
            p = first + n
            for y in range(low, high + 1):
                dst[n, y + H] = stencil(
                    lambda a: row(NW, a, p - 1, y + JW), lambda dx, dy: at(p + dx, y + dy)
                )
            return 0

        lax.fori_loop(0, count, body, 0)

    def y1(p, y):
        return Y1[p - 1, y + H]

    def y2(p, y):
        return Y2[p - 2, y + H]

    power(v, Y1, 1, 6, -2, 17)
    power(y1, Y2, 2, 4, -1, 16)
    power(y2, Y3, 3, 2, 0, 15)
    for n, ((power_, p), without) in enumerate(LACK.items()):
        at = (v, y1, y2)[power_ - 1]
        for y in range(LY):
            PX[n, y] = stencil(
                lambda a: row(NW, a, p - 1, y + JW), lambda dx, dy: at(p + dx, y + dy), without
            )


def fine_outer(vt, wm, cw, xl, xr, yl, yr, W, NW, Y1, Y2, Y3, PX, NE, Y1X, Y2X, Y3X, f, over):
    def own(w, p):
        if 0 <= p < LX:
            return wm[w, p]
        return jnp.concatenate(x_weight(xl, xr, w, p), 0)

    top = lax.broadcasted_iota(jnp.int32, (LY, NZ), 0) == 0
    for n, p in enumerate(NH):
        wy = own(1, p)
        ly = pltpu.roll(wy, 1, 0)
        if p == 0:
            ly = jnp.where(top, jnp.broadcast_to(W[1, 0, JW - 1 : JW], (LY, NZ)), ly)
        normalise(NE, n, own(0, p), own(0, p - 1), wy, ly, own(2, p))

    def power(power_, at, dst, planes_, rows_):
        for n, p in enumerate(planes_):
            low, high = rows_[n if n < 3 else 5 - n]
            lack = LACK.get((power_, p))
            for y in range(low, high + 1):
                if lack is not None:
                    m = list(LACK).index((power_, p))
                    term = w_row(NW, NE, lack, p, y) * at(p + (-1 if lack else 1), y)
                    dst[n, y + H] = PX[m, y] + term
                    continue
                dst[n, y + H] = stencil(
                    lambda a: w_row(NW, NE, a, p, y), lambda dx, dy: at(p + dx, y + dy)
                )

    v = v_cell(vt, xl, xr, yl, yr)
    y1, y2, y3 = pick(Y1, Y1X, Y1E), pick(Y2, Y2X, Y2E), pick(Y3, Y3X, Y3E)
    power(1, v, Y1X, Y1E, ((1, 14), (1, 14), (0, 15)))
    power(2, y1, Y2X, Y2E, ((2, 13), (1, 14), (0, 15)))
    power(3, y2, Y3X, Y3E, ((2, 13), (1, 14), (0, 15)))

    first_row = lax.broadcasted_iota(jnp.int32, (CY, CZ), 0) == 0
    for x in range(CX):
        cx, cy, cz = cw[0, x], cw[1, x], cw[2, x]
        if x:
            lcx = cw[0, x - 1]
        else:
            both = pair_rows()
            flat = jnp.concatenate(
                [compress(t) for t in x_weight(xl, xr, 0, -1)], 0
            )
            lcx = jnp.dot(
                both, flat, precision=lax.Precision.HIGHEST, preferred_element_type=jnp.float32
            )
        edge = coarse_rows(yl, H * LX + LX + x, 1)[3:4]
        lcy = jnp.where(first_row, jnp.broadcast_to(edge, (CY, CZ)), pltpu.roll(cy, 1, 0))
        over[x] = 1.0 / (
            DIAG * (cx + lcx + cy + lcy + cz + down_z(cz)) + SHIFT * cw[3, x]
        )

    for x in range(CX):
        for y in range(CY):
            if x in (0, CX - 1) and y in (0, CY - 1):
                continue
            ra, rb = 0.0, 0.0
            for dx in range(2):
                for dy in range(2):
                    p, q = 2 * x + dx, 2 * y + dy
                    ga, gb = rest(v(p, q), y1(p, q), y2(p, q), y3(p, q))
                    deg = w_row(NW, NE, 6, p, q)
                    ra = ra + deg * ga
                    rb = rb + deg * gb
            inv = row(over, x, y)
            at = 2 * (x * CY + y)
            f[at] = compress(ra) * inv
            f[at + 1] = compress(rb) * inv
    for a in range(4):
        for x in range(CX):
            f[NF + 4 * a + x] = cw[a, x]


NF = 2 * CX * CY


def pair_rows():
    ri = lax.broadcasted_iota(jnp.int32, (CY, LY), 0)
    ci = lax.broadcasted_iota(jnp.int32, (CY, LY), 1)
    return jnp.where((ci >> 1) == ri, 1.0, 0.0)


def rest(v, y1, y2, y3):
    gb = G0 * v + G1 * y1 + G2 * y2
    return gb - (G0 * y1 + G1 * y2 + G2 * y3), gb


def smooth(v, y1, y2, y3):
    b = B0 * v + B1 * y1 + B2 * y2
    return v - (b - (B0 * y1 + B1 * y2 + B2 * y3)), b


def fine_corners(
    vt, xl, xr, yl, yr, W, NW, Y1, Y2, Y3, NE, Y1X, Y2X, Y3X, f_, over, cl, cr, f, fu, fd, fix
):
    f[...] = f_[...]
    old = (
        v_cell(vt, xl, xr, yl, yr),
        pick(Y1, Y1X, Y1E),
        pick(Y2, Y2X, Y2E),
        pick(Y3, Y3X, Y3E),
    )
    for side in range(2):
        for top in range(2):
            msg = cr if top else cl

            def px(dx):
                return LX - 1 + dx if side else -dx

            def py(dy):
                return LY - 1 + dy if top else -dy

            got = {}
            for n, (dx, dy) in enumerate(CELLS):
                got[px(dx), py(dy)] = msg[len(CELLS) * side + n]

            def raw(w, x, y):
                out_x = x < 0 or x >= LX
                out_y = y < 0 or y >= LY
                if out_x and out_y:
                    n = 2 * len(CELLS) + WP.index(x)
                    if top:
                        r = (0, 2, 4)[w] + y - LY
                    else:
                        r = (2, 5, 8)[w] + y
                    return msg[n, r : r + 1]
                if out_x:
                    tile = x_weight(xl, xr, w, x)[y >> 3]
                    return tile[y & 7 : (y & 7) + 1]
                return W[w, x, y + JW : y + JW + 1]

            weights = {}

            def weight(x, y):
                if (x, y) not in weights:
                    wx, lx = raw(0, x, y), raw(0, x - 1, y)
                    wy, ly = raw(1, x, y), raw(1, x, y - 1)
                    wz = raw(2, x, y)
                    ws = (wx, lx, wy, ly, wz, down_z(wz))
                    inv = 1.0 / (wx + lx + wy + ly + wz + ws[5])
                    weights[x, y] = [jnp.broadcast_to(w * inv, (8, NZ)) for w in ws]
                return weights[x, y]

            def look(known, cell):
                def at(x, y):
                    return known[x, y] if (x, y) in known else cell(x, y)

                return at

            def run(at, cells, fresh):
                out = {}
                for dx, dy in cells:
                    x, y = px(dx), py(dy)
                    if fresh(dx, dy):
                        ws = weight(x, y)
                    else:
                        ws = [w_row(NW, NE, a, x, y) for a in range(6)]
                    out[x, y] = stencil(
                        lambda a: ws[a], lambda ex, ey: at(x + ex, y + ey)
                    )
                return out

            def fresh(dx, dy):
                return (dx > 0 and dy >= 0) or (dy > 0 and dx >= 0)

            v = look(got, old[0])
            y1 = look(run(v, [(1, 0), (2, 0), (1, 1), (0, 1), (0, 2)], fresh), old[1])
            y2 = look(run(y1, [(0, 0), (1, 0), (1, -1), (0, 1), (-1, 1)], fresh), old[2])
            y3 = look(run(y2, [(0, 0), (-1, 0), (0, -1)], fresh), old[3])
            ra, rb = 0.0, 0.0
            for n, (dx, dy) in enumerate(((0, 0), (-1, 0), (0, -1), (-1, -1))):
                x, y = px(dx), py(dy)
                four = (v(x, y), y1(x, y), y2(x, y), y3(x, y))
                ga, gb = rest(*four)
                deg = w_row(NW, NE, 6, x, y)
                ra = ra + deg * ga
                rb = rb + deg * gb
                p, b = smooth(*four)
                fix[2 * side + top, n, 0:8] = p
                fix[2 * side + top, n, 8:16] = b
            x, y = (CX - 1) * side, (CY - 1) * top
            inv = row(over, x, y)
            at = 2 * (x * CY + y)
            f[at] = compress(ra) * inv
            f[at + 1] = compress(rb) * inv
    for x in range(CX):
        at = 2 * x * CY
        fd[8 * x : 8 * x + 8] = f[at : at + 8]
        fu[8 * x : 8 * x + 8] = f[at + 8 : at + 16]


def meanwhile(vt, NW, NE, Y1, Y2, Y3, Y1X, Y2X, Y3X, fix, pb, nd):
    y1, y2, y3 = pick(Y1, Y1X, Y1E), pick(Y2, Y2X, Y2E), pick(Y3, Y3X, Y3E)
    num = den = jnp.zeros((8, NZ), jnp.float32)
    corner = {}
    for side in range(2):
        for top in range(2):
            for n, (dx, dy) in enumerate(((0, 0), (-1, 0), (0, -1), (-1, -1))):
                x = LX - 1 + dx if side else -dx
                y = LY - 1 + dy if top else -dy
                corner[x, y] = 2 * side + top, n
    for x in range(LX):
        for y in range(LY):
            v, nv = vt[x, y], y1(x, y)
            if (x, y) in corner:
                pb[x, y] = fix[corner[x, y]]
            else:
                p, b = smooth(v, nv, y2(x, y), y3(x, y))
                pb[x, y, 0:8] = p
                pb[x, y, 8:16] = b
            dv = w_row(NW, NE, 6, x, y) * v
            num = num + dv * (v - nv)
            den = den + dv * v
    nd[0] = num
    nd[1] = den


JC = 8
CCELLS = [(dx, dy) for dx in (1, 2, 3) for dy in range(1, CH + 1 - dx)]


NCC = 4 * len(CCELLS) + 2 * len(CWP)


def coarse_corner_send(left, right, after, yl, yr, cu, cd):
    n = 0
    for side in range(2):
        for dx, dy in CCELLS:
            x = dx - 1 if side else CX - dx
            src = right if side else left
            for half in range(2):
                cu[n] = src[2 * (x * CY + CY - dy) + half]
                cd[n] = src[2 * (x * CY + dy - 1) + half]
                n += 1
    for p in CWP:
        src, x = (left, p + CX) if p < 0 else (right, p - CX)
        for a in range(4):
            w = src[NF + 4 * a + x]
            m, r = n + (a >> 1), 4 * (a & 1)
            cu[m, r : r + 4] = w[4:8]
            cd[m, r : r + 4] = w[0:4]
        n += 2


def beyond(i, j):
    return max(CH - i, i - CH - CX + 1, 0), max(CH - j, j - CH - CY + 1, 0)


def cells_within(radius):
    every = [(i, j) for i in range(CX + 2 * CH) for j in range(CY + 2 * CH)]
    return [c for c in every if sum(beyond(*c)) <= radius]


def early(before, radius):
    out = set()
    for i, j in cells_within(radius):
        dx, dy = beyond(i, j)
        if dx and not CH < j < CH + CY - 1 or dy and not CH < i < CH + CX - 1:
            continue
        if {(i, j), (i + 1, j), (i - 1, j), (i, j + 1), (i, j - 1)} <= before:
            out.add((i, j))
    return out


EARLY0 = {c for c in cells_within(CH) if 0 in beyond(*c)}
EARLY1 = early(EARLY0, 3)
EARLY2 = early(EARLY1, 2)
EARLY3 = early(EARLY2, 1)


def coarse_weights(own, left, right, gl, gr, corner, CW, R):
    for a in range(4):
        for i in range(CX + 2 * CH):
            p = i - CH
            src, x = (left, p + CX) if p < 0 else (own, p) if p < CX else (right, p - CX)
            R[a, i, JC : JC + CY] = src[NF + 4 * a + x]
            if 0 <= p < CX:
                lo = coarse_rows(gl, H * LX + LX + p, a)
                hi = coarse_rows(gr, H * LX + LX + p, a)
            elif corner and p in CWP:
                m, r = 4 * len(CCELLS) + 2 * CWP.index(p) + (a >> 1), 4 * (a & 1)
                lo, hi = corner[0][m, r : r + 4], corner[1][m, r : r + 4]
            else:
                continue
            R[a, i, JC - 4 : JC] = lo
            R[a, i, JC + CY : JC + CY + 4] = hi
    for i in range(1, CX + 2 * CH - 1):
        cx, lcx, cy, cz = R[0, i], R[0, i - 1], R[1, i], R[2, i]
        ws = (cx, lcx, cy, pltpu.roll(cy, 1, 0), cz, down_z(cz))
        total = ws[0] + ws[1] + ws[2] + ws[3] + ws[4] + ws[5]
        inv = OMEGA / (DIAG * total + SHIFT * R[3, i])
        for a in range(6):
            CW[a, i] = ws[a] * inv


def sweep(cells, at, f, CW, dst):
    for i, j in cells:
        ws = [row(CW, a, i, j - CH + JC) for a in range(6)]
        for half in range(2):
            c = at(i, j, half)
            dst[i, j, half] = (
                (1.0 - OMEGA) * c
                + f(i, j, half)
                + ws[0] * at(i + 1, j, half)
                + ws[1] * at(i - 1, j, half)
                + ws[2] * at(i, j + 1, half)
                + ws[3] * at(i, j - 1, half)
                + ws[4] * up_z(c)
                + ws[5] * down_z(c)
            )


def coarse_early(own, left, right, yl, yr, gl, gr, F, E1, E2, E3, CW, R):
    for x in range(CX):
        for half in range(2):
            for y in range(CY):
                at = 2 * (x * CY + y) + half
                F[x, y + CH, half] = OMEGA * left[at]
                F[x + CH, y + CH, half] = OMEGA * own[at]
                F[x + CH + CX, y + CH, half] = OMEGA * right[at]
            for y in range(CH):
                F[x + CH, y, half] = OMEGA * yl[2 * (x * CH + y) + half]
                F[x + CH, y + CH + CY, half] = OMEGA * yr[2 * (x * CH + y) + half]
    coarse_weights(own, left, right, gl, gr, None, CW, R)

    def of(ref):
        return lambda i, j, half: ref[i, j, half]

    sweep(sorted(EARLY1), of(F), of(F), CW, E1)
    sweep(sorted(EARLY2), of(E1), of(F), CW, E2)
    sweep(sorted(EARLY3), of(E2), of(F), CW, E3)


def coarse_level(
    own,
    left,
    right,
    cl,
    cr,
    gl,
    gr,
    F,
    E1,
    E2,
    E3,
    pb,
    NW,
    NE,
    nd,
    po,
    bo,
    mine,
    other,
    X1,
    X2,
    X3,
    EX,
    CW,
    R,
):
    coarse_weights(own, left, right, gl, gr, (cl, cr), CW, R)
    corner = {}
    n = 0
    for side in range(2):
        for dx, dy in CCELLS:
            i = CH + CX - 1 + dx if side else CH - dx
            for half in range(2):
                corner[i, CH - dy, half] = cl, n
                corner[i, CH + CY - 1 + dy, half] = cr, n
                n += 1

    def f(i, j, half):
        if (i, j, half) in corner:
            msg, n = corner[i, j, half]
            return OMEGA * msg[n]
        return F[i, j, half]

    def both(first, cells, then):
        return lambda i, j, half: (first if (i, j) in cells else then)[i, j, half]

    e1, e2, e3 = both(E1, EARLY1, X1), both(E2, EARLY2, X2), both(E3, EARLY3, X3)
    sweep([c for c in cells_within(3) if c not in EARLY1], f, f, CW, X1)
    sweep([c for c in cells_within(2) if c not in EARLY2], e1, f, CW, X2)
    sweep([c for c in cells_within(1) if c not in EARLY3], e2, f, CW, X3)
    for i, j in cells_within(1):
        for half in range(2):
            EX[i, j, half] = expand(e3(i, j, half))

    for x in range(CX):
        for y in range(CY):
            for half in range(2):
                e = EX[x + CH, y + CH, half]
                ez = (up_z(e), down_z(e))
                ke = KEEP * e
                ce = C * e
                for dx in range(2):
                    ex = C * EX[x + CH + 2 * dx - 1, y + CH, half]
                    for dy in range(2):
                        ey = C * EX[x + CH, y + CH + 2 * dy - 1, half]
                        xx, yy = 2 * x + dx, 2 * y + dy
                        nw = [w_row(NW, NE, a, xx, yy) for a in range(6)]
                        s = (
                            ke
                            + (nw[dx] + nw[2 + dy]) * ce
                            + nw[1 - dx] * ex
                            + nw[3 - dy] * ey
                            + C * (nw[4] * ez[0] + nw[5] * ez[1])
                        )
                        if half == 0:
                            po[xx, yy] = pb[xx, yy, 0:8] - s
                        else:
                            bo[xx, yy] = pb[xx, yy, 8:16] + s

    def row8(ref, x, y, m, z):
        return jnp.broadcast_to(ref[x, y, m : m + 1, z], (8, 128))

    def gram(x, edge, acc):
        acc = list(acc)
        for yy in range(LY):
            deg = row(NE, 6, NH.index(0), yy) if edge else row(NW, 6, x - 1, yy + JW)
            for h in range(0, NZ, 128):
                z = slice(h, h + 128)
                p = po[x, yy, :, z]
                b = bo[x, yy, :, z]
                dp = deg[:, z] * p
                db = deg[:, z] * b
                for m in range(8):
                    acc[m] = acc[m] + dp * row8(po, x, yy, m, z)
                    acc[13 + m] = acc[13 + m] + dp * row8(bo, x, yy, m, z)
                for s in range(5):
                    acc[8 + s] = acc[8 + s] + b * (pltpu.roll(db, s, 0) if s else db)
        return tuple(acc)

    zero = jnp.zeros((8, 128), jnp.float32)
    acc = gram(0, True, (zero,) * 21)
    acc = list(lax.fori_loop(1, LX, lambda x, acc: gram(x, False, acc), acc))
    for q in range(2):
        acc.append(nd[q, :, :128] + nd[q, :, 128:])
    lane = lax.broadcasted_iota(jnp.int32, (8, 128), 1)
    sub = lax.broadcasted_iota(jnp.int32, (8, 128), 0)

    def collect(blocks):
        x = zero
        for n, a in enumerate(blocks):
            total = jnp.broadcast_to(jnp.sum(a, axis=1, keepdims=True), (8, 128))
            x = x + jnp.where(lane == 8 * n + sub, total, 0.0)
        return jnp.sum(x, axis=0, keepdims=True)

    t0 = collect(acc[:16])
    t1 = collect(acc[16:])
    even = lax.axis_index("gy") % 2 == 0
    mine[...] = jnp.where(even, t0, t1)
    other[...] = jnp.where(even, t1, t0)


def spread_sums(a, b, out):
    out[...] = jnp.broadcast_to((a[...] + b[...])[None], out.shape)


def finish(parts, po, bo, out, eig, SP):
    t = parts[...]
    n = t.shape[0]
    while n > 2:
        n //= 2
        t = t[:n] + t[n:]
    t = t[:, 0]
    lams = t[1:2] / pltpu.roll(t[1:2], 120, 1)
    eig[...] = pltpu.roll(lams, 88, 1)[:, :K]
    half = [jnp.broadcast_to(t[q : q + 1], (8, 128)) for q in range(2)]

    def entry(block, k):
        at = 8 * (block % 16) + k
        return jnp.broadcast_to(half[block // 16][:, at : at + 1], (8, 128))

    def sym(a, b):
        s = (a - b) % 8
        return entry(8 + s, a) if s < 5 else entry(16 - s, b)

    def cross(a, b):
        return entry(13 + b, a)

    lam = [entry(21, k) / entry(22, k) for k in range(K)]
    voxels = LX * LY * NZ * lax.axis_size("gx") * lax.axis_size("gy")
    g = {}
    for a in range(K):
        for b in range(a + 1):
            g[a, b] = (
                entry(b, a) + lam[b] * cross(a, b) + lam[a] * (cross(b, a) + lam[b] * sym(a, b))
            ) * (1.0 / voxels)
    low, inv = {}, []
    for j in range(K):
        d = g[j, j]
        r = lax.rsqrt(d)
        r = r * (1.5 - 0.5 * d * r * r)
        inv.append(r)
        for a in range(j + 1, K):
            low[a, j] = g[a, j] * r
        for a in range(j + 1, K):
            for b in range(j + 1, a + 1):
                g[a, b] = g[a, b] - low[a, j] * low[b, j]

    sub = lax.broadcasted_iota(jnp.int32, (8, 128), 0)
    lam_rows = jnp.zeros((8, 128), jnp.float32)
    for k in range(K):
        lam_rows = jnp.where(sub == k, lam[k], lam_rows)
        SP[64 + 8 * k : 72 + 8 * k] = inv[k]
    at = {}
    for n, (a, b) in enumerate(sorted(low)):
        at[a, b] = 128 + 8 * n
        SP[128 + 8 * n : 136 + 8 * n] = low[a, b]

    def body(x, _):
        for t in range(0, LY, 8):
            for h in range(0, NZ, 128):
                z = slice(h, h + 128)
                upd = po[x, t : t + 8, :, z] + lam_rows[None] * bo[x, t : t + 8, :, z]
                upd = jnp.swapaxes(upd, 0, 1)
                done = []
                for k in range(K):
                    u = upd[k]
                    for j in range(k):
                        u = u - SP[at[k, j] : at[k, j] + 8] * done[j]
                    u = u * SP[64 + 8 * k : 72 + 8 * k]
                    done.append(u)
                    out[k, x, t : t + 8, z] = u
        return 0

    lax.fori_loop(0, LX, body, 0)


def both_ways(up, down, axis):
    n = lax.axis_size(axis)
    fwd = [(i, (i + 1) % n) for i in range(n)]
    back = [((i + 1) % n, i) for i in range(n)]
    return lax.ppermute(up, axis, fwd), lax.ppermute(down, axis, back)


def per_device(vectors, weight_x, weight_y, weight_z):
    args = (vectors, weight_x, weight_y, weight_z)
    xu, xd = call(
        x_send,
        [(NXU, LY, NZ), (NXD, LY, NZ)],
        args,
        [(NXU, LY, NZ), (NXD, LY, NZ), pltpu.SemaphoreType.DMA((4 * K + 12,))],
        limit=56,
        where=ANY,
    )
    rl, rr = both_ways(xu, xd, "gx")
    vt, wm, cw, yu, yd = call(
        local,
        [
            (LX, LY, K, NZ),
            (3, LX, LY, NZ),
            (4, CX, CY, CZ),
            (NYB, 8, NZ),
            (NYB, 8, NZ),
        ],
        (vectors, jnp.stack(args[1:])),
        [(5, CX * LY, CZ)],
    )
    yl, yr = both_ways(yu, yd, "gy")
    tall = LY + 2 * H
    W, NW, Y1, Y2, Y3, PX = call(
        fine_inner,
        [
            (3, LX, 32, NZ),
            (7, LX - 1, 32, NZ),
            (6, tall, K, NZ),
            (4, tall, K, NZ),
            (2, tall, K, NZ),
            (len(LACK), LY, K, NZ),
        ],
        (vt, wm, cw, yl, yr),
        us=3,
    )
    xl, xr, cu, cd = call(
        x_receive, [(NXB, 8, NZ), (NXB, 8, NZ), (NCB, 8, NZ), (NCB, 8, NZ)], (rl, rr, Y3)
    )
    cl, cr = both_ways(cu, cd, "gy")
    NE, Y1X, Y2X, Y3X, f, over = call(
        fine_outer,
        [
            (7, len(NH), LY, NZ),
            (6, tall, K, NZ),
            (6, tall, K, NZ),
            (6, tall, K, NZ),
            (NF + 4 * CX, 8, CZ),
            (CX, CY, CZ),
        ],
        (vt, wm, cw, xl, xr, yl, yr, W, NW, Y1, Y2, Y3, PX),
        us=4,
    )
    f, fu, fd, fix = call(
        fine_corners,
        [(NF + 4 * CX, 8, CZ), (NF // 2, 8, CZ), (NF // 2, 8, CZ), (4, 4, 16, NZ)],
        (vt, xl, xr, yl, yr, W, NW, Y1, Y2, Y3, NE, Y1X, Y2X, Y3X, f, over, cl, cr),
    )
    left, right = both_ways(f, f, "gx")
    fl, fr = both_ways(fu, fd, "gy")
    pb, nd = call(
        meanwhile,
        [(LX, LY, 16, NZ), (2, 8, NZ)],
        (vt, NW, NE, Y1, Y2, Y3, Y1X, Y2X, Y3X, fix),
    )
    cu, cd = call(coarse_corner_send, [(NCC, 8, CZ)] * 2, (left, right, nd, fl, fr))
    cl, cr = both_ways(cu, cd, "gy")
    cext = (CX + 2 * CH, CY + 2 * CH, 2, 8, CZ)
    weights = [(6, CX + 2 * CH, 24, CZ), (4, CX + 2 * CH, 24, CZ)]
    early_ = call(
        coarse_early, [cext] * 4, (f, left, right, fl, fr, yl, yr), weights, us=2
    )
    po, bo, mine, other = call(
        coarse_level,
        [(LX, LY, K, NZ), (LX, LY, K, NZ), (1, 128), (1, 128)],
        (f, left, right, cl, cr, yl, yr, *early_, pb, NW, NE, nd),
        [cext, cext, cext, (CX + 2 * CH, CY + 2 * CH, 2, 8, NZ)] + weights,
        limit=12,
    )
    n = lax.axis_size("gy")
    theirs = lax.ppermute(other, "gy", [(i, i ^ 1) for i in range(n)])
    (sums,) = call(spread_sums, [(n * lax.axis_size("gx"), 1, 128)], (mine, theirs))
    parts = lax.all_to_all(sums, ("gx", "gy"), 0, 0)
    refined, eig = call(
        finish,
        [(K, LX, LY, NZ), (1, K)],
        (parts, po, bo),
        [(384, 128)],
    )
    return refined, eig.reshape(K)


def solution(mesh):
    return jax.shard_map(
        per_device,
        mesh=mesh,
        in_specs=(
            P(None, "gx", "gy", None),
            P("gx", "gy", None),
            P("gx", "gy", None),
            P("gx", "gy", None),
        ),
        out_specs=(P(None, "gx", "gy", None), P()),
        check_vma=False,
    )
```

```python
import jax
import jax.numpy as jnp
from jax import lax
from jax.experimental import pallas as pl
from jax.experimental.pallas import tpu as pltpu
from jax.sharding import PartitionSpec as P

OMEGA = 0.8
SHIFT = 0.1
DIAG = 1.0 + SHIFT
C = OMEGA / DIAG
Z0 = 2.0 * C - DIAG * C * C
Z1 = C * C
G0, G1, G2 = 1.0 - DIAG * Z0, Z0 - DIAG * Z1, Z1
KEEP = 1.0 - DIAG * C
B0, B1, B2 = KEEP * Z0 + C, KEEP * Z1 + C * Z0, C * Z1

K = 8
LX, LY, NZ = 8, 16, 256
CX, CY, CZ = LX // 2, LY // 2, NZ // 2
H = 3
CH = 4
JW = 8
MIB = 1024 * 1024
VMEM = pl.BlockSpec(memory_space=pltpu.VMEM)


ANY = pl.BlockSpec(memory_space=pl.ANY)


def call(body, outs, ins, scratch=(), limit=8, where=VMEM, us=1):
    return pl.pallas_call(
        body,
        out_shape=[jax.ShapeDtypeStruct(s, jnp.float32) for s in outs],
        in_specs=[where] * len(ins),
        out_specs=[where] * len(outs),
        scratch_shapes=[pltpu.VMEM(s, jnp.float32) if isinstance(s, tuple) else s for s in scratch],
        compiler_params=pltpu.CompilerParams(vmem_limit_bytes=limit * MIB),
        cost_estimate=pl.CostEstimate(
            flops=0, bytes_accessed=us * 3_000_000, transcendentals=0
        ),
    )(*ins)


def row(ref, *at):
    *lead, r = at
    r_ = ref[(*lead, pl.ds(r, 1), slice(None))]
    return jnp.broadcast_to(r_, (8, r_.shape[-1]))


def up_z(a):
    return pltpu.roll(a, a.shape[-1] - 1, a.ndim - 1)


def down_z(a):
    return pltpu.roll(a, 1, a.ndim - 1)


UP_W = [(0, 5), (0, 6), (0, 7), (1, 6), (1, 7), (2, 6), (2, 7)]
DN_W = [(0, 0), (0, 1), (1, 0), (1, 1), (2, 0), (2, 1)]
NV = H * LY
NXU = K * H + len(UP_W)
NXD = K * H + len(DN_W)
NXB = NV + 2 * len(UP_W)
NYB = H * LX + LX + CX
CELLS = [(1, 1), (1, 2), (2, 1)]
WP = [-2, -1, LX, LX + 1]
CWP = [-3, -2, -1, CX, CX + 1, CX + 2]
NCB = 2 * len(CELLS) + len(WP)


def put_rows(up, down, n, lows, highs):
    up[n, 0:2] = highs[0][6:8]
    up[n, 2:5] = highs[1][5:8]
    up[n, 5:8] = highs[2][5:8]
    down[n, 0:2] = lows[0][0:2]
    down[n, 2:4] = lows[1][0:2]
    down[n, 4:8] = lows[2][0:4]


def put_coarse_rows(up, down, n, arrays):
    for a, w in enumerate(arrays):
        r, z = 4 * (a & 1), 128 * (a >> 1)
        up[n, r : r + 4, z : z + 128] = w[4:8]
        down[n, r : r + 4, z : z + 128] = w[0:4]


def coarse_rows(msg, n, a):
    r, z = 4 * (a & 1), 128 * (a >> 1)
    return msg[n, r : r + 4, z : z + 128]


def x_send(v, wx, wy, wz, xu, xd, bu, bd, sem):
    pairs = []
    for k in range(K):
        pairs.append((v.at[k, LX - H : LX], bu.at[H * k : H * k + H], xu.at[H * k : H * k + H]))
        pairs.append((v.at[k, 0:H], bd.at[H * k : H * k + H], xd.at[H * k : H * k + H]))
    for buf, msg, side in ((bu, xu, UP_W), (bd, xd, DN_W)):
        at = K * H
        for w, ref in enumerate((wx, wy, wz)):
            p = [x for q, x in side if q == w]
            here = slice(at, at + len(p))
            pairs.append((ref.at[p[0] : p[-1] + 1], buf.at[here], msg.at[here]))
            at += len(p)
    n = len(pairs)
    ins = [pltpu.make_async_copy(a, b, sem.at[i]) for i, (a, b, _) in enumerate(pairs)]
    outs = [pltpu.make_async_copy(b, c, sem.at[n + i]) for i, (_, b, c) in enumerate(pairs)]
    for c in ins:
        c.start()
    for i, o in zip(ins, outs):
        i.wait()
        o.start()
    for o in outs:
        o.wait()


def local(v, w_, vt, wm, cw, yu, yd, Q):
    last_x = lax.axis_index("gx") == lax.axis_size("gx") - 1
    last_y = lax.axis_index("gy") == lax.axis_size("gy") - 1
    keep_x = jnp.where(last_x, 0.0, 1.0)
    keep_y = jnp.where(last_y, 0.0, 1.0)
    wm[0] = w_[0]
    wm[0, LX - 1] = w_[0, LX - 1] * keep_x
    sub = lax.broadcasted_iota(jnp.int32, (LX, LY, NZ), 1)
    wm[1] = jnp.where(sub == LY - 1, w_[1] * keep_y, w_[1])
    lane = lax.broadcasted_iota(jnp.int32, (LX, LY, NZ), 2)
    wm[2] = jnp.where(lane == NZ - 1, 0.0, w_[2])

    for x in range(CX):
        i = 2 * x
        wyp = wm[1, i] + wm[1, i + 1]
        wzp = wm[2, i] + wm[2, i + 1]
        parts = (
            (wm[0, i + 1], SUM),
            (wm[0, i], SUM),
            (wyp, SUM),
            (wzp, ODD),
            (wzp, EVEN),
        )
        for q, (a, how) in enumerate(parts):
            Q[q, x * LY : x * LY + 8] = compress(a[0:8], how)
            Q[q, x * LY + 8 : x * LY + 16] = compress(a[8:16], how)
    ri = lax.broadcasted_iota(jnp.int32, (CX * CY, CX * LY), 0)
    ci = lax.broadcasted_iota(jnp.int32, (CX * CY, CX * LY), 1)
    both = jnp.where((ci >> 1) == ri, 1.0, 0.0)
    first = jnp.where(ci == 2 * ri, 1.0, 0.0)
    second = jnp.where(ci == 2 * ri + 1, 1.0, 0.0)

    def rows(m, q):
        return jnp.dot(m, Q[q], precision=lax.Precision.HIGHEST, preferred_element_type=jnp.float32)

    inside = 2.0 * (rows(both, 1) + rows(first, 2) + rows(both, 4))
    for a, w in enumerate((rows(both, 0), rows(second, 2), rows(both, 3), inside)):
        for x in range(CX):
            cw[a, x] = w[x * CY : (x + 1) * CY]

    for x in range(LX):
        put_rows(
            yu,
            yd,
            H * LX + x,
            [wm[w, x, 0:8] for w in range(3)],
            [wm[w, x, 8:16] for w in range(3)],
        )
    for x in range(CX):
        put_coarse_rows(yu, yd, H * LX + LX + x, [cw[a, x] for a in range(4)])

    for x in range(LX):
        for t in range(0, LY, 8):
            vt[x, t : t + 8] = jnp.swapaxes(v[:, x, t : t + 8, :], 0, 1)
    for x in range(LX):
        for d in range(1, H + 1):
            yu[x * H + d - 1] = vt[x, LY - d]
            yd[x * H + d - 1] = vt[x, d - 1]


def x_cell(xl, xr, p, y):
    return xl[(p + H) * LY + y] if p < 0 else xr[(p - LX) * LY + y]


def x_weight(xl, xr, w, p):
    if p < 0:
        at = NV + 2 * UP_W.index((w, p + LX))
        return xl[at], xl[at + 1]
    at = NV + 2 * DN_W.index((w, p - LX))
    return xr[at], xr[at + 1]


def x_receive(rl, rr, after, xl, xr, cu, cd):
    first_x = lax.axis_index("gx") == 0
    last_y = lax.axis_index("gy") == lax.axis_size("gy") - 1
    keep_x = jnp.where(first_x, 0.0, 1.0)
    keep_y = jnp.where(last_y, 0.0, 1.0)
    sub = lax.broadcasted_iota(jnp.int32, (8, NZ), 0)
    lane = lax.broadcasted_iota(jnp.int32, (8, NZ), 1)
    for src, dst, side in ((rl, xl, UP_W), (rr, xr, DN_W)):
        for d in range(H):
            for t in range(0, LY, 8):
                block = jnp.stack([src[H * k + d, t : t + 8] for k in range(K)])
                dst[d * LY + t : d * LY + t + 8] = jnp.swapaxes(block, 0, 1)
        for n, (w, x) in enumerate(side):
            lo, hi = src[K * H + n, 0:8], src[K * H + n, 8:16]
            if w == 0 and x == LX - 1:
                lo, hi = lo * keep_x, hi * keep_x
            if w == 1:
                hi = jnp.where(sub == 7, hi * keep_y, hi)
            if w == 2:
                lo = jnp.where(lane == NZ - 1, 0.0, lo)
                hi = jnp.where(lane == NZ - 1, 0.0, hi)
            dst[NV + 2 * n] = lo
            dst[NV + 2 * n + 1] = hi
    n = 0
    for side in (-1, 1):
        for dx, dy in CELLS:
            p = -dx if side < 0 else LX - 1 + dx
            cu[n] = x_cell(xl, xr, p, LY - dy)
            cd[n] = x_cell(xl, xr, p, dy - 1)
            n += 1
    for p in WP:
        tiles = [x_weight(xl, xr, w, p) for w in range(3)]
        put_rows(cu, cd, n, [t[0] for t in tiles], [t[1] for t in tiles])
        n += 1


SUM, EVEN, ODD = 0, 1, 2


def compress(a, how=SUM):
    lane = lax.broadcasted_iota(jnp.int32, (8, 128), 1)
    t = a + up_z(a) if how == SUM else a
    at = (2 * lane + (1 if how == ODD else 0)) & 127
    lo = jnp.take_along_axis(t[:, :128], at, 1)
    hi = jnp.take_along_axis(t[:, 128:], at, 1)
    return jnp.where(lane < 64, lo, hi)


def expand(a):
    lane = lax.broadcasted_iota(jnp.int32, (8, 128), 1)
    half = lane >> 1
    return jnp.concatenate(
        [jnp.take_along_axis(a, half, 1), jnp.take_along_axis(a, half + 64, 1)], 1
    )


def stencil(w, at, without=None):
    c = at(0, 0)
    total = w(2) * at(0, 1) + w(3) * at(0, -1) + w(4) * up_z(c) + w(5) * down_z(c)
    for a, dx in ((0, 1), (1, -1)):
        if a != without:
            total = total + w(a) * at(dx, 0)
    return total


NH = [-2, -1, 0, 8, 9]
Y1E = [-2, -1, 0, 7, 8, 9]
Y2E = [-1, 0, 1, 6, 7, 8]
Y3E = [0, 1, 2, 5, 6, 7]
LACK = {(1, 7): 0, (2, 1): 1, (2, 6): 0, (3, 2): 1, (3, 5): 0}


def pick(near, edge, planes_):
    first = next(p for p in range(LX) if p not in planes_)

    def cell(p, y):
        if p in planes_:
            return edge[planes_.index(p), y + H]
        return near[p - first, y + H]

    return cell


def v_cell(vt, xl, xr, yl, yr):
    def cell(p, y):
        if not isinstance(p, int) or 0 <= p < LX:
            if y < 0:
                return yl[p * H - y - 1]
            if y >= LY:
                return yr[p * H + y - LY]
            return vt[p, y]
        return x_cell(xl, xr, p, y)

    return cell


def w_row(NW, NE, a, p, y):
    if p in NH:
        return row(NE, a, NH.index(p), y)
    return row(NW, a, p - 1, y + JW)


def normalise(dst, i, wx, lx, wy, ly, wz):
    lz = down_z(wz)
    deg = wx + lx + wy + ly + wz + lz
    inv = 1.0 / deg
    for a, w in enumerate((wx, lx, wy, ly, wz, lz)):
        dst[a, i] = w * inv
    dst[6, i] = deg


def fine_inner(vt, wm, cw, yl, yr, W, NW, Y1, Y2, Y3, PX):
    for w in range(3):
        W[w, :, JW : JW + LY] = wm[w]
    for x in range(LX):
        n = H * LX + x
        W[0, x, JW - 2 : JW] = yl[n, 0:2]
        W[1, x, JW - 3 : JW] = yl[n, 2:5]
        W[2, x, JW - 2 : JW] = yl[n, 6:8]
        W[0, x, JW + LY : JW + LY + 2] = yr[n, 0:2]
        W[1, x, JW + LY : JW + LY + 2] = yr[n, 2:4]
        W[2, x, JW + LY : JW + LY + 2] = yr[n, 4:6]

    def norm(x, _):
        wy = W[1, x]
        normalise(NW, x - 1, W[0, x], W[0, x - 1], wy, pltpu.roll(wy, 1, 0), W[2, x])
        return 0

    lax.fori_loop(1, LX, norm, 0)
    v = v_cell(vt, None, None, yl, yr)

    def power(at, dst, first, count, low, high):
        def body(n, _):
            p = first + n
            for y in range(low, high + 1):
                dst[n, y + H] = stencil(
                    lambda a: row(NW, a, p - 1, y + JW), lambda dx, dy: at(p + dx, y + dy)
                )
            return 0

        lax.fori_loop(0, count, body, 0)

    def y1(p, y):
        return Y1[p - 1, y + H]

    def y2(p, y):
        return Y2[p - 2, y + H]

    power(v, Y1, 1, 6, -2, 17)
    power(y1, Y2, 2, 4, -1, 16)
    power(y2, Y3, 3, 2, 0, 15)
    for n, ((power_, p), without) in enumerate(LACK.items()):
        at = (v, y1, y2)[power_ - 1]
        for y in range(LY):
            PX[n, y] = stencil(
                lambda a: row(NW, a, p - 1, y + JW), lambda dx, dy: at(p + dx, y + dy), without
            )


def fine_outer(vt, wm, cw, xl, xr, yl, yr, W, NW, Y1, Y2, Y3, PX, NE, Y1X, Y2X, Y3X, f, over):
    def own(w, p):
        if 0 <= p < LX:
            return wm[w, p]
        return jnp.concatenate(x_weight(xl, xr, w, p), 0)

    top = lax.broadcasted_iota(jnp.int32, (LY, NZ), 0) == 0
    for n, p in enumerate(NH):
        wy = own(1, p)
        ly = pltpu.roll(wy, 1, 0)
        if p == 0:
            ly = jnp.where(top, jnp.broadcast_to(W[1, 0, JW - 1 : JW], (LY, NZ)), ly)
        normalise(NE, n, own(0, p), own(0, p - 1), wy, ly, own(2, p))

    def power(power_, at, dst, planes_, rows_):
        for n, p in enumerate(planes_):
            low, high = rows_[n if n < 3 else 5 - n]
            lack = LACK.get((power_, p))
            for y in range(low, high + 1):
                if lack is not None:
                    m = list(LACK).index((power_, p))
                    term = w_row(NW, NE, lack, p, y) * at(p + (-1 if lack else 1), y)
                    dst[n, y + H] = PX[m, y] + term
                    continue
                dst[n, y + H] = stencil(
                    lambda a: w_row(NW, NE, a, p, y), lambda dx, dy: at(p + dx, y + dy)
                )

    v = v_cell(vt, xl, xr, yl, yr)
    y1, y2, y3 = pick(Y1, Y1X, Y1E), pick(Y2, Y2X, Y2E), pick(Y3, Y3X, Y3E)
    power(1, v, Y1X, Y1E, ((1, 14), (1, 14), (0, 15)))
    power(2, y1, Y2X, Y2E, ((2, 13), (1, 14), (0, 15)))
    power(3, y2, Y3X, Y3E, ((2, 13), (1, 14), (0, 15)))

    first_row = lax.broadcasted_iota(jnp.int32, (CY, CZ), 0) == 0
    for x in range(CX):
        cx, cy, cz = cw[0, x], cw[1, x], cw[2, x]
        if x:
            lcx = cw[0, x - 1]
        else:
            both = pair_rows()
            flat = jnp.concatenate(
                [compress(t) for t in x_weight(xl, xr, 0, -1)], 0
            )
            lcx = jnp.dot(
                both, flat, precision=lax.Precision.HIGHEST, preferred_element_type=jnp.float32
            )
        edge = coarse_rows(yl, H * LX + LX + x, 1)[3:4]
        lcy = jnp.where(first_row, jnp.broadcast_to(edge, (CY, CZ)), pltpu.roll(cy, 1, 0))
        over[x] = 1.0 / (
            DIAG * (cx + lcx + cy + lcy + cz + down_z(cz)) + SHIFT * cw[3, x]
        )

    for x in range(CX):
        for y in range(CY):
            if x in (0, CX - 1) and y in (0, CY - 1):
                continue
            ra, rb = 0.0, 0.0
            for dx in range(2):
                for dy in range(2):
                    p, q = 2 * x + dx, 2 * y + dy
                    ga, gb = rest(v(p, q), y1(p, q), y2(p, q), y3(p, q))
                    deg = w_row(NW, NE, 6, p, q)
                    ra = ra + deg * ga
                    rb = rb + deg * gb
            inv = row(over, x, y)
            at = 2 * (x * CY + y)
            f[at] = compress(ra) * inv
            f[at + 1] = compress(rb) * inv
    for a in range(4):
        for x in range(CX):
            f[NF + 4 * a + x] = cw[a, x]


NF = 2 * CX * CY


def pair_rows():
    ri = lax.broadcasted_iota(jnp.int32, (CY, LY), 0)
    ci = lax.broadcasted_iota(jnp.int32, (CY, LY), 1)
    return jnp.where((ci >> 1) == ri, 1.0, 0.0)


def rest(v, y1, y2, y3):
    gb = G0 * v + G1 * y1 + G2 * y2
    return gb - (G0 * y1 + G1 * y2 + G2 * y3), gb


def smooth(v, y1, y2, y3):
    b = B0 * v + B1 * y1 + B2 * y2
    return v - (b - (B0 * y1 + B1 * y2 + B2 * y3)), b


def fine_corners(
    vt, xl, xr, yl, yr, W, NW, Y1, Y2, Y3, NE, Y1X, Y2X, Y3X, f_, over, cl, cr, f, fu, fd, fix
):
    f[...] = f_[...]
    old = (
        v_cell(vt, xl, xr, yl, yr),
        pick(Y1, Y1X, Y1E),
        pick(Y2, Y2X, Y2E),
        pick(Y3, Y3X, Y3E),
    )
    for side in range(2):
        for top in range(2):
            msg = cr if top else cl

            def px(dx):
                return LX - 1 + dx if side else -dx

            def py(dy):
                return LY - 1 + dy if top else -dy

            got = {}
            for n, (dx, dy) in enumerate(CELLS):
                got[px(dx), py(dy)] = msg[len(CELLS) * side + n]

            def raw(w, x, y):
                out_x = x < 0 or x >= LX
                out_y = y < 0 or y >= LY
                if out_x and out_y:
                    n = 2 * len(CELLS) + WP.index(x)
                    if top:
                        r = (0, 2, 4)[w] + y - LY
                    else:
                        r = (2, 5, 8)[w] + y
                    return msg[n, r : r + 1]
                if out_x:
                    tile = x_weight(xl, xr, w, x)[y >> 3]
                    return tile[y & 7 : (y & 7) + 1]
                return W[w, x, y + JW : y + JW + 1]

            weights = {}

            def weight(x, y):
                if (x, y) not in weights:
                    wx, lx = raw(0, x, y), raw(0, x - 1, y)
                    wy, ly = raw(1, x, y), raw(1, x, y - 1)
                    wz = raw(2, x, y)
                    ws = (wx, lx, wy, ly, wz, down_z(wz))
                    inv = 1.0 / (wx + lx + wy + ly + wz + ws[5])
                    weights[x, y] = [jnp.broadcast_to(w * inv, (8, NZ)) for w in ws]
                return weights[x, y]

            def look(known, cell):
                def at(x, y):
                    return known[x, y] if (x, y) in known else cell(x, y)

                return at

            def run(at, cells, fresh):
                out = {}
                for dx, dy in cells:
                    x, y = px(dx), py(dy)
                    if fresh(dx, dy):
                        ws = weight(x, y)
                    else:
                        ws = [w_row(NW, NE, a, x, y) for a in range(6)]
                    out[x, y] = stencil(
                        lambda a: ws[a], lambda ex, ey: at(x + ex, y + ey)
                    )
                return out

            def fresh(dx, dy):
                return (dx > 0 and dy >= 0) or (dy > 0 and dx >= 0)

            v = look(got, old[0])
            y1 = look(run(v, [(1, 0), (2, 0), (1, 1), (0, 1), (0, 2)], fresh), old[1])
            y2 = look(run(y1, [(0, 0), (1, 0), (1, -1), (0, 1), (-1, 1)], fresh), old[2])
            y3 = look(run(y2, [(0, 0), (-1, 0), (0, -1)], fresh), old[3])
            ra, rb = 0.0, 0.0
            for n, (dx, dy) in enumerate(((0, 0), (-1, 0), (0, -1), (-1, -1))):
                x, y = px(dx), py(dy)
                four = (v(x, y), y1(x, y), y2(x, y), y3(x, y))
                ga, gb = rest(*four)
                deg = w_row(NW, NE, 6, x, y)
                ra = ra + deg * ga
                rb = rb + deg * gb
                p, b = smooth(*four)
                fix[2 * side + top, n, 0:8] = p
                fix[2 * side + top, n, 8:16] = b
            x, y = (CX - 1) * side, (CY - 1) * top
            inv = row(over, x, y)
            at = 2 * (x * CY + y)
            f[at] = compress(ra) * inv
            f[at + 1] = compress(rb) * inv
    for x in range(CX):
        at = 2 * x * CY
        fd[8 * x : 8 * x + 8] = f[at : at + 8]
        fu[8 * x : 8 * x + 8] = f[at + 8 : at + 16]


def meanwhile(vt, NW, NE, Y1, Y2, Y3, Y1X, Y2X, Y3X, fix, pb, nd):
    y1, y2, y3 = pick(Y1, Y1X, Y1E), pick(Y2, Y2X, Y2E), pick(Y3, Y3X, Y3E)
    num = den = jnp.zeros((8, NZ), jnp.float32)
    corner = {}
    for side in range(2):
        for top in range(2):
            for n, (dx, dy) in enumerate(((0, 0), (-1, 0), (0, -1), (-1, -1))):
                x = LX - 1 + dx if side else -dx
                y = LY - 1 + dy if top else -dy
                corner[x, y] = 2 * side + top, n
    for x in range(LX):
        for y in range(LY):
            v, nv = vt[x, y], y1(x, y)
            if (x, y) in corner:
                pb[x, y] = fix[corner[x, y]]
            else:
                p, b = smooth(v, nv, y2(x, y), y3(x, y))
                pb[x, y, 0:8] = p
                pb[x, y, 8:16] = b
            dv = w_row(NW, NE, 6, x, y) * v
            num = num + dv * (v - nv)
            den = den + dv * v
    nd[0] = num
    nd[1] = den


JC = 8
CCELLS = [(dx, dy) for dx in (1, 2, 3) for dy in range(1, CH + 1 - dx)]


NCC = 4 * len(CCELLS) + 2 * len(CWP)


def coarse_corner_send(left, right, after, yl, yr, cu, cd):
    n = 0
    for side in range(2):
        for dx, dy in CCELLS:
            x = dx - 1 if side else CX - dx
            src = right if side else left
            for half in range(2):
                cu[n] = src[2 * (x * CY + CY - dy) + half]
                cd[n] = src[2 * (x * CY + dy - 1) + half]
                n += 1
    for p in CWP:
        src, x = (left, p + CX) if p < 0 else (right, p - CX)
        for a in range(4):
            w = src[NF + 4 * a + x]
            m, r = n + (a >> 1), 4 * (a & 1)
            cu[m, r : r + 4] = w[4:8]
            cd[m, r : r + 4] = w[0:4]
        n += 2


def beyond(i, j):
    return max(CH - i, i - CH - CX + 1, 0), max(CH - j, j - CH - CY + 1, 0)


def cells_within(radius):
    every = [(i, j) for i in range(CX + 2 * CH) for j in range(CY + 2 * CH)]
    return [c for c in every if sum(beyond(*c)) <= radius]


def early(before, radius):
    out = set()
    for i, j in cells_within(radius):
        dx, dy = beyond(i, j)
        if dx and not CH < j < CH + CY - 1 or dy and not CH < i < CH + CX - 1:
            continue
        if {(i, j), (i + 1, j), (i - 1, j), (i, j + 1), (i, j - 1)} <= before:
            out.add((i, j))
    return out


EARLY0 = {c for c in cells_within(CH) if 0 in beyond(*c)}
EARLY1 = early(EARLY0, 3)
EARLY2 = early(EARLY1, 2)
EARLY3 = early(EARLY2, 1)
BLOCKS = [(x, y) for x in range(CX) for y in range(CY)]
DONE = [
    (x, y)
    for x, y in BLOCKS
    if {(x + CH + i, y + CH + j) for i, j in ((0, 0), (1, 0), (-1, 0), (0, 1), (0, -1))} <= EARLY3
]


def coarse_weights(own, left, right, gl, gr, corner, CW, R):
    for a in range(4):
        for i in range(CX + 2 * CH):
            p = i - CH
            src, x = (left, p + CX) if p < 0 else (own, p) if p < CX else (right, p - CX)
            R[a, i, JC : JC + CY] = src[NF + 4 * a + x]
            if 0 <= p < CX:
                lo = coarse_rows(gl, H * LX + LX + p, a)
                hi = coarse_rows(gr, H * LX + LX + p, a)
            elif corner and p in CWP:
                m, r = 4 * len(CCELLS) + 2 * CWP.index(p) + (a >> 1), 4 * (a & 1)
                lo, hi = corner[0][m, r : r + 4], corner[1][m, r : r + 4]
            else:
                continue
            R[a, i, JC - 4 : JC] = lo
            R[a, i, JC + CY : JC + CY + 4] = hi
    for i in range(1, CX + 2 * CH - 1):
        cx, lcx, cy, cz = R[0, i], R[0, i - 1], R[1, i], R[2, i]
        ws = (cx, lcx, cy, pltpu.roll(cy, 1, 0), cz, down_z(cz))
        total = ws[0] + ws[1] + ws[2] + ws[3] + ws[4] + ws[5]
        inv = OMEGA / (DIAG * total + SHIFT * R[3, i])
        for a in range(6):
            CW[a, i] = ws[a] * inv


def sweep(cells, at, f, CW, dst):
    for i, j in cells:
        ws = [row(CW, a, i, j - CH + JC) for a in range(6)]
        for half in range(2):
            c = at(i, j, half)
            dst[i, j, half] = (
                (1.0 - OMEGA) * c
                + f(i, j, half)
                + ws[0] * at(i + 1, j, half)
                + ws[1] * at(i - 1, j, half)
                + ws[2] * at(i, j + 1, half)
                + ws[3] * at(i, j - 1, half)
                + ws[4] * up_z(c)
                + ws[5] * down_z(c)
            )


def last_sweep(blocks, cell, pb, NW, NE, po, bo):
    for x, y in blocks:
        for half in range(2):
            e = cell(x + CH, y + CH, half)
            ez = (up_z(e), down_z(e))
            ke = KEEP * e
            ce = C * e
            for dx in range(2):
                ex = C * cell(x + CH + 2 * dx - 1, y + CH, half)
                for dy in range(2):
                    ey = C * cell(x + CH, y + CH + 2 * dy - 1, half)
                    xx, yy = 2 * x + dx, 2 * y + dy
                    nw = [w_row(NW, NE, a, xx, yy) for a in range(6)]
                    s = (
                        ke
                        + (nw[dx] + nw[2 + dy]) * ce
                        + nw[1 - dx] * ex
                        + nw[3 - dy] * ey
                        + C * (nw[4] * ez[0] + nw[5] * ez[1])
                    )
                    if half == 0:
                        po[xx, yy] = pb[xx, yy, 0:8] - s
                    else:
                        bo[xx, yy] = pb[xx, yy, 8:16] + s


def row8(ref, x, y, m, z):
    return jnp.broadcast_to(ref[x, y, m : m + 1, z], (8, 128))


def add_gram(blocks, acc, po, bo, NW, NE):
    for x, y in blocks:
        for n in range(4):
            xx, yy = 2 * x + (n >> 1), 2 * y + (n & 1)
            deg = w_row(NW, NE, 6, xx, yy)
            for h in range(0, NZ, 128):
                z = slice(h, h + 128)
                p = po[xx, yy, :, z]
                b = bo[xx, yy, :, z]
                dp = deg[:, z] * p
                db = deg[:, z] * b
                for m in range(8):
                    acc[m] = acc[m] + dp * row8(po, xx, yy, m, z)
                    acc[13 + m] = acc[13 + m] + dp * row8(bo, xx, yy, m, z)
                for s in range(5):
                    acc[8 + s] = acc[8 + s] + b * (pltpu.roll(db, s, 0) if s else db)


def coarse_early(
    own, left, right, yl, yr, gl, gr, pb, NW, NE, F, E1, E2, EX, po, bo, g, E3, CW, R
):
    for x in range(CX):
        for half in range(2):
            for y in range(CY):
                at = 2 * (x * CY + y) + half
                F[x, y + CH, half] = OMEGA * left[at]
                F[x + CH, y + CH, half] = OMEGA * own[at]
                F[x + CH + CX, y + CH, half] = OMEGA * right[at]
            for y in range(CH):
                F[x + CH, y, half] = OMEGA * yl[2 * (x * CH + y) + half]
                F[x + CH, y + CH + CY, half] = OMEGA * yr[2 * (x * CH + y) + half]
    coarse_weights(own, left, right, gl, gr, None, CW, R)

    def of(ref):
        return lambda i, j, half: ref[i, j, half]

    sweep(sorted(EARLY1), of(F), of(F), CW, E1)
    sweep(sorted(EARLY2), of(E1), of(F), CW, E2)
    sweep(sorted(EARLY3), of(E2), of(F), CW, E3)
    for i, j in sorted(EARLY3):
        for half in range(2):
            EX[i, j, half] = expand(E3[i, j, half])
    last_sweep(DONE, of(EX), pb, NW, NE, po, bo)
    acc = [jnp.zeros((8, 128), jnp.float32)] * 21
    add_gram(DONE, acc, po, bo, NW, NE)
    for n in range(21):
        g[n] = acc[n]


def coarse_level(
    own,
    left,
    right,
    cl,
    cr,
    gl,
    gr,
    F,
    E1,
    E2,
    EXE,
    pe,
    be,
    ge,
    pb,
    NW,
    NE,
    nd,
    po,
    bo,
    mine,
    other,
    X1,
    X2,
    X3,
    EX,
    CW,
    R,
):
    coarse_weights(own, left, right, gl, gr, (cl, cr), CW, R)
    corner = {}
    n = 0
    for side in range(2):
        for dx, dy in CCELLS:
            i = CH + CX - 1 + dx if side else CH - dx
            for half in range(2):
                corner[i, CH - dy, half] = cl, n
                corner[i, CH + CY - 1 + dy, half] = cr, n
                n += 1

    def f(i, j, half):
        if (i, j, half) in corner:
            msg, n = corner[i, j, half]
            return OMEGA * msg[n]
        return F[i, j, half]

    def both(first, cells, then):
        return lambda i, j, half: (first if (i, j) in cells else then)[i, j, half]

    e1, e2 = both(E1, EARLY1, X1), both(E2, EARLY2, X2)
    sweep([c for c in cells_within(3) if c not in EARLY1], f, f, CW, X1)
    sweep([c for c in cells_within(2) if c not in EARLY2], e1, f, CW, X2)
    sweep([c for c in cells_within(1) if c not in EARLY3], e2, f, CW, X3)
    for i, j in cells_within(1):
        if (i, j) not in EARLY3:
            for half in range(2):
                EX[i, j, half] = expand(X3[i, j, half])
    for x, y in DONE:
        here = slice(2 * x, 2 * x + 2), slice(2 * y, 2 * y + 2)
        po[here] = pe[here]
        bo[here] = be[here]
    left_over = [c for c in BLOCKS if c not in DONE]
    last_sweep(left_over, both(EXE, EARLY3, EX), pb, NW, NE, po, bo)
    zero = jnp.zeros((8, 128), jnp.float32)
    acc = [ge[n] for n in range(21)]
    add_gram(left_over, acc, po, bo, NW, NE)
    for q in range(2):
        acc.append(nd[q, :, :128] + nd[q, :, 128:])
    lane = lax.broadcasted_iota(jnp.int32, (8, 128), 1)
    sub = lax.broadcasted_iota(jnp.int32, (8, 128), 0)

    def collect(blocks):
        x = zero
        for n, a in enumerate(blocks):
            total = jnp.broadcast_to(jnp.sum(a, axis=1, keepdims=True), (8, 128))
            x = x + jnp.where(lane == 8 * n + sub, total, 0.0)
        return jnp.sum(x, axis=0, keepdims=True)

    t0 = collect(acc[:16])
    t1 = collect(acc[16:])
    even = lax.axis_index("gy") % 2 == 0
    mine[...] = jnp.where(even, t0, t1)
    other[...] = jnp.where(even, t1, t0)


def spread_sums(a, b, out):
    out[...] = jnp.broadcast_to((a[...] + b[...])[None], out.shape)


def finish(parts, po, bo, out, eig, SP):
    t = parts[...]
    n = t.shape[0]
    while n > 2:
        n //= 2
        t = t[:n] + t[n:]
    t = t[:, 0]
    lams = t[1:2] / pltpu.roll(t[1:2], 120, 1)
    eig[...] = pltpu.roll(lams, 88, 1)[:, :K]
    half = [jnp.broadcast_to(t[q : q + 1], (8, 128)) for q in range(2)]

    def entry(block, k):
        at = 8 * (block % 16) + k
        return jnp.broadcast_to(half[block // 16][:, at : at + 1], (8, 128))

    def sym(a, b):
        s = (a - b) % 8
        return entry(8 + s, a) if s < 5 else entry(16 - s, b)

    def cross(a, b):
        return entry(13 + b, a)

    lam = [entry(21, k) / entry(22, k) for k in range(K)]
    voxels = LX * LY * NZ * lax.axis_size("gx") * lax.axis_size("gy")
    g = {}
    for a in range(K):
        for b in range(a + 1):
            g[a, b] = (
                entry(b, a) + lam[b] * cross(a, b) + lam[a] * (cross(b, a) + lam[b] * sym(a, b))
            ) * (1.0 / voxels)
    low, inv = {}, []
    for j in range(K):
        d = g[j, j]
        r = lax.rsqrt(d)
        r = r * (1.5 - 0.5 * d * r * r)
        inv.append(r)
        for a in range(j + 1, K):
            low[a, j] = g[a, j] * r
        for a in range(j + 1, K):
            for b in range(j + 1, a + 1):
                g[a, b] = g[a, b] - low[a, j] * low[b, j]

    sub = lax.broadcasted_iota(jnp.int32, (8, 128), 0)
    lam_rows = jnp.zeros((8, 128), jnp.float32)
    for k in range(K):
        lam_rows = jnp.where(sub == k, lam[k], lam_rows)
        SP[64 + 8 * k : 72 + 8 * k] = inv[k]
    at = {}
    for n, (a, b) in enumerate(sorted(low)):
        at[a, b] = 128 + 8 * n
        SP[128 + 8 * n : 136 + 8 * n] = low[a, b]

    def body(x, _):
        for t in range(0, LY, 8):
            for h in range(0, NZ, 128):
                z = slice(h, h + 128)
                upd = po[x, t : t + 8, :, z] + lam_rows[None] * bo[x, t : t + 8, :, z]
                upd = jnp.swapaxes(upd, 0, 1)
                done = []
                for k in range(K):
                    u = upd[k]
                    for j in range(k):
                        u = u - SP[at[k, j] : at[k, j] + 8] * done[j]
                    u = u * SP[64 + 8 * k : 72 + 8 * k]
                    done.append(u)
                    out[k, x, t : t + 8, z] = u
        return 0

    lax.fori_loop(0, LX, body, 0)


def both_ways(up, down, axis):
    n = lax.axis_size(axis)
    fwd = [(i, (i + 1) % n) for i in range(n)]
    back = [((i + 1) % n, i) for i in range(n)]
    return lax.ppermute(up, axis, fwd), lax.ppermute(down, axis, back)


def per_device(vectors, weight_x, weight_y, weight_z):
    args = (vectors, weight_x, weight_y, weight_z)
    xu, xd = call(
        x_send,
        [(NXU, LY, NZ), (NXD, LY, NZ)],
        args,
        [(NXU, LY, NZ), (NXD, LY, NZ), pltpu.SemaphoreType.DMA((4 * K + 12,))],
        limit=56,
        where=ANY,
    )
    rl, rr = both_ways(xu, xd, "gx")
    vt, wm, cw, yu, yd = call(
        local,
        [
            (LX, LY, K, NZ),
            (3, LX, LY, NZ),
            (4, CX, CY, CZ),
            (NYB, 8, NZ),
            (NYB, 8, NZ),
        ],
        (vectors, jnp.stack(args[1:])),
        [(5, CX * LY, CZ)],
    )
    yl, yr = both_ways(yu, yd, "gy")
    tall = LY + 2 * H
    W, NW, Y1, Y2, Y3, PX = call(
        fine_inner,
        [
            (3, LX, 32, NZ),
            (7, LX - 1, 32, NZ),
            (6, tall, K, NZ),
            (4, tall, K, NZ),
            (2, tall, K, NZ),
            (len(LACK), LY, K, NZ),
        ],
        (vt, wm, cw, yl, yr),
        us=3,
    )
    xl, xr, cu, cd = call(
        x_receive, [(NXB, 8, NZ), (NXB, 8, NZ), (NCB, 8, NZ), (NCB, 8, NZ)], (rl, rr, Y3)
    )
    cl, cr = both_ways(cu, cd, "gy")
    NE, Y1X, Y2X, Y3X, f, over = call(
        fine_outer,
        [
            (7, len(NH), LY, NZ),
            (6, tall, K, NZ),
            (6, tall, K, NZ),
            (6, tall, K, NZ),
            (NF + 4 * CX, 8, CZ),
            (CX, CY, CZ),
        ],
        (vt, wm, cw, xl, xr, yl, yr, W, NW, Y1, Y2, Y3, PX),
        us=4,
    )
    f, fu, fd, fix = call(
        fine_corners,
        [(NF + 4 * CX, 8, CZ), (NF // 2, 8, CZ), (NF // 2, 8, CZ), (4, 4, 16, NZ)],
        (vt, xl, xr, yl, yr, W, NW, Y1, Y2, Y3, NE, Y1X, Y2X, Y3X, f, over, cl, cr),
    )
    left, right = both_ways(f, f, "gx")
    fl, fr = both_ways(fu, fd, "gy")
    pb, nd = call(
        meanwhile,
        [(LX, LY, 16, NZ), (2, 8, NZ)],
        (vt, NW, NE, Y1, Y2, Y3, Y1X, Y2X, Y3X, fix),
    )
    cu, cd = call(coarse_corner_send, [(NCC, 8, CZ)] * 2, (left, right, nd, fl, fr))
    cl, cr = both_ways(cu, cd, "gy")
    cext = (CX + 2 * CH, CY + 2 * CH, 2, 8, CZ)
    weights = [(6, CX + 2 * CH, 24, CZ), (4, CX + 2 * CH, 24, CZ)]
    early_ = call(
        coarse_early,
        [cext] * 3
        + [(CX + 2 * CH, CY + 2 * CH, 2, 8, NZ), (LX, LY, K, NZ), (LX, LY, K, NZ), (21, 8, 128)],
        (f, left, right, fl, fr, yl, yr, pb, NW, NE),
        [cext] + weights,
        us=2,
    )
    po, bo, mine, other = call(
        coarse_level,
        [(LX, LY, K, NZ), (LX, LY, K, NZ), (1, 128), (1, 128)],
        (f, left, right, cl, cr, yl, yr, *early_, pb, NW, NE, nd),
        [cext, cext, cext, (CX + 2 * CH, CY + 2 * CH, 2, 8, NZ)] + weights,
        limit=12,
    )
    n = lax.axis_size("gy")
    theirs = lax.ppermute(other, "gy", [(i, i ^ 1) for i in range(n)])
    (sums,) = call(spread_sums, [(n * lax.axis_size("gx"), 1, 128)], (mine, theirs))
    parts = lax.all_to_all(sums, ("gx", "gy"), 0, 0)
    refined, eig = call(
        finish,
        [(K, LX, LY, NZ), (1, K)],
        (parts, po, bo),
        [(384, 128)],
    )
    return refined, eig.reshape(K)


def solution(mesh):
    return jax.shard_map(
        per_device,
        mesh=mesh,
        in_specs=(
            P(None, "gx", "gy", None),
            P("gx", "gy", None),
            P("gx", "gy", None),
            P("gx", "gy", None),
        ),
        out_specs=(P(None, "gx", "gy", None), P()),
        check_vma=False,
    )
```

```python
import jax
import jax.numpy as jnp
from jax import lax
from jax.experimental import pallas as pl
from jax.experimental.pallas import tpu as pltpu
from jax.sharding import PartitionSpec as P

OMEGA = 0.8
SHIFT = 0.1
DIAG = 1.0 + SHIFT
C = OMEGA / DIAG
Z0 = 2.0 * C - DIAG * C * C
Z1 = C * C
G0, G1, G2 = 1.0 - DIAG * Z0, Z0 - DIAG * Z1, Z1
KEEP = 1.0 - DIAG * C
B0, B1, B2 = KEEP * Z0 + C, KEEP * Z1 + C * Z0, C * Z1

K = 8
LX, LY, NZ = 8, 16, 256
CX, CY, CZ = LX // 2, LY // 2, NZ // 2
H = 3
CH = 4
JW = 8
MIB = 1024 * 1024
VMEM = pl.BlockSpec(memory_space=pltpu.VMEM)


ANY = pl.BlockSpec(memory_space=pl.ANY)


def call(body, outs, ins, scratch=(), limit=8, where=VMEM, us=1):
    return pl.pallas_call(
        body,
        out_shape=[jax.ShapeDtypeStruct(s, jnp.float32) for s in outs],
        in_specs=[where] * len(ins),
        out_specs=[where] * len(outs),
        scratch_shapes=[pltpu.VMEM(s, jnp.float32) if isinstance(s, tuple) else s for s in scratch],
        compiler_params=pltpu.CompilerParams(vmem_limit_bytes=limit * MIB),
        cost_estimate=pl.CostEstimate(
            flops=0, bytes_accessed=us * 3_000_000, transcendentals=0
        ),
    )(*ins)


def row(ref, *at):
    *lead, r = at
    r_ = ref[(*lead, pl.ds(r, 1), slice(None))]
    return jnp.broadcast_to(r_, (8, r_.shape[-1]))


def up_z(a):
    return pltpu.roll(a, a.shape[-1] - 1, a.ndim - 1)


def down_z(a):
    return pltpu.roll(a, 1, a.ndim - 1)


UP_W = [(0, 5), (0, 6), (0, 7), (1, 6), (1, 7), (2, 6), (2, 7)]
DN_W = [(0, 0), (0, 1), (1, 0), (1, 1), (2, 0), (2, 1)]
NV = H * LY
NXU = K * H + len(UP_W)
NXD = K * H + len(DN_W)
NXB = NV + 2 * len(UP_W)
NYB = H * LX + LX + CX
CELLS = [(1, 1), (1, 2), (2, 1)]
WP = [-2, -1, LX, LX + 1]
CWP = [-3, -2, -1, CX, CX + 1, CX + 2]
NCB = 2 * len(CELLS) + len(WP)


def put_rows(up, down, n, lows, highs):
    up[n, 0:2] = highs[0][6:8]
    up[n, 2:5] = highs[1][5:8]
    up[n, 5:8] = highs[2][5:8]
    down[n, 0:2] = lows[0][0:2]
    down[n, 2:4] = lows[1][0:2]
    down[n, 4:8] = lows[2][0:4]


def put_coarse_rows(up, down, n, arrays):
    for a, w in enumerate(arrays):
        r, z = 4 * (a & 1), 128 * (a >> 1)
        up[n, r : r + 4, z : z + 128] = w[4:8]
        down[n, r : r + 4, z : z + 128] = w[0:4]


def coarse_rows(msg, n, a):
    r, z = 4 * (a & 1), 128 * (a >> 1)
    return msg[n, r : r + 4, z : z + 128]


def x_send(v, wx, wy, wz, xu, xd, bu, bd, sem):
    pairs = []
    for k in range(K):
        pairs.append((v.at[k, LX - H : LX], bu.at[H * k : H * k + H], xu.at[H * k : H * k + H]))
        pairs.append((v.at[k, 0:H], bd.at[H * k : H * k + H], xd.at[H * k : H * k + H]))
    for buf, msg, side in ((bu, xu, UP_W), (bd, xd, DN_W)):
        at = K * H
        for w, ref in enumerate((wx, wy, wz)):
            p = [x for q, x in side if q == w]
            here = slice(at, at + len(p))
            pairs.append((ref.at[p[0] : p[-1] + 1], buf.at[here], msg.at[here]))
            at += len(p)
    n = len(pairs)
    ins = [pltpu.make_async_copy(a, b, sem.at[i]) for i, (a, b, _) in enumerate(pairs)]
    outs = [pltpu.make_async_copy(b, c, sem.at[n + i]) for i, (_, b, c) in enumerate(pairs)]
    for c in ins:
        c.start()
    for i, o in zip(ins, outs):
        i.wait()
        o.start()
    for o in outs:
        o.wait()


def local(v, w_, vt, wm, cw, yu, yd, Q):
    last_x = lax.axis_index("gx") == lax.axis_size("gx") - 1
    last_y = lax.axis_index("gy") == lax.axis_size("gy") - 1
    keep_x = jnp.where(last_x, 0.0, 1.0)
    keep_y = jnp.where(last_y, 0.0, 1.0)
    wm[0] = w_[0]
    wm[0, LX - 1] = w_[0, LX - 1] * keep_x
    sub = lax.broadcasted_iota(jnp.int32, (LX, LY, NZ), 1)
    wm[1] = jnp.where(sub == LY - 1, w_[1] * keep_y, w_[1])
    lane = lax.broadcasted_iota(jnp.int32, (LX, LY, NZ), 2)
    wm[2] = jnp.where(lane == NZ - 1, 0.0, w_[2])

    for x in range(CX):
        i = 2 * x
        wyp = wm[1, i] + wm[1, i + 1]
        wzp = wm[2, i] + wm[2, i + 1]
        parts = (
            (wm[0, i + 1], SUM),
            (wm[0, i], SUM),
            (wyp, SUM),
            (wzp, ODD),
            (wzp, EVEN),
        )
        for q, (a, how) in enumerate(parts):
            Q[q, x * LY : x * LY + 8] = compress(a[0:8], how)
            Q[q, x * LY + 8 : x * LY + 16] = compress(a[8:16], how)
    ri = lax.broadcasted_iota(jnp.int32, (CX * CY, CX * LY), 0)
    ci = lax.broadcasted_iota(jnp.int32, (CX * CY, CX * LY), 1)
    both = jnp.where((ci >> 1) == ri, 1.0, 0.0)
    first = jnp.where(ci == 2 * ri, 1.0, 0.0)
    second = jnp.where(ci == 2 * ri + 1, 1.0, 0.0)

    def rows(m, q):
        return jnp.dot(m, Q[q], precision=lax.Precision.HIGHEST, preferred_element_type=jnp.float32)

    inside = 2.0 * (rows(both, 1) + rows(first, 2) + rows(both, 4))
    for a, w in enumerate((rows(both, 0), rows(second, 2), rows(both, 3), inside)):
        for x in range(CX):
            cw[a, x] = w[x * CY : (x + 1) * CY]

    for x in range(LX):
        put_rows(
            yu,
            yd,
            H * LX + x,
            [wm[w, x, 0:8] for w in range(3)],
            [wm[w, x, 8:16] for w in range(3)],
        )
    for x in range(CX):
        put_coarse_rows(yu, yd, H * LX + LX + x, [cw[a, x] for a in range(4)])

    for x in range(LX):
        for t in range(0, LY, 8):
            vt[x, t : t + 8] = jnp.swapaxes(v[:, x, t : t + 8, :], 0, 1)
    for x in range(LX):
        for d in range(1, H + 1):
            yu[x * H + d - 1] = vt[x, LY - d]
            yd[x * H + d - 1] = vt[x, d - 1]


def x_cell(xl, xr, p, y):
    return xl[(p + H) * LY + y] if p < 0 else xr[(p - LX) * LY + y]


def x_weight(xl, xr, w, p):
    if p < 0:
        at = NV + 2 * UP_W.index((w, p + LX))
        return xl[at], xl[at + 1]
    at = NV + 2 * DN_W.index((w, p - LX))
    return xr[at], xr[at + 1]


def x_receive(rl, rr, after, xl, xr, cu, cd):
    first_x = lax.axis_index("gx") == 0
    last_y = lax.axis_index("gy") == lax.axis_size("gy") - 1
    keep_x = jnp.where(first_x, 0.0, 1.0)
    keep_y = jnp.where(last_y, 0.0, 1.0)
    sub = lax.broadcasted_iota(jnp.int32, (8, NZ), 0)
    lane = lax.broadcasted_iota(jnp.int32, (8, NZ), 1)
    for src, dst, side in ((rl, xl, UP_W), (rr, xr, DN_W)):
        for d in range(H):
            for t in range(0, LY, 8):
                block = jnp.stack([src[H * k + d, t : t + 8] for k in range(K)])
                dst[d * LY + t : d * LY + t + 8] = jnp.swapaxes(block, 0, 1)
        for n, (w, x) in enumerate(side):
            lo, hi = src[K * H + n, 0:8], src[K * H + n, 8:16]
            if w == 0 and x == LX - 1:
                lo, hi = lo * keep_x, hi * keep_x
            if w == 1:
                hi = jnp.where(sub == 7, hi * keep_y, hi)
            if w == 2:
                lo = jnp.where(lane == NZ - 1, 0.0, lo)
                hi = jnp.where(lane == NZ - 1, 0.0, hi)
            dst[NV + 2 * n] = lo
            dst[NV + 2 * n + 1] = hi
    n = 0
    for side in (-1, 1):
        for dx, dy in CELLS:
            p = -dx if side < 0 else LX - 1 + dx
            cu[n] = x_cell(xl, xr, p, LY - dy)
            cd[n] = x_cell(xl, xr, p, dy - 1)
            n += 1
    for p in WP:
        tiles = [x_weight(xl, xr, w, p) for w in range(3)]
        put_rows(cu, cd, n, [t[0] for t in tiles], [t[1] for t in tiles])
        n += 1


SUM, EVEN, ODD = 0, 1, 2


def compress(a, how=SUM):
    lane = lax.broadcasted_iota(jnp.int32, (8, 128), 1)
    t = a + up_z(a) if how == SUM else a
    at = (2 * lane + (1 if how == ODD else 0)) & 127
    lo = jnp.take_along_axis(t[:, :128], at, 1)
    hi = jnp.take_along_axis(t[:, 128:], at, 1)
    return jnp.where(lane < 64, lo, hi)


def expand(a):
    lane = lax.broadcasted_iota(jnp.int32, (8, 128), 1)
    half = lane >> 1
    return jnp.concatenate(
        [jnp.take_along_axis(a, half, 1), jnp.take_along_axis(a, half + 64, 1)], 1
    )


def stencil(w, at, without=None):
    c = at(0, 0)
    total = w(2) * at(0, 1) + w(3) * at(0, -1) + w(4) * up_z(c) + w(5) * down_z(c)
    for a, dx in ((0, 1), (1, -1)):
        if a != without:
            total = total + w(a) * at(dx, 0)
    return total


NH = [-2, -1, 0, 8, 9]
Y1E = [-2, -1, 0, 7, 8, 9]
Y2E = [-1, 0, 1, 6, 7, 8]
Y3E = [0, 1, 2, 5, 6, 7]
LACK = {(1, 7): 0, (2, 1): 1, (2, 6): 0, (3, 2): 1, (3, 5): 0}


def pick(near, edge, planes_):
    first = next(p for p in range(LX) if p not in planes_)

    def cell(p, y):
        if p in planes_:
            return edge[planes_.index(p), y + H]
        return near[p - first, y + H]

    return cell


def v_cell(vt, xl, xr, yl, yr):
    def cell(p, y):
        if not isinstance(p, int) or 0 <= p < LX:
            if y < 0:
                return yl[p * H - y - 1]
            if y >= LY:
                return yr[p * H + y - LY]
            return vt[p, y]
        return x_cell(xl, xr, p, y)

    return cell


def w_row(NW, NE, a, p, y):
    if p in NH:
        return row(NE, a, NH.index(p), y)
    return row(NW, a, p - 1, y + JW)


def normalise(dst, i, wx, lx, wy, ly, wz):
    lz = down_z(wz)
    deg = wx + lx + wy + ly + wz + lz
    inv = 1.0 / deg
    for a, w in enumerate((wx, lx, wy, ly, wz, lz)):
        dst[a, i] = w * inv
    dst[6, i] = deg


def fine_inner(vt, wm, cw, yl, yr, W, NW, Y1, Y2, Y3, PX):
    for w in range(3):
        W[w, :, JW : JW + LY] = wm[w]
    for x in range(LX):
        n = H * LX + x
        W[0, x, JW - 2 : JW] = yl[n, 0:2]
        W[1, x, JW - 3 : JW] = yl[n, 2:5]
        W[2, x, JW - 2 : JW] = yl[n, 6:8]
        W[0, x, JW + LY : JW + LY + 2] = yr[n, 0:2]
        W[1, x, JW + LY : JW + LY + 2] = yr[n, 2:4]
        W[2, x, JW + LY : JW + LY + 2] = yr[n, 4:6]

    def norm(x, _):
        wy = W[1, x]
        normalise(NW, x - 1, W[0, x], W[0, x - 1], wy, pltpu.roll(wy, 1, 0), W[2, x])
        return 0

    lax.fori_loop(1, LX, norm, 0)
    v = v_cell(vt, None, None, yl, yr)

    def power(at, dst, first, count, low, high):
        def body(n, _):
            p = first + n
            for y in range(low, high + 1):
                dst[n, y + H] = stencil(
                    lambda a: row(NW, a, p - 1, y + JW), lambda dx, dy: at(p + dx, y + dy)
                )
            return 0

        lax.fori_loop(0, count, body, 0)

    def y1(p, y):
        return Y1[p - 1, y + H]

    def y2(p, y):
        return Y2[p - 2, y + H]

    power(v, Y1, 1, 6, -2, 17)
    power(y1, Y2, 2, 4, -1, 16)
    power(y2, Y3, 3, 2, 0, 15)
    for n, ((power_, p), without) in enumerate(LACK.items()):
        at = (v, y1, y2)[power_ - 1]
        for y in range(LY):
            PX[n, y] = stencil(
                lambda a: row(NW, a, p - 1, y + JW), lambda dx, dy: at(p + dx, y + dy), without
            )


def fine_outer(vt, wm, cw, xl, xr, yl, yr, W, NW, Y1, Y2, Y3, PX, NE, Y1X, Y2X, Y3X, f, over):
    def own(w, p):
        if 0 <= p < LX:
            return wm[w, p]
        return jnp.concatenate(x_weight(xl, xr, w, p), 0)

    top = lax.broadcasted_iota(jnp.int32, (LY, NZ), 0) == 0
    for n, p in enumerate(NH):
        wy = own(1, p)
        ly = pltpu.roll(wy, 1, 0)
        if p == 0:
            ly = jnp.where(top, jnp.broadcast_to(W[1, 0, JW - 1 : JW], (LY, NZ)), ly)
        normalise(NE, n, own(0, p), own(0, p - 1), wy, ly, own(2, p))

    def power(power_, at, dst, planes_, rows_):
        for n, p in enumerate(planes_):
            low, high = rows_[n if n < 3 else 5 - n]
            lack = LACK.get((power_, p))
            for y in range(low, high + 1):
                if lack is not None:
                    m = list(LACK).index((power_, p))
                    term = w_row(NW, NE, lack, p, y) * at(p + (-1 if lack else 1), y)
                    dst[n, y + H] = PX[m, y] + term
                    continue
                dst[n, y + H] = stencil(
                    lambda a: w_row(NW, NE, a, p, y), lambda dx, dy: at(p + dx, y + dy)
                )

    v = v_cell(vt, xl, xr, yl, yr)
    y1, y2, y3 = pick(Y1, Y1X, Y1E), pick(Y2, Y2X, Y2E), pick(Y3, Y3X, Y3E)
    power(1, v, Y1X, Y1E, ((1, 14), (1, 14), (0, 15)))
    power(2, y1, Y2X, Y2E, ((2, 13), (1, 14), (0, 15)))
    power(3, y2, Y3X, Y3E, ((2, 13), (1, 14), (0, 15)))

    first_row = lax.broadcasted_iota(jnp.int32, (CY, CZ), 0) == 0
    for x in range(CX):
        cx, cy, cz = cw[0, x], cw[1, x], cw[2, x]
        if x:
            lcx = cw[0, x - 1]
        else:
            both = pair_rows()
            flat = jnp.concatenate(
                [compress(t) for t in x_weight(xl, xr, 0, -1)], 0
            )
            lcx = jnp.dot(
                both, flat, precision=lax.Precision.HIGHEST, preferred_element_type=jnp.float32
            )
        edge = coarse_rows(yl, H * LX + LX + x, 1)[3:4]
        lcy = jnp.where(first_row, jnp.broadcast_to(edge, (CY, CZ)), pltpu.roll(cy, 1, 0))
        over[x] = 1.0 / (
            DIAG * (cx + lcx + cy + lcy + cz + down_z(cz)) + SHIFT * cw[3, x]
        )

    for x in range(CX):
        for y in range(CY):
            if x in (0, CX - 1) and y in (0, CY - 1):
                continue
            ra, rb = 0.0, 0.0
            for dx in range(2):
                for dy in range(2):
                    p, q = 2 * x + dx, 2 * y + dy
                    ga, gb = rest(v(p, q), y1(p, q), y2(p, q), y3(p, q))
                    deg = w_row(NW, NE, 6, p, q)
                    ra = ra + deg * ga
                    rb = rb + deg * gb
            inv = row(over, x, y)
            at = 2 * (x * CY + y)
            f[at] = compress(ra) * inv
            f[at + 1] = compress(rb) * inv
    for a in range(4):
        for x in range(CX):
            f[NF + 4 * a + x] = cw[a, x]


NF = 2 * CX * CY


def pair_rows():
    ri = lax.broadcasted_iota(jnp.int32, (CY, LY), 0)
    ci = lax.broadcasted_iota(jnp.int32, (CY, LY), 1)
    return jnp.where((ci >> 1) == ri, 1.0, 0.0)


def rest(v, y1, y2, y3):
    gb = G0 * v + G1 * y1 + G2 * y2
    return gb - (G0 * y1 + G1 * y2 + G2 * y3), gb


def smooth(v, y1, y2, y3):
    b = B0 * v + B1 * y1 + B2 * y2
    return v - (b - (B0 * y1 + B1 * y2 + B2 * y3)), b


def fine_corners(
    vt, xl, xr, yl, yr, W, NW, Y1, Y2, Y3, NE, Y1X, Y2X, Y3X, f_, over, cl, cr, f, fu, fd, fix
):
    f[...] = f_[...]
    old = (
        v_cell(vt, xl, xr, yl, yr),
        pick(Y1, Y1X, Y1E),
        pick(Y2, Y2X, Y2E),
        pick(Y3, Y3X, Y3E),
    )
    for side in range(2):
        for top in range(2):
            msg = cr if top else cl

            def px(dx):
                return LX - 1 + dx if side else -dx

            def py(dy):
                return LY - 1 + dy if top else -dy

            got = {}
            for n, (dx, dy) in enumerate(CELLS):
                got[px(dx), py(dy)] = msg[len(CELLS) * side + n]

            def raw(w, x, y):
                out_x = x < 0 or x >= LX
                out_y = y < 0 or y >= LY
                if out_x and out_y:
                    n = 2 * len(CELLS) + WP.index(x)
                    if top:
                        r = (0, 2, 4)[w] + y - LY
                    else:
                        r = (2, 5, 8)[w] + y
                    return msg[n, r : r + 1]
                if out_x:
                    tile = x_weight(xl, xr, w, x)[y >> 3]
                    return tile[y & 7 : (y & 7) + 1]
                return W[w, x, y + JW : y + JW + 1]

            weights = {}

            def weight(x, y):
                if (x, y) not in weights:
                    wx, lx = raw(0, x, y), raw(0, x - 1, y)
                    wy, ly = raw(1, x, y), raw(1, x, y - 1)
                    wz = raw(2, x, y)
                    ws = (wx, lx, wy, ly, wz, down_z(wz))
                    inv = 1.0 / (wx + lx + wy + ly + wz + ws[5])
                    weights[x, y] = [jnp.broadcast_to(w * inv, (8, NZ)) for w in ws]
                return weights[x, y]

            def look(known, cell):
                def at(x, y):
                    return known[x, y] if (x, y) in known else cell(x, y)

                return at

            def run(at, cells, fresh):
                out = {}
                for dx, dy in cells:
                    x, y = px(dx), py(dy)
                    if fresh(dx, dy):
                        ws = weight(x, y)
                    else:
                        ws = [w_row(NW, NE, a, x, y) for a in range(6)]
                    out[x, y] = stencil(
                        lambda a: ws[a], lambda ex, ey: at(x + ex, y + ey)
                    )
                return out

            def fresh(dx, dy):
                return (dx > 0 and dy >= 0) or (dy > 0 and dx >= 0)

            v = look(got, old[0])
            y1 = look(run(v, [(1, 0), (2, 0), (1, 1), (0, 1), (0, 2)], fresh), old[1])
            y2 = look(run(y1, [(0, 0), (1, 0), (1, -1), (0, 1), (-1, 1)], fresh), old[2])
            y3 = look(run(y2, [(0, 0), (-1, 0), (0, -1)], fresh), old[3])
            ra, rb = 0.0, 0.0
            for n, (dx, dy) in enumerate(((0, 0), (-1, 0), (0, -1), (-1, -1))):
                x, y = px(dx), py(dy)
                four = (v(x, y), y1(x, y), y2(x, y), y3(x, y))
                ga, gb = rest(*four)
                deg = w_row(NW, NE, 6, x, y)
                ra = ra + deg * ga
                rb = rb + deg * gb
                p, b = smooth(*four)
                fix[2 * side + top, n, 0:8] = p
                fix[2 * side + top, n, 8:16] = b
            x, y = (CX - 1) * side, (CY - 1) * top
            inv = row(over, x, y)
            at = 2 * (x * CY + y)
            f[at] = compress(ra) * inv
            f[at + 1] = compress(rb) * inv
    for x in range(CX):
        at = 2 * x * CY
        fd[8 * x : 8 * x + 8] = f[at : at + 8]
        fu[8 * x : 8 * x + 8] = f[at + 8 : at + 16]


def meanwhile(vt, NW, NE, Y1, Y2, Y3, Y1X, Y2X, Y3X, fix, pb, nd):
    y1, y2, y3 = pick(Y1, Y1X, Y1E), pick(Y2, Y2X, Y2E), pick(Y3, Y3X, Y3E)
    num = den = jnp.zeros((8, NZ), jnp.float32)
    corner = {}
    for side in range(2):
        for top in range(2):
            for n, (dx, dy) in enumerate(((0, 0), (-1, 0), (0, -1), (-1, -1))):
                x = LX - 1 + dx if side else -dx
                y = LY - 1 + dy if top else -dy
                corner[x, y] = 2 * side + top, n
    for x in range(LX):
        for y in range(LY):
            v, nv = vt[x, y], y1(x, y)
            if (x, y) in corner:
                pb[x, y] = fix[corner[x, y]]
            else:
                p, b = smooth(v, nv, y2(x, y), y3(x, y))
                pb[x, y, 0:8] = p
                pb[x, y, 8:16] = b
            dv = w_row(NW, NE, 6, x, y) * v
            num = num + dv * (v - nv)
            den = den + dv * v
    nd[0] = num
    nd[1] = den


JC = 8
CCELLS = [(dx, dy) for dx in (1, 2, 3) for dy in range(1, CH + 1 - dx)]


NCC = 4 * len(CCELLS) + 2 * len(CWP)


def coarse_corner_send(left, right, after, yl, yr, cu, cd):
    n = 0
    for side in range(2):
        for dx, dy in CCELLS:
            x = dx - 1 if side else CX - dx
            src = right if side else left
            for half in range(2):
                cu[n] = src[2 * (x * CY + CY - dy) + half]
                cd[n] = src[2 * (x * CY + dy - 1) + half]
                n += 1
    for p in CWP:
        src, x = (left, p + CX) if p < 0 else (right, p - CX)
        for a in range(4):
            w = src[NF + 4 * a + x]
            m, r = n + (a >> 1), 4 * (a & 1)
            cu[m, r : r + 4] = w[4:8]
            cd[m, r : r + 4] = w[0:4]
        n += 2


def beyond(i, j):
    return max(CH - i, i - CH - CX + 1, 0), max(CH - j, j - CH - CY + 1, 0)


def cells_within(radius):
    every = [(i, j) for i in range(CX + 2 * CH) for j in range(CY + 2 * CH)]
    return [c for c in every if sum(beyond(*c)) <= radius]


def early(before, radius):
    out = set()
    for i, j in cells_within(radius):
        dx, dy = beyond(i, j)
        if dx and not CH < j < CH + CY - 1 or dy and not CH < i < CH + CX - 1:
            continue
        if {(i, j), (i + 1, j), (i - 1, j), (i, j + 1), (i, j - 1)} <= before:
            out.add((i, j))
    return out


EARLY0 = {c for c in cells_within(CH) if 0 in beyond(*c)}
EARLY1 = early(EARLY0, 3)
EARLY2 = early(EARLY1, 2)
EARLY3 = early(EARLY2, 1)
BLOCKS = [(x, y) for x in range(CX) for y in range(CY)]
DONE = [
    (x, y)
    for x, y in BLOCKS
    if {(x + CH + i, y + CH + j) for i, j in ((0, 0), (1, 0), (-1, 0), (0, 1), (0, -1))} <= EARLY3
]


def coarse_weights(own, left, right, gl, gr, corner, CW, R):
    for a in range(4):
        for i in range(CX + 2 * CH):
            p = i - CH
            src, x = (left, p + CX) if p < 0 else (own, p) if p < CX else (right, p - CX)
            R[a, i, JC : JC + CY] = src[NF + 4 * a + x]
            if 0 <= p < CX:
                lo = coarse_rows(gl, H * LX + LX + p, a)
                hi = coarse_rows(gr, H * LX + LX + p, a)
            elif corner and p in CWP:
                m, r = 4 * len(CCELLS) + 2 * CWP.index(p) + (a >> 1), 4 * (a & 1)
                lo, hi = corner[0][m, r : r + 4], corner[1][m, r : r + 4]
            else:
                continue
            R[a, i, JC - 4 : JC] = lo
            R[a, i, JC + CY : JC + CY + 4] = hi
    for i in range(1, CX + 2 * CH - 1):
        cx, lcx, cy, cz = R[0, i], R[0, i - 1], R[1, i], R[2, i]
        ws = (cx, lcx, cy, pltpu.roll(cy, 1, 0), cz, down_z(cz))
        total = ws[0] + ws[1] + ws[2] + ws[3] + ws[4] + ws[5]
        inv = OMEGA / (DIAG * total + SHIFT * R[3, i])
        for a in range(6):
            CW[a, i] = ws[a] * inv


def sweep(cells, at, f, CW, dst):
    for i, j in cells:
        ws = [row(CW, a, i, j - CH + JC) for a in range(6)]
        for half in range(2):
            c = at(i, j, half)
            dst[i, j, half] = (
                (1.0 - OMEGA) * c
                + f(i, j, half)
                + ws[0] * at(i + 1, j, half)
                + ws[1] * at(i - 1, j, half)
                + ws[2] * at(i, j + 1, half)
                + ws[3] * at(i, j - 1, half)
                + ws[4] * up_z(c)
                + ws[5] * down_z(c)
            )


def last_sweep(blocks, cell, pb, NW, NE, po, bo):
    for x, y in blocks:
        for half in range(2):
            e = cell(x + CH, y + CH, half)
            ez = (up_z(e), down_z(e))
            ke = KEEP * e
            ce = C * e
            for dx in range(2):
                ex = C * cell(x + CH + 2 * dx - 1, y + CH, half)
                for dy in range(2):
                    ey = C * cell(x + CH, y + CH + 2 * dy - 1, half)
                    xx, yy = 2 * x + dx, 2 * y + dy
                    nw = [w_row(NW, NE, a, xx, yy) for a in range(6)]
                    s = (
                        ke
                        + (nw[dx] + nw[2 + dy]) * ce
                        + nw[1 - dx] * ex
                        + nw[3 - dy] * ey
                        + C * (nw[4] * ez[0] + nw[5] * ez[1])
                    )
                    if half == 0:
                        po[xx, yy] = pb[xx, yy, 0:8] - s
                    else:
                        bo[xx, yy] = pb[xx, yy, 8:16] + s


def row8(ref, x, y, m, z):
    return jnp.broadcast_to(ref[x, y, m : m + 1, z], (8, 128))


def add_gram(blocks, acc, po, bo, NW, NE):
    for x, y in blocks:
        for n in range(4):
            xx, yy = 2 * x + (n >> 1), 2 * y + (n & 1)
            deg = w_row(NW, NE, 6, xx, yy)
            for h in range(0, NZ, 128):
                z = slice(h, h + 128)
                p = po[xx, yy, :, z]
                b = bo[xx, yy, :, z]
                dp = deg[:, z] * p
                db = deg[:, z] * b
                for m in range(8):
                    acc[m] = acc[m] + dp * row8(po, xx, yy, m, z)
                    acc[13 + m] = acc[13 + m] + dp * row8(bo, xx, yy, m, z)
                for s in range(5):
                    acc[8 + s] = acc[8 + s] + b * (pltpu.roll(db, s, 0) if s else db)


def coarse_early(
    own, left, right, yl, yr, gl, gr, pb, NW, NE, F, E1, E2, EX, po, bo, g, E3, CW, R
):
    for x in range(CX):
        for half in range(2):
            for y in range(CY):
                at = 2 * (x * CY + y) + half
                F[x, y + CH, half] = OMEGA * left[at]
                F[x + CH, y + CH, half] = OMEGA * own[at]
                F[x + CH + CX, y + CH, half] = OMEGA * right[at]
            for y in range(CH):
                F[x + CH, y, half] = OMEGA * yl[2 * (x * CH + y) + half]
                F[x + CH, y + CH + CY, half] = OMEGA * yr[2 * (x * CH + y) + half]
    coarse_weights(own, left, right, gl, gr, None, CW, R)

    def of(ref):
        return lambda i, j, half: ref[i, j, half]

    sweep(sorted(EARLY1), of(F), of(F), CW, E1)
    sweep(sorted(EARLY2), of(E1), of(F), CW, E2)
    sweep(sorted(EARLY3), of(E2), of(F), CW, E3)
    for i, j in sorted(EARLY3):
        for half in range(2):
            EX[i, j, half] = expand(E3[i, j, half])
    last_sweep(DONE, of(EX), pb, NW, NE, po, bo)
    acc = [jnp.zeros((8, 128), jnp.float32)] * 21
    add_gram(DONE, acc, po, bo, NW, NE)
    for n in range(21):
        g[n] = acc[n]


def coarse_level(
    own,
    left,
    right,
    cl,
    cr,
    gl,
    gr,
    F,
    E1,
    E2,
    EXE,
    pe,
    be,
    ge,
    pb,
    NW,
    NE,
    nd,
    po,
    bo,
    mine,
    other,
    X1,
    X2,
    X3,
    EX,
    CW,
    R,
):
    coarse_weights(own, left, right, gl, gr, (cl, cr), CW, R)
    corner = {}
    n = 0
    for side in range(2):
        for dx, dy in CCELLS:
            i = CH + CX - 1 + dx if side else CH - dx
            for half in range(2):
                corner[i, CH - dy, half] = cl, n
                corner[i, CH + CY - 1 + dy, half] = cr, n
                n += 1

    def f(i, j, half):
        if (i, j, half) in corner:
            msg, n = corner[i, j, half]
            return OMEGA * msg[n]
        return F[i, j, half]

    def both(first, cells, then):
        return lambda i, j, half: (first if (i, j) in cells else then)[i, j, half]

    e1, e2 = both(E1, EARLY1, X1), both(E2, EARLY2, X2)
    sweep([c for c in cells_within(3) if c not in EARLY1], f, f, CW, X1)
    sweep([c for c in cells_within(2) if c not in EARLY2], e1, f, CW, X2)
    sweep([c for c in cells_within(1) if c not in EARLY3], e2, f, CW, X3)
    for i, j in cells_within(1):
        if (i, j) not in EARLY3:
            for half in range(2):
                EX[i, j, half] = expand(X3[i, j, half])
    for x, y in DONE:
        here = slice(2 * x, 2 * x + 2), slice(2 * y, 2 * y + 2)
        po[here] = pe[here]
        bo[here] = be[here]
    left_over = [c for c in BLOCKS if c not in DONE]
    last_sweep(left_over, both(EXE, EARLY3, EX), pb, NW, NE, po, bo)
    zero = jnp.zeros((8, 128), jnp.float32)
    acc = [ge[n] for n in range(21)]
    add_gram(left_over, acc, po, bo, NW, NE)
    for q in range(2):
        acc.append(nd[q, :, :128] + nd[q, :, 128:])
    lane = lax.broadcasted_iota(jnp.int32, (8, 128), 1)
    sub = lax.broadcasted_iota(jnp.int32, (8, 128), 0)

    def collect(blocks):
        x = zero
        for n, a in enumerate(blocks):
            total = jnp.broadcast_to(jnp.sum(a, axis=1, keepdims=True), (8, 128))
            x = x + jnp.where(lane == 8 * n + sub, total, 0.0)
        return jnp.sum(x, axis=0, keepdims=True)

    t0 = collect(acc[:16])
    t1 = collect(acc[16:])
    even = lax.axis_index("gy") % 2 == 0
    mine[...] = jnp.where(even, t0, t1)
    other[...] = jnp.where(even, t1, t0)


def spread_sums(a, b, out):
    out[...] = jnp.broadcast_to((a[...] + b[...])[None], out.shape)


def finish(parts, po, bo, out, eig, SP):
    t = parts[...]
    n = t.shape[0]
    while n > 2:
        n //= 2
        t = t[:n] + t[n:]
    t = t[:, 0]
    lams = t[1:2] / pltpu.roll(t[1:2], 120, 1)
    eig[...] = pltpu.roll(lams, 88, 1)[:, :K]
    half = [jnp.broadcast_to(t[q : q + 1], (8, 128)) for q in range(2)]

    def entry(block, k):
        at = 8 * (block % 16) + k
        return jnp.broadcast_to(half[block // 16][:, at : at + 1], (8, 128))

    def sym(a, b):
        s = (a - b) % 8
        return entry(8 + s, a) if s < 5 else entry(16 - s, b)

    def cross(a, b):
        return entry(13 + b, a)

    lam = [entry(21, k) / entry(22, k) for k in range(K)]
    voxels = LX * LY * NZ * lax.axis_size("gx") * lax.axis_size("gy")
    g = {}
    for a in range(K):
        for b in range(a + 1):
            g[a, b] = (
                entry(b, a) + lam[b] * cross(a, b) + lam[a] * (cross(b, a) + lam[b] * sym(a, b))
            ) * (1.0 / voxels)
    low, inv = {}, []
    for j in range(K):
        d = g[j, j]
        r = lax.rsqrt(d)
        r = r * (1.5 - 0.5 * d * r * r)
        inv.append(r)
        for a in range(j + 1, K):
            low[a, j] = g[a, j] * r
        for a in range(j + 1, K):
            for b in range(j + 1, a + 1):
                g[a, b] = g[a, b] - low[a, j] * low[b, j]

    sub = lax.broadcasted_iota(jnp.int32, (8, 128), 0)
    lam_rows = jnp.zeros((8, 128), jnp.float32)
    for k in range(K):
        lam_rows = jnp.where(sub == k, lam[k], lam_rows)
        SP[64 + 8 * k : 72 + 8 * k] = inv[k]
    at = {}
    for n, (a, b) in enumerate(sorted(low)):
        at[a, b] = 128 + 8 * n
        SP[128 + 8 * n : 136 + 8 * n] = low[a, b]

    def body(x, _):
        for t in range(0, LY, 8):
            for h in range(0, NZ, 128):
                z = slice(h, h + 128)
                upd = po[x, t : t + 8, :, z] + lam_rows[None] * bo[x, t : t + 8, :, z]
                upd = jnp.swapaxes(upd, 0, 1)
                done = []
                for k in range(K):
                    u = upd[k]
                    for j in range(k):
                        u = u - SP[at[k, j] : at[k, j] + 8] * done[j]
                    u = u * SP[64 + 8 * k : 72 + 8 * k]
                    done.append(u)
                    out[k, x, t : t + 8, z] = u
        return 0

    lax.fori_loop(0, LX, body, 0, unroll=2)


def both_ways(up, down, axis):
    n = lax.axis_size(axis)
    fwd = [(i, (i + 1) % n) for i in range(n)]
    back = [((i + 1) % n, i) for i in range(n)]
    return lax.ppermute(up, axis, fwd), lax.ppermute(down, axis, back)


def per_device(vectors, weight_x, weight_y, weight_z):
    args = (vectors, weight_x, weight_y, weight_z)
    xu, xd = call(
        x_send,
        [(NXU, LY, NZ), (NXD, LY, NZ)],
        args,
        [(NXU, LY, NZ), (NXD, LY, NZ), pltpu.SemaphoreType.DMA((4 * K + 12,))],
        limit=56,
        where=ANY,
    )
    rl, rr = both_ways(xu, xd, "gx")
    vt, wm, cw, yu, yd = call(
        local,
        [
            (LX, LY, K, NZ),
            (3, LX, LY, NZ),
            (4, CX, CY, CZ),
            (NYB, 8, NZ),
            (NYB, 8, NZ),
        ],
        (vectors, jnp.stack(args[1:])),
        [(5, CX * LY, CZ)],
    )
    yl, yr = both_ways(yu, yd, "gy")
    tall = LY + 2 * H
    W, NW, Y1, Y2, Y3, PX = call(
        fine_inner,
        [
            (3, LX, 32, NZ),
            (7, LX - 1, 32, NZ),
            (6, tall, K, NZ),
            (4, tall, K, NZ),
            (2, tall, K, NZ),
            (len(LACK), LY, K, NZ),
        ],
        (vt, wm, cw, yl, yr),
        us=3,
    )
    xl, xr, cu, cd = call(
        x_receive, [(NXB, 8, NZ), (NXB, 8, NZ), (NCB, 8, NZ), (NCB, 8, NZ)], (rl, rr, Y3)
    )
    cl, cr = both_ways(cu, cd, "gy")
    NE, Y1X, Y2X, Y3X, f, over = call(
        fine_outer,
        [
            (7, len(NH), LY, NZ),
            (6, tall, K, NZ),
            (6, tall, K, NZ),
            (6, tall, K, NZ),
            (NF + 4 * CX, 8, CZ),
            (CX, CY, CZ),
        ],
        (vt, wm, cw, xl, xr, yl, yr, W, NW, Y1, Y2, Y3, PX),
        us=4,
    )
    f, fu, fd, fix = call(
        fine_corners,
        [(NF + 4 * CX, 8, CZ), (NF // 2, 8, CZ), (NF // 2, 8, CZ), (4, 4, 16, NZ)],
        (vt, xl, xr, yl, yr, W, NW, Y1, Y2, Y3, NE, Y1X, Y2X, Y3X, f, over, cl, cr),
    )
    left, right = both_ways(f, f, "gx")
    fl, fr = both_ways(fu, fd, "gy")
    pb, nd = call(
        meanwhile,
        [(LX, LY, 16, NZ), (2, 8, NZ)],
        (vt, NW, NE, Y1, Y2, Y3, Y1X, Y2X, Y3X, fix),
    )
    cu, cd = call(coarse_corner_send, [(NCC, 8, CZ)] * 2, (left, right, nd, fl, fr))
    cl, cr = both_ways(cu, cd, "gy")
    cext = (CX + 2 * CH, CY + 2 * CH, 2, 8, CZ)
    weights = [(6, CX + 2 * CH, 24, CZ), (4, CX + 2 * CH, 24, CZ)]
    early_ = call(
        coarse_early,
        [cext] * 3
        + [(CX + 2 * CH, CY + 2 * CH, 2, 8, NZ), (LX, LY, K, NZ), (LX, LY, K, NZ), (21, 8, 128)],
        (f, left, right, fl, fr, yl, yr, pb, NW, NE),
        [cext] + weights,
        us=2,
    )
    po, bo, mine, other = call(
        coarse_level,
        [(LX, LY, K, NZ), (LX, LY, K, NZ), (1, 128), (1, 128)],
        (f, left, right, cl, cr, yl, yr, *early_, pb, NW, NE, nd),
        [cext, cext, cext, (CX + 2 * CH, CY + 2 * CH, 2, 8, NZ)] + weights,
        limit=12,
    )
    n = lax.axis_size("gy")
    theirs = lax.ppermute(other, "gy", [(i, i ^ 1) for i in range(n)])
    (sums,) = call(spread_sums, [(n * lax.axis_size("gx"), 1, 128)], (mine, theirs))
    parts = lax.all_to_all(sums, ("gx", "gy"), 0, 0)
    refined, eig = call(
        finish,
        [(K, LX, LY, NZ), (1, K)],
        (parts, po, bo),
        [(384, 128)],
    )
    return refined, eig.reshape(K)


def solution(mesh):
    return jax.shard_map(
        per_device,
        mesh=mesh,
        in_specs=(
            P(None, "gx", "gy", None),
            P("gx", "gy", None),
            P("gx", "gy", None),
            P("gx", "gy", None),
        ),
        out_specs=(P(None, "gx", "gy", None), P()),
        check_vma=False,
    )
```
